128 devices in a mesh: pipe: 2 (over x_lo), tensor: 4 (over z), dp: 16 (over y, x_hi, core).
Axes of the slice: x: 4 (x_hi: 2, x_lo: 2; x = x_hi * 2 + x_lo), y: 4, z: 4, core: 2. Of those that a mesh axis runs over, the one named last changes fastest.
Arguments:
- tokens: bfloat16 [2, 6304, 768], P(None, 'dp'), may hold values from -6 to 6
- cotangent: bfloat16 [2, 6304, 768], P(None, 'dp'), may hold values from -6 to 6
- image_counts: int32 [2, 16], replicated, may hold values from 1 to 2, 20 in all within a row
- routes: int32 [2, 6304, 2], P(None, 'dp'), may hold values from 0 to 31, all different within a row; in each aligned block of 394 rows (0 to 393, 394 to 787, ..., all dimensions but the last counted through in order) at most 30 rows name the same one
- attn_norm_gain: float32 [2, 768], P('pipe'), may hold values from 0.5 to 1.5
- query_key_value: bfloat16 [2, 768, 3, 768], P('pipe', None, None, 'tensor'), may hold values from -0.21875 to 0.21875
- attn_output: bfloat16 [2, 768, 768], P('pipe', 'tensor'), may hold values from -1.75 to 1.75
- moe_norm_gain: float32 [2, 768], P('pipe'), may hold values from 0.5 to 1.5
- router_weight: bfloat16 [2, 768, 32], P('pipe'), may hold values from -0.15917969 to 0.15917969
- expert_in: bfloat16 [2, 32, 768, 3072], P('pipe', 'dp', None, 'tensor'), may hold values from -0.21875 to 0.21875
- expert_down: bfloat16 [2, 32, 3072, 768], P('pipe', 'dp', 'tensor'), may hold values from -3 to 3
Outputs:
- section_out: bfloat16 [2, 2, 6304, 768], P('pipe', None, 'dp')
- input_grad: bfloat16 [2, 2, 6304, 768], P('pipe', None, 'dp')
- grad_attn_norm: float32 [2, 768], P('pipe')
- grad_query_key_value: float32 [2, 768, 3, 768], P('pipe', None, None, 'tensor')
- grad_attn_output: float32 [2, 768, 768], P('pipe', 'tensor')
- grad_moe_norm: float32 [2, 768], P('pipe')
- grad_router: float32 [2, 768, 32], P('pipe')
- grad_expert_in: float32 [2, 32, 768, 3072], P('pipe', 'dp', None, 'tensor')
- grad_expert_down: float32 [2, 32, 3072, 768], P('pipe', 'dp', 'tensor')
The draws below stay inside these ranges and needn't reach their ends.
Inputs may be any that keep to these rules, and one draw needn't show every extreme that they name: `image_counts`: in each micro-batch the counts sum to 20, and some dp index holds 2 images. `routes`: each row names two different experts; in the rows of one dp index of one micro-batch no expert is named by more than 30 rows, a bound that some expert reaches in some of these blocks.
All inputs are finite; a program needn't handle non-finite values.
Results may differ from the reference program's by a relative error of at most 0.03.
Values may be sent and summed in bfloat16 or wider, within the bound.
A program may use at most 256 MiB of HBM per device.

```python
import math
import jax
import jax.numpy as jnp
import numpy as np
from jax import lax

D = 768
HEADS = 12
HD = 64
FF = 3072
IMG_LEN = 197
SLOT = 2
MICRO = 2
EXPERTS = 32
TOK_DEV = 394
TOKENS = 6304
IMAGES = 20
CAP = 30
N_PIPE = 2
N_TENSOR = 4
N_DP = 16


def block_levels(stream_key, shape, cuts, least, largest):
    def one(dim, shards_of):
        steps = jax.random.uniform(jax.random.fold_in(jax.random.fold_in(stream_key, 6), dim), (shards_of,), jnp.float32, least / len(cuts), largest / len(cuts))
        return jnp.repeat(jnp.exp(steps), shape[dim] // shards_of).reshape((-1,) + (1,) * (len(shape) - dim - 1))

    factor_of = one(*cuts[0])
    for cut in cuts[1:]:
        factor_of = factor_of * one(*cut)
    return factor_of


def profile(count, total, reach, slope):
    weights = [(1 << 20) // math.isqrt(standing ** slope) + 1 for standing in range(2, count + 1)]
    spare, given = total - reach - (count - 1), [1] * (count - 1)
    while spare > 0:
        candidates = [i for i in range(count - 1) if given[i] < reach]
        whole, budget = sum([weights[i] for i in candidates]), spare
        for i in candidates:
            addition = min(reach - given[i], max(1, budget * weights[i] // whole), spare)
            given[i] = given[i] + addition
            spare = spare - addition
    return np.array([reach] + given)


def ragged_sizes(stream_key, amount, total, reach, lean):
    if amount == 2:
        one = jax.random.randint(stream_key, (), max(1, total - reach), min(reach, total - 1) + 1)
        return jnp.stack([one, total - one])
    tallies = jnp.asarray(profile(amount, total, reach, lean), jnp.int32)
    pairs = (amount - 1) // 2
    giver, taker = tallies[1:1 + 2 * pairs:2], tallies[2:2 + 2 * pairs:2]
    margin = jnp.minimum(giver - 1, reach - taker)
    passed = jax.random.randint(jax.random.fold_in(stream_key, 1), (pairs,), 0, 1 << 20) % (margin + 1)
    tallies = tallies.at[1:1 + 2 * pairs:2].set(giver - passed).at[2:2 + 2 * pairs:2].set(taker + passed)
    return tallies[jax.random.permutation(jax.random.fold_in(stream_key, 2), amount)]


def assign_block(own_key, own, number, rows, number_of, top, most, skew):
    sequence = jax.random.permutation(own_key, number_of)
    heavy_load, usual = load_shares(number_of, rows * top, most, skew, True), load_shares(number_of, rows * top, most, skew, False)
    places = jnp.arange(number_of)

    def named(lengths, rotation):
        used = int((lengths > 0).sum())
        fixed = max(1, used // 4)
        passed = fixed + (places - fixed + rotation * (used - fixed)) % max(1, number_of - fixed)
        return jnp.zeros((number_of,), jnp.int32).at[sequence[jnp.where(places < fixed, places, passed)]].set(jnp.asarray(lengths, jnp.int32))

    lengths = jnp.where(number % 4 == 0, named(heavy_load, number // 4), named(usual, number - number // 4 - 1))
    mixed = jax.random.permutation(jax.random.fold_in(own, 3), number_of)
    source_of, receiver = mixed[0:number_of // 2 * 2:2], mixed[1:number_of // 2 * 2:2]
    room = jnp.minimum(lengths[source_of] - 1, most - lengths[receiver]) // 2
    room = jnp.where((source_of == sequence[0]) | (receiver == sequence[0]) | (lengths[receiver] == 0), 0, jnp.maximum(room, 0))
    passed = jax.random.randint(jax.random.fold_in(own, 4), (number_of // 2,), 0, 1 << 20) % (room + 1)
    lengths = lengths.at[source_of].add(-passed).at[receiver].add(passed)
    items = jnp.searchsorted(jnp.cumsum(lengths), jnp.arange(rows * top), side="right").astype(jnp.int32)
    grid = items.reshape(top, rows).T
    grid = grid[jax.random.permutation(jax.random.fold_in(own, 1), rows)]
    rotation = jax.random.randint(jax.random.fold_in(own, 2), (rows, 1), 0, top)
    return jnp.take_along_axis(grid, (jnp.arange(top)[None, :] + rotation) % top, axis=1)


def load_shares(count, total, limit, slope, full):
    weights = [(1 << 20) // math.isqrt(rank ** slope) + 1 for rank in range(1, count + 1)]
    largest = limit if full else min(limit, max(-(-total // count), total * weights[0] // sum(weights)))
    least = 1 if total - largest >= count - 1 else 0
    holding, spare = [largest] + [least] * (count - 1), total - largest - least * (count - 1)
    while spare > 0:
        movable = [i for i in range(1, count) if holding[i] < largest] or [i for i in range(1, count) if holding[i] < limit]
        mass, budget = sum([weights[i] for i in movable]), spare
        for i in movable:
            more = min(limit - holding[i], max(1, budget * weights[i] // mass), spare)
            holding[i] = holding[i] + more
            spare = spare - more
    return np.array(holding)


def bell_draw(key, shape, width, bound, cuts=(), held_as=jnp.bfloat16):
    array = jax.random.normal(key, shape, jnp.float32) * width
    if len(cuts) > 0:
        array = block_levels(key, shape, cuts, -0.22, 0.18) * array
    return jnp.clip(array, min=-bound, max=bound).astype(held_as)


def setup_inputs(seed: int = 0) -> dict:
    key_list = jax.random.split(jax.random.key(seed), 12)
    tokens = bell_draw(key_list[0], (MICRO, TOKENS, D), 1.0, 6.0, ((1, 16),))
    cotangent = bell_draw(key_list[1], (MICRO, TOKENS, D), 1.0, 6.0, ((1, 16),))
    image_counts = jax.vmap(lambda own: ragged_sizes(own, N_DP, IMAGES, SLOT, 2))(jax.random.split(key_list[2], MICRO)).reshape((MICRO, N_DP)).astype(jnp.int32)
    routes_keys = jax.random.split(jax.random.fold_in(key_list[3], 1), MICRO * TOKENS // TOK_DEV)
    routes_turns = jax.random.permutation(jax.random.fold_in(key_list[3], 3), MICRO * TOKENS // TOK_DEV)
    routes = jax.vmap(lambda own, number: assign_block(jax.random.fold_in(key_list[3], 2), own, number, TOK_DEV, EXPERTS, 2, CAP, 1))(routes_keys, routes_turns).reshape((MICRO, TOKENS, 2))
    attn_norm_gain = jnp.clip(1.0 + 0.1 * jax.random.normal(key_list[4], (2, D), jnp.float32), 0.5, 1.5)
    query_key_value = bell_draw(key_list[5], (2, D, 3, HEADS * HD), D ** -0.5, 0.21875, ((0, 2), (3, 4)))
    attn_output = bell_draw(key_list[6], (2, HEADS * HD, D), (HEADS * HD // 64) ** -0.5, 1.75, ((0, 2), (1, 4)))
    moe_norm_gain = jnp.clip(1.0 + 0.1 * jax.random.normal(key_list[7], (2, D), jnp.float32), 0.5, 1.5)
    router_weight = bell_draw(key_list[8], (2, D, EXPERTS), 0.027, 0.15917969, ((0, 2),))
    expert_in = bell_draw(key_list[9], (2, EXPERTS, D, FF), D ** -0.5, 0.21875, ((0, 2), (1, 16), (3, 4)))
    expert_down = bell_draw(key_list[10], (2, EXPERTS, FF, D), 0.5, 3.0, ((0, 2), (1, 16), (2, 4)))
    return {"tokens": tokens, "cotangent": cotangent, "image_counts": image_counts, "routes": routes, "attn_norm_gain": attn_norm_gain, "query_key_value": query_key_value, "attn_output": attn_output, "moe_norm_gain": moe_norm_gain, "router_weight": router_weight, "expert_in": expert_in, "expert_down": expert_down}


@jax.custom_vjp
def low(v):
    return lax.optimization_barrier(v.astype(jnp.bfloat16)).astype(jnp.float32)

@jax.custom_vjp
def low_back(v):
    return v

def low_keep(v):
    return (low(v), None)

def low_pass(kept, grad):
    return (grad,)

def back_keep(v):
    return (v, None)

def back_low(kept, grad):
    return (low(grad),)
low.defvjp(low_keep, low_pass)
low_back.defvjp(back_keep, back_low)
EPSILON = 1e-06
HIGHEST_PRECISION = lax.Precision.HIGHEST

def layer_norm(values, gain_vector):
    average = lax.optimization_barrier(jnp.mean(values, axis=-1, keepdims=True))
    centred = values - average
    spread = lax.optimization_barrier(jnp.mean(centred * centred, axis=-1, keepdims=True))
    return centred * lax.rsqrt(spread + EPSILON) * gain_vector

def slot_numbers(route_ids, live_int):
    matches = (route_ids[:, :, None] == jnp.arange(EXPERTS, dtype=jnp.int32)).astype(jnp.int32)
    matches = matches * live_int[:, None, None]
    matches_flat = matches.reshape(-1, EXPERTS)
    before = jnp.cumsum(matches_flat, axis=0) - matches_flat
    return lax.optimization_barrier(jnp.sum(before * matches_flat, axis=1)).reshape(route_ids.shape)

def attention_block(state, gain_vector, project_weight, output_weight):
    normed = low(layer_norm(state, gain_vector))
    group = HEADS // N_TENSOR
    group_width = group * HD
    images = state.shape[0] // IMG_LEN
    summed_parts = jnp.zeros(state.shape, jnp.float32)
    for member in range(N_TENSOR):
        columns = project_weight[:, :, member * group_width:(member + 1) * group_width].reshape(D, 3 * group_width)
        projected = low_back(low(jnp.dot(normed, columns, precision=HIGHEST_PRECISION)))
        projected = projected.reshape(images, IMG_LEN, 3, group, HD)
        scores = jnp.einsum('sihd,sjhd->shij', projected[:, :, 0], projected[:, :, 1], precision=HIGHEST_PRECISION)
        scores = low_back(scores * HD ** (-0.5))
        weights_low = low(jax.nn.softmax(scores, axis=-1))
        context = jnp.einsum('shij,sjhd->sihd', weights_low, projected[:, :, 2], precision=HIGHEST_PRECISION)
        context = low_back(low(context.reshape(state.shape[0], group_width)))
        rows_out = output_weight[member * group_width:(member + 1) * group_width]
        summed_parts = summed_parts + low(jnp.dot(context, rows_out, precision=HIGHEST_PRECISION))
    return state + low_back(summed_parts)

def expert_block(state, gain_vector, router, first_matrix, second_matrix, route_ids, slot_ids, live_int):
    row_total = state.shape[0]
    live_rows = live_int.astype(jnp.float32)
    normed = low(layer_norm(state, gain_vector))
    gate_probs = jax.nn.softmax(jnp.dot(normed, router, precision=HIGHEST_PRECISION), axis=-1)
    gate_picks = jnp.take_along_axis(gate_probs, route_ids, axis=1) * live_rows[:, None]
    source = jnp.arange(row_total, dtype=jnp.int32)[:, None] // TOK_DEV
    slots_all = N_DP * EXPERTS * CAP
    position = (source * EXPERTS + route_ids) * CAP + slot_ids
    position = jnp.where(live_int[:, None] > 0, position, slots_all)
    copies = jnp.broadcast_to(normed[:, None, :], (row_total, 2, D)).reshape(row_total * 2, D)
    buffer_rows = jnp.zeros((slots_all, D), jnp.float32).at[position.reshape(-1)].add(copies, mode='drop')
    arrived = buffer_rows.reshape(N_DP, EXPERTS, CAP, D).transpose(1, 0, 2, 3).reshape(EXPERTS, N_DP * CAP, D)
    part_width = FF // N_TENSOR
    summed_parts = jnp.zeros(arrived.shape, jnp.float32)
    for member in range(N_TENSOR):
        first_part = first_matrix[:, :, member * part_width:(member + 1) * part_width]
        second_part = second_matrix[:, member * part_width:(member + 1) * part_width]
        preact = low_back(jnp.einsum('erd,edf->erf', arrived, first_part, precision=HIGHEST_PRECISION))
        hidden = low_back(low(jax.nn.gelu(preact)))
        summed_parts = summed_parts + low(jnp.einsum('erf,efd->erd', hidden, second_part, precision=HIGHEST_PRECISION))
    returned = low_back(summed_parts).reshape(EXPERTS, N_DP, CAP, D).transpose(1, 0, 2, 3).reshape(slots_all, D)
    pieces = returned[jnp.minimum(position, slots_all - 1)]
    mixed = lax.optimization_barrier(jnp.sum(pieces * gate_picks[:, :, None], axis=1))
    return live_rows[:, None] * (state + mixed)

def reference(tokens, cotangent, image_counts, routes, attn_norm_gain, query_key_value, attn_output, moe_norm_gain, router_weight, expert_in, expert_down):
    row_ids = jnp.arange(TOKENS, dtype=jnp.int32)
    owner = row_ids // TOK_DEV
    picture = row_ids % TOK_DEV // IMG_LEN
    live_list = []
    slot_list = []
    for batch in range(MICRO):
        live_int = (picture < image_counts[batch][owner]).astype(jnp.int32)
        slot_ids = jax.vmap(slot_numbers)(routes[batch].reshape(N_DP, TOK_DEV, 2), live_int.reshape(N_DP, TOK_DEV))
        live_list.append(live_int)
        slot_list.append(slot_ids.reshape(TOKENS, 2))
    params = (attn_norm_gain.astype(jnp.float32), query_key_value.astype(jnp.float32), attn_output.astype(jnp.float32), moe_norm_gain.astype(jnp.float32), router_weight.astype(jnp.float32), expert_in.astype(jnp.float32), expert_down.astype(jnp.float32))
    probe = jnp.zeros((N_PIPE - 1, MICRO, TOKENS, D), jnp.float32)

    def forward(start, probe_values, gain_one, project_weight, output_weight, gain_two, router, first_matrix, second_matrix):
        finals = []
        middles = []
        for batch in range(MICRO):
            state = start[batch]
            section_values = []
            for layer in range(N_PIPE):
                state = attention_block(state, gain_one[layer], project_weight[layer], output_weight[layer])
                state = expert_block(state, gain_two[layer], router[layer], first_matrix[layer], second_matrix[layer], routes[batch], slot_list[batch], live_list[batch])
                if layer + 1 < N_PIPE:
                    state = low_back(low(state) + probe_values[layer, batch])
                    section_values.append(state)
            finals.append(state)
            middles.append(jnp.stack(section_values))
        return (jnp.stack(finals), jnp.stack(middles))
    finals, pull, middles = jax.vjp(forward, tokens.astype(jnp.float32), probe, *params, has_aux=True)
    grads = pull(cotangent.astype(jnp.float32))
    section_out = jnp.concatenate([middles.transpose(1, 0, 2, 3), finals[None]], axis=0).astype(jnp.bfloat16)
    input_grad = jnp.concatenate([grads[0][None], grads[1]], axis=0).astype(jnp.bfloat16)
    return (section_out, input_grad, grads[2], grads[3], grads[4], grads[5], grads[6], grads[7], grads[8])
```

```python
import functools

import jax
import jax.numpy as jnp
from jax import lax
from jax.experimental import pallas as pl
from jax.experimental.pallas import tpu as pltpu
from jax.sharding import PartitionSpec as P

BF = jnp.bfloat16
F32 = jnp.float32
MESH = pl.DeviceIdType.MESH
D = 768
HD = 64
NH = 3
GW = NH * HD
IMG_LEN = 197
R = 224
NR = 2 * R
CH = NR // 4
EXPERTS = 32
SL = 32
NT = 4
NDP = 16
Q = D // NT
EPSILON = 1e-06
VMEM_BYTES = 48 * 1024 * 1024
GP = 896


def dot(a, b, ca=1, cb=0):
    return lax.dot_general(a, b, (((ca,), (cb,)), ((), ())), preferred_element_type=F32)


def params(**more):
    return pltpu.CompilerParams(vmem_limit_bytes=VMEM_BYTES, **more)


def norm_parts(values):
    mean = jnp.mean(values, axis=-1, keepdims=True)
    centred = values - mean
    inverse = lax.rsqrt(jnp.mean(centred * centred, axis=-1, keepdims=True) + EPSILON)
    return centred * inverse, inverse


def norm_back(delta, gain, normal, inverse):
    scaled = delta * gain
    return inverse * (
        scaled
        - jnp.mean(scaled, axis=-1, keepdims=True)
        - normal * jnp.mean(scaled * normal, axis=-1, keepdims=True)
    )


def pick(index, options):
    result = options[0]
    for number in range(1, len(options)):
        result = jnp.where(index == number, options[number], result)
    return result


def column_quarter(values, member):
    return pick(member, [values[:, Q * q : Q * (q + 1)] for q in range(NT)])


def unpack(packed):
    images = [
        jnp.concatenate([packed[q][:, Q * i : Q * (i + 1)] for q in range(NT)], axis=1)
        for i in range(2)
    ]
    return jnp.concatenate(images, axis=0)


def head_parts(projected, image, head):
    rows = slice(image * R, (image + 1) * R)
    return [
        projected[rows, part * GW + head * HD : part * GW + (head + 1) * HD] for part in range(3)
    ]


def probabilities(queries, keys):
    scores = dot(queries, keys, 1, 1) * (HD**-0.5)
    held = lax.broadcasted_iota(jnp.int32, scores.shape, 1) < IMG_LEN
    scores = jnp.where(held, scores, -1e30)
    exponent = jnp.exp(scores - jnp.max(scores, axis=-1, keepdims=True))
    return exponent / jnp.sum(exponent, axis=-1, keepdims=True)


def attention_forward_kernel(mode, *refs):
    if mode == "plain":
        plain, gain, project, output, part, qkv, ctx = refs
        state = plain[...]
    elif mode == "packed":
        packed, gain, project, output, part, qkv, ctx, kept = refs
        state = unpack(packed)
        kept[...] = state
    else:
        plain, packed, gain, project, output, part, qkv, ctx, kept = refs
        first = lax.axis_index("pipe") == 0
        state = jnp.where(first, plain[...], unpack(packed))
        kept[...] = state
    normal, _ = norm_parts(state.astype(F32))
    normed = (normal * gain[...]).astype(BF)
    projected = dot(normed, project[...]).astype(BF)
    qkv[...] = projected
    for image in range(2):
        for head in range(NH):
            queries, keys, values = head_parts(projected, image, head)
            weights = probabilities(queries, keys).astype(BF)
            ctx[image * R : (image + 1) * R, head * HD : (head + 1) * HD] = dot(
                weights, values
            ).astype(BF)
    part[...] = dot(ctx[...], output[...]).astype(BF)


def attention_forward(mode, inputs, gain, project, output):
    shapes = [
        jax.ShapeDtypeStruct((NR, D), BF),
        jax.ShapeDtypeStruct((NR, 3 * GW), BF),
        jax.ShapeDtypeStruct((NR, GW), BF),
    ]
    if mode != "plain":
        shapes.append(jax.ShapeDtypeStruct((NR, D), BF))
    return pl.pallas_call(
        functools.partial(attention_forward_kernel, mode),
        out_shape=shapes,
        compiler_params=params(),
        name="attention_forward",
    )(*inputs, gain, project, output)


def live_rows(count):
    row = lax.broadcasted_iota(jnp.int32, (NR, 1), 0)
    image = (row >= R).astype(jnp.int32)
    return (image < count) & (row - image * R < IMG_LEN)


def dispatch_kernel(count, state, summed, gain, router, routes, outbox, x1, meta):
    values = state[...].astype(F32) + summed[...].astype(F32)
    x1[...] = values
    normal, _ = norm_parts(values)
    normed = (normal * gain[...]).astype(BF)
    logits = dot(normed, router[...])
    exponent = jnp.exp(logits - jnp.max(logits, axis=-1, keepdims=True))
    gate = exponent / jnp.sum(exponent, axis=-1, keepdims=True)
    live = live_rows(count[0, 0])
    experts = lax.broadcasted_iota(jnp.int32, (NR, EXPERTS), 1)
    route = [routes[:, k : k + 1] for k in range(2)]
    match = [jnp.where(live & (route[k] == experts), 1.0, 0.0) for k in range(2)]
    above = lax.broadcasted_iota(jnp.int32, (NR, NR), 1) < lax.broadcasted_iota(
        jnp.int32, (NR, NR), 0
    )
    before = dot(jnp.where(above, 1.0, 0.0).astype(BF), (match[0] + match[1]).astype(BF))
    meta[:, 0:EXPERTS] = gate
    hot = None
    slots = lax.broadcasted_iota(jnp.int32, (NR, EXPERTS * SL), 1)
    for k in range(2):
        slot = jnp.sum(match[k] * before, axis=1, keepdims=True).astype(jnp.int32)
        position = jnp.where(live, route[k] * SL + slot, -1)
        meta[:, 32 + k : 33 + k] = jnp.sum(match[k] * gate, axis=1, keepdims=True)
        meta[:, 34 + k : 35 + k] = position.astype(F32)
        meta[:, 36 + k : 37 + k] = route[k].astype(F32)
        same = slots == position
        hot = same if hot is None else hot | same
    meta[:, 38:39] = jnp.where(live, 1.0, 0.0)
    outbox[...] = dot(jnp.where(hot, 1.0, 0.0).astype(BF), normed, 0, 0).astype(BF)


def dispatch(count, state, summed, gain, router, routes):
    return pl.pallas_call(
        dispatch_kernel,
        in_specs=[pl.BlockSpec(memory_space=pltpu.SMEM)]
        + [pl.BlockSpec(memory_space=pltpu.VMEM)] * 5,
        out_shape=[
            jax.ShapeDtypeStruct((EXPERTS * SL, D), BF),
            jax.ShapeDtypeStruct((NR, D), F32),
            jax.ShapeDtypeStruct((NR, 128), F32),
        ],
        compiler_params=params(),
        name="dispatch",
    )(count, state, summed, gain, router, routes)


CUBE = 0.044715
ROOT = 0.7978845608028654


def gelu_parts(pre):
    squared = pre * pre
    inner = jnp.tanh(ROOT * (pre + CUBE * pre * squared))
    return 0.5 * pre * (1.0 + inner), inner, squared


def store_quarters(target, half, values):
    for q in range(NT):
        target[q, :, half * Q : (half + 1) * Q] = values[:, q * Q : (q + 1) * Q].astype(BF)


def experts_forward_kernel(arrived, first, second, part):
    rows = arrived[...].reshape(NDP * SL, D)
    hidden = gelu_parts(dot(rows, first[0]))[0].astype(BF)
    result = dot(hidden, second[0])
    for half in range(2):

        @pl.when(pl.program_id(0) == half)
        def _():
            store_quarters(part, half, result)


def experts_forward(arrived, first, second):
    return pl.pallas_call(
        experts_forward_kernel,
        grid=(2,),
        in_specs=[
            pl.BlockSpec((NDP, SL, D), lambda p: (0, p, 0)),
            pl.BlockSpec((1, D, D), lambda p: (p, 0, 0)),
            pl.BlockSpec((1, D, D), lambda p: (p, 0, 0)),
        ],
        out_specs=pl.BlockSpec((NT, NDP * SL, 2 * Q), lambda p: (0, 0, 0)),
        out_shape=jax.ShapeDtypeStruct((NT, NDP * SL, 2 * Q), BF),
        compiler_params=params(),
        name="experts_forward",
    )(arrived, first, second)


def experts_backward_kernel(arrived, delta, first, second, part, hidden_out, dpre_out):
    rows = arrived[...].reshape(NDP * SL, D)
    grads = delta[...].reshape(NDP * SL, D)
    pre = dot(rows, first[0])
    hidden, inner, squared = gelu_parts(pre)
    hidden_out[...] = hidden.astype(BF).reshape(NDP, SL, D)
    slope = 0.5 * (1.0 + inner) + (0.5 * ROOT) * pre * (1.0 - inner * inner) * (
        1.0 + 3.0 * CUBE * squared
    )
    dhidden = dot(grads, second[0], 1, 1).astype(BF).astype(F32)
    dpre = (dhidden * slope).astype(BF)
    dpre_out[...] = dpre.reshape(NDP, SL, D)
    result = dot(dpre, first[0], 1, 1)
    for half in range(2):

        @pl.when(pl.program_id(0) == half)
        def _():
            store_quarters(part, half, result)


def experts_backward(arrived, delta, first, second):
    rows = pl.BlockSpec((NDP, SL, D), lambda p: (0, p, 0))
    weights = pl.BlockSpec((1, D, D), lambda p: (p, 0, 0))
    return pl.pallas_call(
        experts_backward_kernel,
        grid=(2,),
        in_specs=[rows, rows, weights, weights],
        out_specs=[pl.BlockSpec((NT, NDP * SL, 2 * Q), lambda p: (0, 0, 0)), rows, rows],
        out_shape=[
            jax.ShapeDtypeStruct((NT, NDP * SL, 2 * Q), BF),
            jax.ShapeDtypeStruct((NDP, 2 * SL, D), BF),
            jax.ShapeDtypeStruct((NDP, 2 * SL, D), BF),
        ],
        compiler_params=params(),
        name="experts_backward",
    )(arrived, delta, first, second)


def expert_grads_kernel(a0, a1, b0, b1, c0, c1, d0, d1, grad_first, grad_second):
    def flat(ref):
        return ref[...].reshape(NDP * SL, D)

    grad_first[0] = dot(flat(a0), flat(b0), 0, 0) + dot(flat(a1), flat(b1), 0, 0)
    grad_second[0] = dot(flat(c0), flat(d0), 0, 0) + dot(flat(c1), flat(d1), 0, 0)


def expert_grads(*inputs):
    rows = pl.BlockSpec((NDP, SL, D), lambda p: (0, p, 0))
    weights = pl.BlockSpec((1, D, D), lambda p: (p, 0, 0))
    return pl.pallas_call(
        expert_grads_kernel,
        grid=(2,),
        in_specs=[rows] * 8,
        out_specs=[weights, weights],
        out_shape=[jax.ShapeDtypeStruct((2, D, D), F32)] * 2,
        compiler_params=params(),
        name="expert_grads",
    )(*inputs)


def gathered(returned, meta, k):
    position = meta[:, 34 + k : 35 + k].astype(jnp.int32)
    place = jnp.where(position >= 0, (position // 64) * SL + position % SL, -1)
    odd = (position // SL) % 2 == 1
    hot = lax.broadcasted_iota(jnp.int32, (NR, NDP * SL), 1) == place
    both = dot(jnp.where(hot, 1.0, 0.0).astype(BF), returned)
    return jnp.where(odd, both[:, Q:], both[:, :Q])


def combine_kernel(returned, x1, meta, packed, pieces):
    member = lax.axis_index("tensor")
    live = meta[:, 38:39]
    total = column_quarter(x1, member)
    for k in range(2):
        piece = gathered(returned[...], meta, k)
        pieces[k] = piece.astype(BF)
        total = total + meta[:, 32 + k : 33 + k] * piece
    total = (total * live).astype(BF)
    packed[:, :Q] = total[:R]
    packed[:, Q:] = total[R:]


def combine(returned, x1, meta):
    return pl.pallas_call(
        combine_kernel,
        out_shape=[
            jax.ShapeDtypeStruct((R, 2 * Q), BF),
            jax.ShapeDtypeStruct((2, NR, Q), BF),
        ],
        compiler_params=params(),
        name="combine",
    )(returned, x1, meta)


def spread_kernel(delta, meta, outbox):
    values = delta[...].astype(F32) * meta[:, 38:39]
    slots = lax.broadcasted_iota(jnp.int32, (NR, EXPERTS * SL), 1)
    total = None
    for k in range(2):
        position = meta[:, 34 + k : 35 + k].astype(jnp.int32)
        hot = jnp.where(slots == position, 1.0, 0.0).astype(BF)
        scaled = (values * meta[:, 32 + k : 33 + k]).astype(BF)
        term = dot(hot, scaled, 0, 0)
        total = term if total is None else total + term
    outbox[...] = total.astype(BF)


def spread(delta, meta):
    return pl.pallas_call(
        spread_kernel,
        out_shape=jax.ShapeDtypeStruct((EXPERTS * SL, D), BF),
        compiler_params=params(),
        name="spread",
    )(delta, meta)


def collect_kernel(returned, meta, pieces, delta, packed, dpicks):
    member = lax.axis_index("tensor")
    total = None
    lanes = lax.broadcasted_iota(jnp.int32, (NR, 128), 1)
    columns = jnp.zeros((NR, 128), F32)
    part = column_quarter(delta, member).astype(F32) * meta[:, 38:39]
    for k in range(2):
        piece = gathered(returned[...], meta, k)
        total = piece if total is None else total + piece
        dots = jnp.sum(pieces[k].astype(F32) * part, axis=1, keepdims=True)
        columns = jnp.where(lanes == k, dots, columns)
    total = total.astype(BF)
    packed[:, :Q] = total[:R]
    packed[:, Q:] = total[R:]
    dpicks[:, :NR] = jnp.transpose(columns)[:8]
    dpicks[:, NR:] = jnp.zeros((8, 512 - NR), F32)


def collect(returned, meta, pieces, delta):
    return pl.pallas_call(
        collect_kernel,
        out_shape=[jax.ShapeDtypeStruct((R, 2 * Q), BF), jax.ShapeDtypeStruct((8, 512), F32)],
        compiler_params=params(),
        name="collect",
    )(returned, meta, pieces, delta)


def halves(values):
    high = values.astype(BF)
    return high, (values - high.astype(F32)).astype(BF)


def layer_backward_kernel(
    packed, dpicks, delta, x1, meta, gain_two, router, state, gain_one, qkv, ctx, project, output,
    part, dx1_out, grads, grad_gain, dqkv,
):
    live = meta[:, 38:39]
    gate = meta[:, 0:EXPERTS]
    dx2 = delta[...].astype(F32) * live
    total = dpicks[0] + dpicks[1] + dpicks[2] + dpicks[3]
    total = jnp.concatenate([total, jnp.zeros((120, 512), F32)], axis=0)
    columns = jnp.transpose(total)[:NR]
    experts = lax.broadcasted_iota(jnp.int32, (NR, EXPERTS), 1)
    dgate = jnp.zeros((NR, EXPERTS), F32)
    for k in range(2):
        route = meta[:, 36 + k : 37 + k].astype(jnp.int32)
        dgate = dgate + jnp.where(route == experts, columns[:, k : k + 1] * live, 0.0)
    dlogits = gate * (dgate - jnp.sum(gate * dgate, axis=-1, keepdims=True))
    normal, inverse = norm_parts(x1[...])
    normed = (normal * gain_two[...]).astype(BF)
    high, low = halves(dlogits)
    grads[:, 768:800] = dot(normed, high, 0, 0) + dot(normed, low, 0, 0)
    grads[:, 800:] = jnp.zeros((D, GP - 800), F32)
    dz2 = unpack(packed).astype(F32) + dot(high, router[...], 1, 1) + dot(low, router[...], 1, 1)
    grad_gain[...] = jnp.broadcast_to(jnp.sum(dz2 * normal, axis=0, keepdims=True), (8, D))
    dx1 = dx2 + norm_back(dz2, gain_two[...], normal, inverse)
    dx1_out[...] = dx1
    dattn = dx1.astype(BF)
    grads[:, 576:768] = dot(dattn, ctx[...], 0, 0)
    dctx = dot(dattn, output[...], 1, 1).astype(BF)
    scale = HD**-0.5
    projected = qkv[...]
    for image in range(2):
        rows = slice(image * R, (image + 1) * R)
        for head in range(NH):
            queries, keys, values = head_parts(projected, image, head)
            dc = dctx[rows, head * HD : (head + 1) * HD]
            weights = probabilities(queries, keys)
            dweights = dot(dc, values, 1, 1)
            dvalues = dot(weights.astype(BF), dc, 0, 0)
            dscores = weights * (dweights - jnp.sum(weights * dweights, axis=-1, keepdims=True))
            dscores = dscores.astype(BF)
            dqueries = dot(dscores, keys) * scale
            dkeys = dot(dscores, queries, 0, 0) * scale
            for number, value in enumerate((dqueries, dkeys, dvalues)):
                start = number * GW + head * HD
                dqkv[rows, start : start + HD] = value.astype(BF)
    normal_one, _ = norm_parts(state[...].astype(F32))
    normed_one = (normal_one * gain_one[...]).astype(BF)
    part[...] = dot(dqkv[...], project[...], 1, 1).astype(BF)
    grads[:, 0:576] = dot(normed_one, dqkv[...], 0, 0)


def layer_backward(*inputs):
    return pl.pallas_call(
        layer_backward_kernel,
        out_shape=[
            jax.ShapeDtypeStruct((NR, D), BF),
            jax.ShapeDtypeStruct((NR, D), F32),
            jax.ShapeDtypeStruct((D, GP), F32),
            jax.ShapeDtypeStruct((8, D), F32),
        ],
        scratch_shapes=[pltpu.VMEM((NR, 3 * GW), BF)],
        compiler_params=params(),
        name="layer_backward",
    )(*inputs)


def greet(tensor=False, dp=False, pipe=False):
    barrier = pltpu.get_barrier_semaphore()
    count = 0
    for used, axis, size in ((tensor, "tensor", NT), (dp, "dp", NDP), (pipe, "pipe", 2)):
        if used:
            me = lax.axis_index(axis)
            for step in range(1, size):
                pl.semaphore_signal(
                    barrier, inc=1, device_id={axis: (me + step) % size}, device_id_type=MESH
                )
            count += size - 1
    return barrier, count


def send(source, target, send_sem, recv_sem, axis, peer):
    copy = pltpu.make_async_remote_copy(
        src_ref=source,
        dst_ref=target,
        send_sem=send_sem,
        recv_sem=recv_sem,
        device_id={axis: peer},
        device_id_type=MESH,
    )
    copy.start()
    return copy


def add_up(own, held, me, count):
    total = own.astype(F32)
    for step in range(1, count):
        total = total + held[(me + step) % count].astype(F32)
    return total


def sum_tensor_kernel(part, result, held, mine, sems):
    barrier, count = greet(tensor=True)
    pl.semaphore_wait(barrier, count)
    me = lax.axis_index("tensor")
    copies = []
    for step in range(1, NT):
        peer = (me + step) % NT
        copies.append(
            send(part.at[peer], held.at[me], sems.at[0, step], sems.at[1, step], "tensor", peer)
        )
    for copy in copies:
        copy.wait()
    mine[...] = add_up(part[me], held, me, NT).astype(BF)
    copies = []
    for step in range(1, NT):
        peer = (me + step) % NT
        copies.append(
            send(mine, result.at[me], sems.at[2, step], sems.at[3, step], "tensor", peer)
        )
    result[me] = mine[...]
    for copy in copies:
        copy.wait()


def sum_tensor(part):
    return pl.pallas_call(
        sum_tensor_kernel,
        in_specs=[pl.BlockSpec(memory_space=pltpu.VMEM)],
        out_specs=pl.BlockSpec(memory_space=pltpu.VMEM),
        out_shape=jax.ShapeDtypeStruct((NT, CH, D), BF),
        scratch_shapes=[
            pltpu.VMEM((NT, CH, D), BF),
            pltpu.VMEM((CH, D), BF),
            pltpu.SemaphoreType.DMA((4, NT)),
        ],
        compiler_params=params(collective_id=1, has_side_effects=True),
        name="sum_tensor",
    )(part.reshape(NT, CH, D)).reshape(NR, D)


def to_experts_kernel(outbox, result, sems):
    barrier, count = greet(dp=True)
    me = lax.axis_index("dp")
    result[me] = outbox[me]
    pl.semaphore_wait(barrier, count)
    copies = []
    for step in range(1, NDP):
        peer = (me + step) % NDP
        copies.append(
            send(outbox.at[peer], result.at[me], sems.at[0, step], sems.at[1, step], "dp", peer)
        )
    for copy in copies:
        copy.wait()


def to_experts(outbox):
    return pl.pallas_call(
        to_experts_kernel,
        in_specs=[pl.BlockSpec(memory_space=pltpu.VMEM)],
        out_specs=pl.BlockSpec(memory_space=pltpu.VMEM),
        out_shape=jax.ShapeDtypeStruct((NDP, 2 * SL, D), BF),
        scratch_shapes=[pltpu.SemaphoreType.DMA((2, NDP))],
        compiler_params=params(collective_id=2, has_side_effects=True),
        name="to_experts",
    )(outbox.reshape(NDP, 2 * SL, D))


def to_tokens_kernel(part, result, held, mine, sums, copies_sems):
    barrier, count = greet(tensor=True, dp=True)
    pl.semaphore_wait(barrier, count)
    me = lax.axis_index("tensor")
    home = lax.axis_index("dp")
    group = home // 4
    scattered = []
    for turn in range(4):
        block = ((group + turn + 1) % 4) * 4
        for step in range(1, NT):
            peer = (me + step) % NT
            scattered.append(
                send(
                    part.at[peer, pl.ds(block, 4)],
                    held.at[me, pl.ds(block, 4)],
                    sums.at[0, turn, step],
                    sums.at[1, turn, step],
                    "tensor",
                    peer,
                )
            )
    returned = []
    for turn in range(4):
        block = ((group + turn + 1) % 4) * 4
        for step in range(1, NT):
            scattered[turn * 3 + step - 1].wait_recv()
        total = part[me, pl.ds(block, 4)].astype(F32)
        for step in range(1, NT):
            total = total + held[(me + step) % NT, pl.ds(block, 4)].astype(F32)
        mine[pl.ds(block, 4)] = total.astype(BF)
        for number in range(4):
            if turn < 3:
                offset = (turn + 1) * 4 + number
                peer = block + (home + number) % 4
                returned.append((offset, peer))
            elif number > 0:
                offset = number
                peer = block + (home + number) % 4
                returned.append((offset, peer))
            else:
                result[home] = mine[home]
                continue
            returned[-1] = send(
                mine.at[peer],
                result.at[home],
                copies_sems.at[0, offset],
                copies_sems.at[1, offset],
                "dp",
                peer,
            )
    for copy in returned:
        copy.wait()
    for copy in scattered:
        copy.wait_send()


def to_tokens(part):
    return pl.pallas_call(
        to_tokens_kernel,
        in_specs=[pl.BlockSpec(memory_space=pltpu.VMEM)],
        out_specs=pl.BlockSpec(memory_space=pltpu.VMEM),
        out_shape=jax.ShapeDtypeStruct((NDP, SL, 2 * Q), BF),
        scratch_shapes=[
            pltpu.VMEM((NT, NDP, SL, 2 * Q), BF),
            pltpu.VMEM((NDP, SL, 2 * Q), BF),
            pltpu.SemaphoreType.DMA((2, 4, NT)),
            pltpu.SemaphoreType.DMA((2, NDP)),
        ],
        compiler_params=params(collective_id=3, has_side_effects=True),
        name="to_tokens",
    )(part.reshape(NT, NDP, SL, 2 * Q)).reshape(NDP * SL, 2 * Q)


def gather_over_tensor(source, result, sems, row):
    me = lax.axis_index("tensor")
    copies = []
    for step in range(1, NT):
        peer = (me + step) % NT
        copies.append(
            send(
                source, result.at[me], sems.at[row, step], sems.at[row + 1, step], "tensor", peer
            )
        )
    return copies


def next_stage_kernel(packed, result, near, chosen, sems):
    barrier, count = greet(tensor=True, pipe=True)
    pl.semaphore_wait(barrier, count)
    stage = lax.axis_index("pipe")
    across = send(packed, near, sems.at[0, 0], sems.at[1, 0], "pipe", 1 - stage)
    across.wait_recv()
    chosen[...] = jnp.where(stage == 0, packed[...], near[...])
    copies = gather_over_tensor(chosen, result, sems, 0)
    result[lax.axis_index("tensor")] = chosen[...]
    for copy in copies:
        copy.wait()
    across.wait_send()


def next_stage(packed):
    return pl.pallas_call(
        next_stage_kernel,
        in_specs=[pl.BlockSpec(memory_space=pltpu.VMEM)],
        out_specs=pl.BlockSpec(memory_space=pltpu.VMEM),
        out_shape=jax.ShapeDtypeStruct((NT, R, 2 * Q), BF),
        scratch_shapes=[
            pltpu.VMEM((R, 2 * Q), BF),
            pltpu.VMEM((R, 2 * Q), BF),
            pltpu.SemaphoreType.DMA((2, NT)),
        ],
        compiler_params=params(collective_id=4, has_side_effects=True),
        name="next_stage",
    )(packed)


def gather_kernel(packed, dpicks, result, dpicks_all, sems):
    barrier, count = greet(tensor=True)
    pl.semaphore_wait(barrier, count)
    me = lax.axis_index("tensor")
    copies = gather_over_tensor(packed, result, sems, 0)
    copies += gather_over_tensor(dpicks, dpicks_all, sems, 2)
    result[me] = packed[...]
    dpicks_all[me] = dpicks[...]
    for copy in copies:
        copy.wait()


def gather(packed, dpicks):
    return pl.pallas_call(
        gather_kernel,
        in_specs=[pl.BlockSpec(memory_space=pltpu.VMEM)] * 2,
        out_specs=[pl.BlockSpec(memory_space=pltpu.VMEM)] * 2,
        out_shape=[
            jax.ShapeDtypeStruct((NT, R, 2 * Q), BF),
            jax.ShapeDtypeStruct((NT, 8, 512), F32),
        ],
        scratch_shapes=[pltpu.SemaphoreType.DMA((4, NT))],
        compiler_params=params(collective_id=5, has_side_effects=True),
        name="gather",
    )(packed, dpicks)


def state_grad_kernel(
    piped, part, dx1, state, gain, result, chunk, gains, held, near, chosen, own, sems
):
    barrier, count = greet(tensor=True, pipe=piped)
    pl.semaphore_wait(barrier, count)
    me = lax.axis_index("tensor")
    stage = lax.axis_index("pipe")
    copies = []
    for step in range(1, NT):
        peer = (me + step) % NT
        copies.append(
            send(part.at[peer], held.at[me], sems.at[0, step], sems.at[1, step], "tensor", peer)
        )
    normal, inverse = norm_parts(state[me].astype(F32))
    for copy in copies:
        copy.wait()
    dz1 = add_up(part[me], held, me, NT)
    chunk[...] = (dx1[me] + norm_back(dz1, gain[...], normal, inverse)).astype(BF)
    if piped:
        across = send(chunk, near, sems.at[0, 0], sems.at[1, 0], "pipe", 1 - stage)
    own[...] = jnp.broadcast_to(jnp.sum(dz1 * normal, axis=0, keepdims=True), (8, D))
    small = gather_over_tensor(own, gains, sems, 2)
    gains[me] = own[...]
    if piped:
        across.wait_recv()
        chosen[...] = jnp.where(stage == 1, chunk[...], near[...])
    else:
        chosen[...] = chunk[...]
    copies = gather_over_tensor(chosen, result, sems, 4)
    result[me] = chosen[...]
    for copy in copies + small:
        copy.wait()
    if piped:
        across.wait_send()


def state_grad(piped, part, dx1, state, gain):
    result, chunk, gains = pl.pallas_call(
        functools.partial(state_grad_kernel, piped),
        in_specs=[pl.BlockSpec(memory_space=pltpu.VMEM)] * 4,
        out_specs=[pl.BlockSpec(memory_space=pltpu.VMEM)] * 3,
        out_shape=[
            jax.ShapeDtypeStruct((NT, CH, D), BF),
            jax.ShapeDtypeStruct((CH, D), BF),
            jax.ShapeDtypeStruct((NT, 8, D), F32),
        ],
        scratch_shapes=[
            pltpu.VMEM((NT, CH, D), BF),
            pltpu.VMEM((CH, D), BF),
            pltpu.VMEM((CH, D), BF),
            pltpu.VMEM((8, D), F32),
            pltpu.SemaphoreType.DMA((6, NT)),
        ],
        compiler_params=params(collective_id=6 if piped else 7, has_side_effects=True),
        name="state_grad",
    )(part.reshape(NT, CH, D), dx1.reshape(NT, CH, D), state.reshape(NT, CH, D), gain)
    return result.reshape(NR, D), chunk, gains


GR = D // NDP


def sum_dp_kernel(part, result, held, mine, sems):
    barrier, count = greet(dp=True)
    pl.semaphore_wait(barrier, count)
    me = lax.axis_index("dp")
    copies = []
    for step in range(1, NDP):
        peer = (me + step) % NDP
        copies.append(
            send(part.at[peer], held.at[me], sems.at[0, step], sems.at[1, step], "dp", peer)
        )
    for copy in copies:
        copy.wait()
    mine[...] = add_up(part[me], held, me, NDP).astype(BF)
    copies = []
    for step in range(1, NDP):
        peer = (me + step) % NDP
        copies.append(send(mine, result.at[me], sems.at[2, step], sems.at[3, step], "dp", peer))
    result[me] = mine[...]
    for copy in copies:
        copy.wait()


def sum_dp(part):
    return pl.pallas_call(
        sum_dp_kernel,
        in_specs=[pl.BlockSpec(memory_space=pltpu.VMEM)],
        out_specs=pl.BlockSpec(memory_space=pltpu.VMEM),
        out_shape=jax.ShapeDtypeStruct((NDP, GR, GP), BF),
        scratch_shapes=[
            pltpu.VMEM((NDP, GR, GP), BF),
            pltpu.VMEM((GR, GP), BF),
            pltpu.SemaphoreType.DMA((4, NDP)),
        ],
        compiler_params=params(collective_id=8, has_side_effects=True),
        name="sum_dp",
    )(part.reshape(NDP, GR, GP)).reshape(D, GP)


def pad_rows(values):
    micro, _, width = values.shape
    values = values.reshape(micro, 2, IMG_LEN, width)
    return jnp.pad(values, ((0, 0), (0, 0), (0, R - IMG_LEN), (0, 0))).reshape(micro, NR, width)


def unpad_rows(values):
    lead = values.shape[:-2]
    width = values.shape[-1]
    values = values.reshape(*lead, 2, R, width)[..., :IMG_LEN, :]
    return values.reshape(*lead, 2 * IMG_LEN, width)


def unpack_rows(gathered_parts):
    micro = gathered_parts.shape[1]
    values = gathered_parts[:, :, :IMG_LEN].reshape(NT, micro, IMG_LEN, 2, Q)
    return values.transpose(1, 3, 2, 0, 4).reshape(micro, 2 * IMG_LEN, D)


def body(
    tokens,
    cotangent,
    image_counts,
    routes,
    attn_norm_gain,
    query_key_value,
    attn_output,
    moe_norm_gain,
    router_weight,
    expert_in,
    expert_down,
):
    gain_one = attn_norm_gain
    gain_two = moe_norm_gain
    project = query_key_value[0].reshape(D, 3 * GW)
    output = attn_output[0]
    router = router_weight[0]
    first, second = expert_in[0], expert_down[0]
    stage = lax.axis_index("pipe")
    early = stage == 0
    counts = image_counts[:, lax.axis_index("dp")].reshape(2, 1, 1)
    plain = pad_rows(tokens)
    upstream = pad_rows(cotangent)
    paths = pad_rows(routes)

    def chosen(one, other):
        return jax.tree.map(lambda a, b: jnp.where(early, a, b), one, other)

    saved = []
    packed_list = []
    arriving = None
    for moment in range(3):
        if moment == 0:
            mode, inputs = "plain", (plain[0],)
            count, path = counts[0], paths[0]
        elif moment == 1:
            mode, inputs = "mixed", (plain[1], arriving)
            count, path = chosen((counts[1], paths[1]), (counts[0], paths[0]))
        else:
            mode, inputs = "packed", (arriving,)
            count, path = counts[1], paths[1]
        results = attention_forward(mode, inputs, gain_one, project, output)
        part, qkv, ctx = results[:3]
        state = inputs[0] if mode == "plain" else results[3]
        outbox, x1, meta = dispatch(count, state, sum_tensor(part), gain_two, router, path)
        arrived = to_experts(outbox)
        returned = to_tokens(experts_forward(arrived, first, second))
        packed, pieces = combine(returned, x1, meta)
        packed_list.append(packed)
        saved.append((state, qkv, ctx, x1, meta, arrived, pieces))
        if moment < 2:
            arriving = next_stage(packed)

    late_stored = [saved[1], chosen(saved[0], saved[2]), saved[1]]
    terms = []
    chunks = []
    gathered_grads = []
    arriving = None
    for moment in range(3):
        state, qkv, ctx, x1, meta, arrived, pieces = late_stored[moment]
        if moment == 0:
            delta = upstream[0]
        elif moment == 1:
            delta = jnp.where(early, arriving, upstream[1])
        else:
            delta = arriving
        delta_arrived = to_experts(spread(delta, meta))
        part, hidden, dpre = experts_backward(arrived, delta_arrived, first, second)
        returned = to_tokens(part)
        packed, dpicks = collect(returned, meta, pieces, delta)
        packed, dpicks = gather(packed, dpicks)
        part, dx1, grads, grad_gain_two = layer_backward(
            packed, dpicks, delta, x1, meta, gain_two, router, state, gain_one, qkv, ctx, project,
            output,
        )
        arriving, chunk, grad_gain_one = state_grad(moment < 2, part, dx1, state, gain_one)
        gathered_grads.append(arriving)
        chunks.append(chunk)
        terms.append(
            (
                (grads, grad_gain_two[0], grad_gain_one[:, 0].sum(axis=0)),
                (arrived, dpre, hidden, delta_arrived),
            )
        )
    ends = chosen(terms[2], terms[0])
    grads, grad_gain_two, grad_gain_one = jax.tree.map(jnp.add, terms[1][0], ends[0])
    pairs = [half for pair in zip(terms[1][1], ends[1]) for half in pair]
    grad_first, grad_second = expert_grads(*pairs)
    columns = jnp.stack([grad_gain_two, grad_gain_one], axis=1)
    whole = jnp.concatenate([grads[:, :800], columns, grads[:, 802:]], axis=1)
    whole = sum_dp(whole.astype(BF)).astype(F32)

    late_packed = jnp.stack([chosen(packed_list[0], packed_list[1]), chosen(packed_list[1], packed_list[2])])
    section_out = unpack_rows(lax.all_gather(late_packed, "tensor"))
    own = lax.all_gather(chunks[1], "tensor").reshape(NR, D)
    input_grad = unpad_rows(
        jnp.stack(
            [jnp.where(early, own, gathered_grads[0]), jnp.where(early, gathered_grads[2], gathered_grads[1])]
        )
    )
    return (
        section_out[None],
        input_grad[None],
        whole[:, 801][None],
        whole[:, :576].reshape(1, D, 3, GW),
        whole[:, 576:768].T[None],
        whole[:, 800][None],
        whole[:, 768:800][None],
        grad_first[None],
        grad_second[None],
    )


def solution(mesh):
    placed = (
        P(None, "dp", None),
        P(None, "dp", None),
        P(),
        P(None, "dp", None),
        P("pipe", None),
        P("pipe", None, None, "tensor"),
        P("pipe", "tensor", None),
        P("pipe", None),
        P("pipe", None, None),
        P("pipe", "dp", None, "tensor"),
        P("pipe", "dp", "tensor", None),
    )
    return jax.shard_map(
        body,
        mesh=mesh,
        in_specs=placed,
        out_specs=(
            P("pipe", None, "dp", None),
            P("pipe", None, "dp", None),
            P("pipe", None),
            P("pipe", None, None, "tensor"),
            P("pipe", "tensor", None),
            P("pipe", None),
            P("pipe", None, None),
            P("pipe", "dp", None, "tensor"),
            P("pipe", "dp", "tensor", None),
        ),
        check_vma=False,
    )
```

```python
import functools

import jax
import jax.numpy as jnp
from jax import lax
from jax.experimental import pallas as pl
from jax.experimental.pallas import tpu as pltpu
from jax.sharding import PartitionSpec as P

BF = jnp.bfloat16
F32 = jnp.float32
MESH = pl.DeviceIdType.MESH
D = 768
HD = 64
NH = 3
GW = NH * HD
IMG_LEN = 197
R = 224
NR = 2 * R
CH = NR // 4
EXPERTS = 32
SL = 32
NT = 4
NDP = 16
Q = D // NT
EPSILON = 1e-06
VMEM_BYTES = 48 * 1024 * 1024
GP = 896


def dot(a, b, ca=1, cb=0):
    return lax.dot_general(a, b, (((ca,), (cb,)), ((), ())), preferred_element_type=F32)


def params(**more):
    return pltpu.CompilerParams(vmem_limit_bytes=VMEM_BYTES, **more)


def norm_parts(values):
    mean = jnp.mean(values, axis=-1, keepdims=True)
    centred = values - mean
    inverse = lax.rsqrt(jnp.mean(centred * centred, axis=-1, keepdims=True) + EPSILON)
    return centred * inverse, inverse


def norm_back(delta, gain, normal, inverse):
    scaled = delta * gain
    return inverse * (
        scaled
        - jnp.mean(scaled, axis=-1, keepdims=True)
        - normal * jnp.mean(scaled * normal, axis=-1, keepdims=True)
    )


def pick(index, options):
    result = options[0]
    for number in range(1, len(options)):
        result = jnp.where(index == number, options[number], result)
    return result


def column_quarter(values, member):
    return pick(member, [values[:, Q * q : Q * (q + 1)] for q in range(NT)])


def unpack(packed):
    images = [
        jnp.concatenate([packed[q][:, Q * i : Q * (i + 1)] for q in range(NT)], axis=1)
        for i in range(2)
    ]
    return jnp.concatenate(images, axis=0)


def head_parts(projected, image, head):
    rows = slice(image * R, (image + 1) * R)
    return [
        projected[rows, part * GW + head * HD : part * GW + (head + 1) * HD] for part in range(3)
    ]


def probabilities(queries, keys):
    scores = dot(queries, keys, 1, 1) * (HD**-0.5)
    held = lax.broadcasted_iota(jnp.int32, scores.shape, 1) < IMG_LEN
    scores = jnp.where(held, scores, -1e30)
    exponent = jnp.exp(scores - jnp.max(scores, axis=-1, keepdims=True))
    return exponent / jnp.sum(exponent, axis=-1, keepdims=True)


VMEM = pl.BlockSpec(memory_space=pltpu.VMEM)
SMEM = pl.BlockSpec(memory_space=pltpu.SMEM)
ANYWHERE = pl.BlockSpec(memory_space=pl.ANY)


class Part:
    def __init__(self, steps, inputs, outs, scratch, specs=None):
        self.steps = steps
        self.inputs = inputs
        self.outs = outs
        self.scratch = scratch
        self.specs = specs or [VMEM] * len(inputs)


def drive(running):
    running = list(running)
    while running:
        for steps in list(running):
            if next(steps, StopIteration) is StopIteration:
                running.remove(steps)


def greet(axes):
    barrier = pltpu.get_barrier_semaphore()
    count = 0
    for axis in axes:
        size = lax.axis_size(axis)
        me = lax.axis_index(axis)
        for step in range(1, size):
            pl.semaphore_signal(
                barrier, inc=1, device_id={axis: (me + step) % size}, device_id_type=MESH
            )
        count += size - 1
    return barrier, count


def run(name, number, axes, parts):
    def kernel(*refs):
        barrier, count = greet(axes)
        ins = sum(len(part.inputs) for part in parts)
        outs = sum(len(part.outs) for part in parts)
        place = [0, ins, ins + outs]
        running = []
        for part in parts:
            pieces = []
            for which, items in enumerate((part.inputs, part.outs, part.scratch)):
                pieces.append(refs[place[which] : place[which] + len(items)])
                place[which] += len(items)
            running.append(part.steps(*pieces))
        running = [steps for steps in running if next(steps, StopIteration) is not StopIteration]
        pl.semaphore_wait(barrier, count)
        drive(running)

    flat = [item for part in parts for item in part.inputs]
    results = pl.pallas_call(
        kernel,
        in_specs=[spec for part in parts for spec in part.specs],
        out_specs=[VMEM for part in parts for _ in part.outs],
        out_shape=[jax.ShapeDtypeStruct(*out) for part in parts for out in part.outs],
        scratch_shapes=[item for part in parts for item in part.scratch],
        compiler_params=params(collective_id=number, has_side_effects=True),
        name=name,
    )(*flat)
    split = []
    for part in parts:
        split.append(results[: len(part.outs)])
        results = results[len(part.outs) :]
    return split


def send(source, target, send_sem, recv_sem, axis, peer):
    copy = pltpu.make_async_remote_copy(
        src_ref=source,
        dst_ref=target,
        send_sem=send_sem,
        recv_sem=recv_sem,
        device_id={axis: peer},
        device_id_type=MESH,
    )
    copy.start()
    return copy


def sems(*shape):
    return pltpu.SemaphoreType.DMA(shape)


def spread_over_tensor(source, target_of, pairs, row):
    me = lax.axis_index("tensor")
    return [
        send(
            source, target_of(me), pairs.at[row, step], pairs.at[row + 1, step], "tensor",
            (me + step) % NT,
        )
        for step in range(1, NT)
    ]


def attention_part(mode, inputs, gain, project, output):
    def steps(ins, outs, scratch):
        part, held, mine, pairs = scratch
        if mode == "plain":
            plain, gain, project, output = ins
            summed, qkv, ctx = outs
            state = plain[...]
        else:
            summed, qkv, ctx, kept = outs
            if mode == "packed":
                packed, gain, project, output = ins
                state = unpack(packed)
            else:
                plain, packed, gain, project, output = ins
                state = jnp.where(lax.axis_index("pipe") == 0, plain[...], unpack(packed))
            kept[...] = state
        normal, _ = norm_parts(state.astype(F32))
        normed = (normal * gain[...]).astype(BF)
        projected = dot(normed, project[...]).astype(BF)
        qkv[...] = projected
        for image in range(2):
            for head in range(NH):
                queries, keys, values = head_parts(projected, image, head)
                weights = probabilities(queries, keys).astype(BF)
                ctx[image * R : (image + 1) * R, head * HD : (head + 1) * HD] = dot(
                    weights, values
                ).astype(BF)
        part[...] = dot(ctx[...], output[...]).astype(BF).reshape(NT, CH, D)
        yield
        me = lax.axis_index("tensor")
        copies = [
            send(
                part.at[(me + step) % NT], held.at[me], pairs.at[0, step], pairs.at[1, step],
                "tensor", (me + step) % NT,
            )
            for step in range(1, NT)
        ]
        yield
        for copy in copies:
            copy.wait()
        total = part[me].astype(F32)
        for step in range(1, NT):
            total = total + held[(me + step) % NT].astype(F32)
        mine[...] = total.astype(BF)
        copies = spread_over_tensor(mine, lambda me: summed.at[me], pairs, 2)
        summed[me] = mine[...]
        yield
        for copy in copies:
            copy.wait()

    outs = [((NT, CH, D), BF), ((NR, 3 * GW), BF), ((NR, GW), BF)]
    if mode != "plain":
        outs.append(((NR, D), BF))
    return Part(
        steps,
        [*inputs, gain, project, output],
        outs,
        [
            pltpu.VMEM((NT, CH, D), BF),
            pltpu.VMEM((NT, CH, D), BF),
            pltpu.VMEM((CH, D), BF),
            sems(4, NT),
        ],
    )


RELATIVE = [(dy, dx, dc) for dy in (2, 1, 3, 0) for dx in (1, 0) for dc in (0, 1)]
RELATIVE.remove((0, 0, 0))


def peer_at(relative, sign):
    dy, dx, dc = relative
    me = lax.axis_index("dp")
    row = (me // 4 + sign * dy + 4) % 4
    return row * 4 + ((me // 2 + dx) % 2) * 2 + (me + dc) % 2


def quartered(relative):
    return relative[0] != 0 and relative[1] == 1


SHORT = [relative for relative in RELATIVE if quartered(relative)]


def to_experts(outbox, arrived, pairs, relayed, hybrid):
    me = lax.axis_index("dp")
    member = lax.axis_index("tensor")
    rows = pl.ds(pl.multiple_of(member * 16, 16), 16)
    direct, relays, order = [], [], []
    for number, relative in enumerate(RELATIVE):
        peer = peer_at(relative, 1)
        short = hybrid and quartered(relative)
        copy = send(
            outbox.at[peer, rows] if short else outbox.at[peer],
            arrived.at[me, rows] if short else arrived.at[me],
            pairs.at[0, number],
            pairs.at[1, number],
            "dp",
            peer,
        )
        if short:
            order.append((number, relative, copy))
        else:
            direct.append(copy)
    arrived[me] = outbox[me]
    yield
    order.sort(key=lambda item: item[1][0] == 2)
    for _, relative, copy in order:
        number = SHORT.index(relative)
        copy.wait_recv()
        source = peer_at(relative, -1)
        for step in range(1, NT):
            relays.append(
                send(
                    arrived.at[source, rows],
                    arrived.at[source, rows],
                    relayed.at[0, number, step],
                    relayed.at[1, number, step],
                    "tensor",
                    (member + step) % NT,
                )
            )
    for _ in range(6):
        yield
    for copy in direct:
        copy.wait()
    for _, _, copy in order:
        copy.wait_send()
    for copy in relays:
        copy.wait()


def to_experts_scratch(hybrid):
    return [
        pltpu.VMEM((NDP, 2 * SL, D), BF),
        sems(2, NDP),
        sems(2, len(SHORT), NT) if hybrid else sems(2, 1, 1),
    ]


def live_rows(count):
    row = lax.broadcasted_iota(jnp.int32, (NR, 1), 0)
    image = (row >= R).astype(jnp.int32)
    return (image < count) & (row - image * R < IMG_LEN)


def dispatch_part(hybrid, count, state, summed, gain, router, routes):
    def steps(ins, outs, scratch):
        count, state, summed, gain, router, routes = ins
        arrived, x1, meta = outs
        outbox, pairs, relayed = scratch
        values = state[...].astype(F32) + summed[...].reshape(NR, D).astype(F32)
        x1[...] = values
        normal, _ = norm_parts(values)
        normed = (normal * gain[...]).astype(BF)
        logits = dot(normed, router[...])
        exponent = jnp.exp(logits - jnp.max(logits, axis=-1, keepdims=True))
        gate = exponent / jnp.sum(exponent, axis=-1, keepdims=True)
        live = live_rows(count[0, 0])
        experts = lax.broadcasted_iota(jnp.int32, (NR, EXPERTS), 1)
        route = [routes[:, k : k + 1] for k in range(2)]
        match = [jnp.where(live & (route[k] == experts), 1.0, 0.0) for k in range(2)]
        above = lax.broadcasted_iota(jnp.int32, (NR, NR), 1) < lax.broadcasted_iota(
            jnp.int32, (NR, NR), 0
        )
        before = dot(jnp.where(above, 1.0, 0.0).astype(BF), (match[0] + match[1]).astype(BF))
        meta[:, 0:EXPERTS] = gate
        hot = None
        slots = lax.broadcasted_iota(jnp.int32, (NR, EXPERTS * SL), 1)
        for k in range(2):
            slot = jnp.sum(match[k] * before, axis=1, keepdims=True).astype(jnp.int32)
            position = jnp.where(live, route[k] * SL + slot, -1)
            meta[:, 32 + k : 33 + k] = jnp.sum(match[k] * gate, axis=1, keepdims=True)
            meta[:, 34 + k : 35 + k] = position.astype(F32)
            meta[:, 36 + k : 37 + k] = route[k].astype(F32)
            same = slots == position
            hot = same if hot is None else hot | same
        meta[:, 38:39] = jnp.where(live, 1.0, 0.0)
        result = dot(jnp.where(hot, 1.0, 0.0).astype(BF), normed, 0, 0).astype(BF)
        outbox[...] = result.reshape(NDP, 2 * SL, D)
        yield
        yield from to_experts(outbox, arrived, pairs, relayed, hybrid)

    return Part(
        steps,
        [count, state, summed, gain, router, routes],
        [((NDP, 2 * SL, D), BF), ((NR, D), F32), ((NR, 128), F32)],
        to_experts_scratch(hybrid),
        [SMEM] + [VMEM] * 5,
    )


def spread_part(hybrid, delta, meta):
    def steps(ins, outs, scratch):
        delta, meta = ins
        (arrived,) = outs
        outbox, pairs, relayed = scratch
        values = delta[...].astype(F32) * meta[:, 38:39]
        slots = lax.broadcasted_iota(jnp.int32, (NR, EXPERTS * SL), 1)
        total = None
        for k in range(2):
            position = meta[:, 34 + k : 35 + k].astype(jnp.int32)
            hot = jnp.where(slots == position, 1.0, 0.0).astype(BF)
            scaled = (values * meta[:, 32 + k : 33 + k]).astype(BF)
            term = dot(hot, scaled, 0, 0)
            total = term if total is None else total + term
        outbox[...] = total.astype(BF).reshape(NDP, 2 * SL, D)
        yield
        yield from to_experts(outbox, arrived, pairs, relayed, hybrid)

    return Part(steps, [delta, meta], [((NDP, 2 * SL, D), BF)], to_experts_scratch(hybrid))


CUBE = 0.044715
ROOT = 0.7978845608028654


def gelu_parts(pre):
    squared = pre * pre
    inner = jnp.tanh(ROOT * (pre + CUBE * pre * squared))
    return 0.5 * pre * (1.0 + inner), inner, squared


def store_quarters(target, expert, values):
    values = values.astype(BF).reshape(NDP, 2, 16, D)
    for q in range(NT):
        for half in range(2):
            target[q, expert, :, :, half * Q : (half + 1) * Q] = values[
                :, half, :, q * Q : (q + 1) * Q
            ]


def expert_steps(first, second, compute, result, scratch):
    w1, w2, loads, part, held, mine, sums, pairs = scratch
    loading = []
    for expert in range(2):
        for number, (source, target) in enumerate(((first, w1), (second, w2))):
            copy = pltpu.make_async_copy(
                source.at[expert], target.at[expert], loads.at[number, expert]
            )
            copy.start()
            loading.append(copy)
    loading[0].wait()
    store_quarters(part, 0, compute(0, w1, w2, loading[1]))
    yield
    me = lax.axis_index("tensor")
    home = lax.axis_index("dp")
    whole = [
        send(
            part.at[(me + step) % NT, 0], held.at[me, 0], sums.at[0, 4, step], sums.at[1, 4, step],
            "tensor", (me + step) % NT,
        )
        for step in range(1, NT)
    ]
    loading[2].wait()
    store_quarters(part, 1, compute(1, w1, w2, loading[3]))
    group = home // 4
    scattered = []
    for turn in range(4):
        block = ((group + turn + 1) % 4) * 4
        for step in range(1, NT):
            peer = (me + step) % NT
            scattered.append(
                send(
                    part.at[peer, 1, pl.ds(block, 4)],
                    held.at[me, 1, pl.ds(block, 4)],
                    sums.at[0, turn, step],
                    sums.at[1, turn, step],
                    "tensor",
                    peer,
                )
            )
    yield
    for copy in whole:
        copy.wait()
    total = part[me, 0].astype(F32)
    for step in range(1, NT):
        total = total + held[(me + step) % NT, 0].astype(F32)
    mine[:, 0] = total.astype(BF)
    returned = []
    for turn in range(4):
        block = ((group + turn + 1) % 4) * 4
        for step in range(1, NT):
            scattered[turn * 3 + step - 1].wait_recv()
        total = part[me, 1, pl.ds(block, 4)].astype(F32)
        for step in range(1, NT):
            total = total + held[(me + step) % NT, 1, pl.ds(block, 4)].astype(F32)
        mine[pl.ds(block, 4), 1] = total.astype(BF)
        for number in range(4):
            if turn == 3 and number == 0:
                result[home] = mine[home]
                continue
            offset = (turn + 1) % 4 * 4 + number
            peer = block + (home + number) % 4
            returned.append(
                send(
                    mine.at[peer], result.at[home], pairs.at[0, offset], pairs.at[1, offset], "dp",
                    peer,
                )
            )
        yield
    for copy in returned:
        copy.wait()
    for copy in scattered:
        copy.wait_send()


EXPERT_SCRATCH = [
    pltpu.VMEM((2, D, D), BF),
    pltpu.VMEM((2, D, D), BF),
    sems(2, 2),
    pltpu.VMEM((NT, 2, NDP, 16, 2 * Q), BF),
    pltpu.VMEM((NT, 2, NDP, 16, 2 * Q), BF),
    pltpu.VMEM((NDP, 2, 16, 2 * Q), BF),
    sems(2, 5, NT),
    sems(2, NDP),
]
RETURNED = ((NDP, 2, 16, 2 * Q), BF)


def expert_rows(ref, expert):
    return ref[:, expert * SL : (expert + 1) * SL].reshape(NDP * SL, D)


def experts_forward_part(arrived, first, second):
    def steps(ins, outs, scratch):
        arrived, first, second = ins

        def compute(expert, w1, w2, loading):
            hidden = gelu_parts(dot(expert_rows(arrived, expert), w1[expert]))[0].astype(BF)
            loading.wait()
            return dot(hidden, w2[expert])

        yield from expert_steps(first, second, compute, outs[0], scratch)

    return Part(
        steps, [arrived, first, second], [RETURNED], EXPERT_SCRATCH, [VMEM, ANYWHERE, ANYWHERE]
    )


def experts_backward_part(arrived, delta, first, second):
    def steps(ins, outs, scratch):
        arrived, delta, first, second = ins
        result, hidden_out, dpre_out = outs

        def compute(expert, w1, w2, loading):
            place = slice(expert * SL, (expert + 1) * SL)
            pre = dot(expert_rows(arrived, expert), w1[expert])
            hidden, inner, squared = gelu_parts(pre)
            hidden_out[:, place] = hidden.astype(BF).reshape(NDP, SL, D)
            slope = 0.5 * (1.0 + inner) + (0.5 * ROOT) * pre * (1.0 - inner * inner) * (
                1.0 + 3.0 * CUBE * squared
            )
            loading.wait()
            dhidden = dot(expert_rows(delta, expert), w2[expert], 1, 1).astype(BF).astype(F32)
            dpre = (dhidden * slope).astype(BF)
            dpre_out[:, place] = dpre.reshape(NDP, SL, D)
            return dot(dpre, w1[expert], 1, 1)

        yield from expert_steps(first, second, compute, result, scratch)

    rows = ((NDP, 2 * SL, D), BF)
    return Part(
        steps,
        [arrived, delta, first, second],
        [RETURNED, rows, rows],
        EXPERT_SCRATCH,
        [VMEM, VMEM, ANYWHERE, ANYWHERE],
    )


def expert_grads_kernel(stage, *refs):
    grad_first, grad_second = refs[12:]

    def flat(ref):
        return ref[...].reshape(NDP * SL, D)

    def pairs(a, b):
        grad_first[0] = dot(flat(a[0]), flat(a[1]), 0, 0) + dot(flat(b[0]), flat(b[1]), 0, 0)
        grad_second[0] = dot(flat(a[2]), flat(a[3]), 0, 0) + dot(flat(b[2]), flat(b[3]), 0, 0)

    @pl.when(stage[0] == 0)
    def _():
        pairs(refs[0:4], refs[4:8])

    @pl.when(stage[0] != 0)
    def _():
        pairs(refs[0:4], refs[8:12])


def expert_grads(stage, both, first_only, last_only):
    shape = (NDP, SL, D)
    weights = pl.BlockSpec((1, D, D), lambda p, s: (p, 0, 0))
    return pl.pallas_call(
        expert_grads_kernel,
        grid_spec=pltpu.PrefetchScalarGridSpec(
            num_scalar_prefetch=1,
            grid=(2,),
            in_specs=[pl.BlockSpec(shape, lambda p, s: (0, p, 0))] * 4
            + [pl.BlockSpec(shape, lambda p, s: (0, p * (1 - s[0]), 0))] * 4
            + [pl.BlockSpec(shape, lambda p, s: (0, p * s[0], 0))] * 4,
            out_specs=[weights, weights],
        ),
        out_shape=[jax.ShapeDtypeStruct((2, D, D), F32)] * 2,
        compiler_params=params(),
        name="expert_grads",
    )(stage, *both, *first_only, *last_only)


def gathered(returned, meta, k):
    position = meta[:, 34 + k : 35 + k].astype(jnp.int32)
    place = jnp.where(position >= 0, (position // SL) * 16 + position % 16, -1)
    odd = (position // 16) % 2 == 1
    hot = lax.broadcasted_iota(jnp.int32, (NR, NDP * SL), 1) == place
    both = dot(jnp.where(hot, 1.0, 0.0).astype(BF), returned)
    return jnp.where(odd, both[:, Q:], both[:, :Q])


HALVES = (slice(0, CH), slice(CH, R))


def combine_part(onward, returned, x1, meta):
    def steps(ins, outs, scratch):
        returned, x1, meta = ins
        packed, pieces = outs[:2]
        member = lax.axis_index("tensor")
        live = meta[:, 38:39]
        total = column_quarter(x1, member)
        rows = returned[...].reshape(NDP * SL, 2 * Q)
        for k in range(2):
            piece = gathered(rows, meta, k)
            pieces[k] = piece.astype(BF)
            total = total + meta[:, 32 + k : 33 + k] * piece
        total = (total * live).astype(BF)
        packed[:, :Q] = total[:R]
        packed[:, Q:] = total[R:]
        if not onward:
            return
        yield
        result = outs[2]
        near, chosen, across_sems, pairs = scratch
        stage = lax.axis_index("pipe")
        across = [
            send(
                packed.at[half], near.at[half], across_sems.at[0, i], across_sems.at[1, i], "pipe",
                1 - stage,
            )
            for i, half in enumerate(HALVES)
        ]
        copies = []
        for i, half in enumerate(HALVES):
            across[i].wait_recv()
            chosen[half] = jnp.where(stage == 0, packed[half], near[half])
            copies += spread_over_tensor(
                chosen.at[half], lambda me: result.at[me, half], pairs, 2 * i
            )
        result[member] = chosen[...]
        yield
        for copy in copies:
            copy.wait()
        for copy in across:
            copy.wait_send()

    outs = [((R, 2 * Q), BF), ((2, NR, Q), BF)]
    scratch = []
    if onward:
        outs.append(((NT, R, 2 * Q), BF))
        scratch = [pltpu.VMEM((R, 2 * Q), BF), pltpu.VMEM((R, 2 * Q), BF), sems(2, 2), sems(4, NT)]
    return Part(steps, [returned, x1, meta], outs, scratch)


def collect_part(returned, meta, pieces, delta):
    def steps(ins, outs, scratch):
        returned, meta, pieces, delta = ins
        result, dpicks_all = outs
        packed, dpicks, pairs = scratch
        member = lax.axis_index("tensor")
        total = None
        rows = returned[...].reshape(NDP * SL, 2 * Q)
        lanes = lax.broadcasted_iota(jnp.int32, (NR, 128), 1)
        columns = jnp.zeros((NR, 128), F32)
        part = column_quarter(delta, member).astype(F32) * meta[:, 38:39]
        for k in range(2):
            piece = gathered(rows, meta, k)
            total = piece if total is None else total + piece
            dots = jnp.sum(pieces[k].astype(F32) * part, axis=1, keepdims=True)
            columns = jnp.where(lanes == k, dots, columns)
        total = total.astype(BF)
        packed[:, :Q] = total[:R]
        packed[:, Q:] = total[R:]
        dpicks[:, :NR] = jnp.transpose(columns)[:8]
        dpicks[:, NR:] = jnp.zeros((8, 512 - NR), F32)
        yield
        copies = spread_over_tensor(packed, lambda me: result.at[me], pairs, 0)
        copies += spread_over_tensor(dpicks, lambda me: dpicks_all.at[me], pairs, 2)
        result[member] = packed[...]
        dpicks_all[member] = dpicks[...]
        for _ in range(6):
            yield
        for copy in copies:
            copy.wait()

    return Part(
        steps,
        [returned, meta, pieces, delta],
        [((NT, R, 2 * Q), BF), ((NT, 8, 512), F32)],
        [pltpu.VMEM((R, 2 * Q), BF), pltpu.VMEM((8, 512), F32), sems(4, NT)],
    )


def halves(values):
    high = values.astype(BF)
    return high, (values - high.astype(F32)).astype(BF)


RS_ROWS = ((0, 64), (64, 48))
GR = D // NDP


def sum_dp(pack, result, near, half, held, mine, tile, tiles, core_sems, chip_sems, tile_sems):
    home = lax.axis_index("dp")
    core = home % 2
    chip = home // 2
    partner = home + 1 - 2 * core
    copy = send(pack.at[1 - core], near, core_sems.at[0, 0], core_sems.at[1, 0], "dp", partner)
    yield
    copy.wait()
    half[...] = (pack[core].astype(F32) + near[...].astype(F32)).astype(BF)
    chips = [(dy, dx) for dy in (2, 1, 3, 0) for dx in (1, 0) if (dy, dx) != (0, 0)]

    def chip_at(dy, dx):
        return ((chip // 2 + dy) % 4) * 2 + (chip + dx) % 2

    copies = []
    for number, (dy, dx) in enumerate(chips):
        other = chip_at(dy, dx)
        copies.append(
            send(
                half.at[other], held.at[chip], chip_sems.at[0, number], chip_sems.at[1, number],
                "dp", other * 2 + core,
            )
        )
    yield
    for copy in copies:
        copy.wait()
    total = half[chip].astype(F32)
    for step in range(1, 8):
        total = total + held[(chip + step) % 8].astype(F32)
    mine[...] = total[:, :768].astype(BF)
    tile[...] = total[:, 768:]
    small = spread_over_tensor(tile, lambda me: tiles.at[me], tile_sems, 0)
    copies = []
    for number, (dy, dx) in enumerate(chips):
        other = chip_at(dy, dx)
        copies.append(
            send(
                mine, result.at[core, chip, :, pl.ds(0, 768)], chip_sems.at[2, number],
                chip_sems.at[3, number], "dp", other * 2 + core,
            )
        )
    result[core, chip, :, 0:768] = mine[...]
    yield
    for copy in small:
        copy.wait()
    me = lax.axis_index("tensor")
    others = tile[...]
    for step in range(1, NT):
        others = others + tiles[(me + step) % NT]
    lanes = lax.broadcasted_iota(jnp.int32, (GR, 128), 1)
    result[core, chip, :, 768:] = jnp.where(lanes == 33, others, tile[...]).astype(BF)
    for number, (dy, dx) in enumerate(chips):
        other = chip_at(dy, dx)
        place = result.at[core, chip, :, pl.ds(768, 128)]
        copies.append(
            send(
                place, place, chip_sems.at[4, number], chip_sems.at[5, number], "dp",
                other * 2 + core,
            )
        )
    yield
    for copy in copies:
        copy.wait()
    copy = send(
        result.at[core], result.at[core], core_sems.at[0, 1], core_sems.at[1, 1], "dp", partner
    )
    yield
    copy.wait()


SUM_SCRATCH = [
    pltpu.VMEM((8, GR, GP), BF),
    pltpu.VMEM((8, GR, GP), BF),
    pltpu.VMEM((8, GR, GP), BF),
    pltpu.VMEM((GR, D), BF),
    pltpu.VMEM((GR, 128), F32),
    pltpu.VMEM((NT, GR, 128), F32),
    sems(2, 2),
    sems(6, 8),
    sems(2, NT),
]


def gathers(sources, targets, pairs, begin):
    def handle(chosen):
        me = lax.axis_index("tensor")
        for number in chosen:
            for step in range(1, NT):
                copy = pltpu.make_async_remote_copy(
                    src_ref=sources[number],
                    dst_ref=targets[number].at[me],
                    send_sem=pairs.at[2 * number, step],
                    recv_sem=pairs.at[2 * number + 1, step],
                    device_id={"tensor": (me + step) % NT},
                    device_id_type=MESH,
                )
                if begin:
                    copy.start()
                else:
                    copy.wait()

    @pl.when(lax.axis_index("pipe") == 0)
    def _():
        handle((0,))

    @pl.when(lax.axis_index("pipe") == 1)
    def _():
        handle((1, 2))


def layer_part(last, inputs, finals=()):
    def steps(ins, outs, scratch):
        (
            packed, dpicks, delta, x1, meta, gain_two, router, state, gain_one, qkv, ctx, project,
            output,
        ) = ins[:13]
        dqkv, part, dx1_kept, held, near, chosen, pairs, across_sems = scratch[:8]
        live = meta[:, 38:39]
        gate = meta[:, 0:EXPERTS]
        dx2 = delta[...].astype(F32) * live
        total = dpicks[0] + dpicks[1] + dpicks[2] + dpicks[3]
        total = jnp.concatenate([total, jnp.zeros((120, 512), F32)], axis=0)
        columns = jnp.transpose(total)[:NR]
        experts = lax.broadcasted_iota(jnp.int32, (NR, EXPERTS), 1)
        dgate = jnp.zeros((NR, EXPERTS), F32)
        for k in range(2):
            route = meta[:, 36 + k : 37 + k].astype(jnp.int32)
            dgate = dgate + jnp.where(route == experts, columns[:, k : k + 1] * live, 0.0)
        dlogits = gate * (dgate - jnp.sum(gate * dgate, axis=-1, keepdims=True))
        normal, inverse = norm_parts(x1[...])
        high, low = halves(dlogits)
        dz2 = (
            unpack(packed).astype(F32) + dot(high, router[...], 1, 1) + dot(low, router[...], 1, 1)
        )
        dx1 = dx2 + norm_back(dz2, gain_two[...], normal, inverse)
        dx1_kept[...] = dx1.reshape(NT, CH, D)
        dattn = dx1.astype(BF)
        if last:
            yield
            gathers(ins[15:18], outs[2:5], scratch[8], True)
            for source, target in zip(ins[15:18], outs[2:5]):
                target[lax.axis_index("tensor")] = source[...]
        dctx = dot(dattn, output[...], 1, 1).astype(BF)
        scale = HD**-0.5
        projected = qkv[...]
        for image in range(2):
            rows = slice(image * R, (image + 1) * R)
            for head in range(NH):
                queries, keys, values = head_parts(projected, image, head)
                dc = dctx[rows, head * HD : (head + 1) * HD]
                weights = probabilities(queries, keys)
                dweights = dot(dc, values, 1, 1)
                dvalues = dot(weights.astype(BF), dc, 0, 0)
                dscores = weights * (dweights - jnp.sum(weights * dweights, axis=-1, keepdims=True))
                dscores = dscores.astype(BF)
                dqueries = dot(dscores, keys) * scale
                dkeys = dot(dscores, queries, 0, 0) * scale
                for number, value in enumerate((dqueries, dkeys, dvalues)):
                    start = number * GW + head * HD
                    dqkv[rows, start : start + HD] = value.astype(BF)
        own_part = dot(dqkv[...], project[...], 1, 1).astype(BF)
        part[...] = own_part.reshape(NT, CH, D)
        if not last:
            yield
        me = lax.axis_index("tensor")
        stage = lax.axis_index("pipe")
        scattered = [
            [
                send(
                    part.at[(me + step) % NT, pl.ds(start, size)],
                    held.at[me, pl.ds(start, size)],
                    pairs.at[2 * i, step],
                    pairs.at[2 * i + 1, step],
                    "tensor",
                    (me + step) % NT,
                )
                for step in range(1, NT)
            ]
            for i, (start, size) in enumerate(RS_ROWS)
        ]
        normal_one, _ = norm_parts(state[...].astype(F32))
        normed_one = (normal_one * gain_one[...]).astype(BF)
        normed = (normal * gain_two[...]).astype(BF)
        gain_rows = [
            jnp.sum(dz2 * normal, axis=0, keepdims=True),
            jnp.sum(own_part.astype(F32) * normal_one, axis=0, keepdims=True),
        ]
        places = lax.broadcasted_iota(jnp.int32, (128, D), 0)
        tall = jnp.where(places == 32, gain_rows[0], 0.0)
        tall = jnp.where(places == 33, gain_rows[1], tall)
        terms = [
            (0, 576, dot(normed_one, dqkv[...], 0, 0)),
            (576, 768, dot(dattn, ctx[...], 0, 0)),
        ]
        side = jnp.transpose(tall)
        router_term = dot(normed, high, 0, 0) + dot(normed, low, 0, 0)
        side = side + jnp.concatenate([router_term, jnp.zeros((D, 96), F32)], axis=1)
        terms.append((768, GP, side))
        if last:
            one, first = ins[13:15]
            pack = scratch[9]
            for low_end, high_end, term in terms:
                term = jnp.where(stage == 0, term, first[:, low_end:high_end])
                term = term + one[:, low_end:high_end]
                pack[:, :, :, low_end:high_end] = term.astype(BF).reshape(
                    2, 8, GR, high_end - low_end
                )
            summing = sum_dp(pack, outs[1], *scratch[10:])
            next(summing)
            next(summing)
        else:
            for low_end, high_end, term in terms:
                outs[2][:, low_end:high_end] = term
            summing = iter(())
        waiting = []
        result = outs[0]
        chunk = chosen if last else outs[1]
        across = []
        for i, (start, size) in enumerate(RS_ROWS):
            rows = pl.ds(start, size)
            for copy in scattered[i]:
                copy.wait_recv()
            dz1 = part[me, rows].astype(F32)
            for step in range(1, NT):
                dz1 = dz1 + held[(me + step) % NT, rows].astype(F32)
            here = pl.ds(pl.multiple_of(me * CH + start, 16), size)
            normal_here, inverse_here = norm_parts(state[here].astype(F32))
            delta_here = norm_back(dz1, gain_one[...], normal_here, inverse_here)
            chunk[rows] = (dx1_kept[me, rows] + delta_here).astype(BF)
            if not last:
                across.append(
                    send(
                        chunk.at[rows], near.at[rows], across_sems.at[0, i], across_sems.at[1, i],
                        "pipe", 1 - stage,
                    )
                )
        for i, (start, size) in enumerate(RS_ROWS):
            rows = pl.ds(start, size)
            if not last:
                across[i].wait_recv()
                chosen[rows] = jnp.where(stage == 1, chunk[rows], near[rows])
            waiting += spread_over_tensor(
                chosen.at[rows], lambda me: result.at[me, rows], pairs, 4 + 2 * i
            )
        result[me] = chosen[...]
        yield
        for _ in summing:
            yield
        if last:
            gathers(ins[15:18], outs[2:5], scratch[8], False)
        for copy in waiting:
            copy.wait()
        for group in scattered:
            for copy in group:
                copy.wait_send()
        for copy in across:
            copy.wait_send()

    outs = [((NT, CH, D), BF)]
    scratch = [
        pltpu.VMEM((NR, 3 * GW), BF),
        pltpu.VMEM((NT, CH, D), BF),
        pltpu.VMEM((NT, CH, D), F32),
        pltpu.VMEM((NT, CH, D), BF),
        pltpu.VMEM((CH, D), BF),
        pltpu.VMEM((CH, D), BF),
        sems(8, NT),
        sems(2, 2),
    ]
    if last:
        wide = ((NT, R, 2 * Q), BF)
        outs += [((2, 8, GR, GP), BF), ((NT, CH, D), BF), wide, wide]
        scratch += [sems(6, NT), pltpu.VMEM((2, 8, GR, GP), BF)] + SUM_SCRATCH
    else:
        outs += [((CH, D), BF), ((D, GP), F32)]
    return Part(steps, [*inputs, *finals], outs, scratch)


def finish_kernel(stage, *refs):
    states, grads, whole = refs[:4], refs[4:8], refs[8]
    section_out, input_grad, project_grad, output_grad, router_grad, gains = refs[9:]

    def rows(values):
        values = values.astype(F32)
        return jnp.concatenate([values[:IMG_LEN], values[R : R + IMG_LEN]], axis=0).astype(BF)

    def place(base):
        for micro in range(2):
            section_out[micro] = rows(unpack(states[base + micro]))
            input_grad[micro] = rows(grads[base + micro][...])

    @pl.when(stage[0, 0] == 0)
    def _():
        place(0)

    @pl.when(stage[0, 0] != 0)
    def _():
        place(2)

    project_grad[...] = whole[:, :576].astype(F32)
    output_grad[...] = jnp.transpose(whole[:, 576:768].astype(F32))
    side = whole[:, 768:].astype(F32)
    router_grad[...] = side[:, :EXPERTS]
    gains[...] = jnp.transpose(side)[32:40]


def finish(stage, states, grads, whole):
    return pl.pallas_call(
        finish_kernel,
        in_specs=[SMEM] + [VMEM] * 9,
        out_shape=[
            jax.ShapeDtypeStruct((2, 2 * IMG_LEN, D), BF),
            jax.ShapeDtypeStruct((2, 2 * IMG_LEN, D), BF),
            jax.ShapeDtypeStruct((D, 3 * GW), F32),
            jax.ShapeDtypeStruct((GW, D), F32),
            jax.ShapeDtypeStruct((D, EXPERTS), F32),
            jax.ShapeDtypeStruct((8, D), F32),
        ],
        compiler_params=params(),
        name="finish",
    )(stage, *states, *grads, whole)


def pad_rows(values):
    micro, _, width = values.shape
    values = values.reshape(micro, 2, IMG_LEN, width)
    return jnp.pad(values, ((0, 0), (0, 0), (0, R - IMG_LEN), (0, 0))).reshape(micro, NR, width)


def body(
    tokens,
    cotangent,
    image_counts,
    routes,
    attn_norm_gain,
    query_key_value,
    attn_output,
    moe_norm_gain,
    router_weight,
    expert_in,
    expert_down,
):
    gain_one = attn_norm_gain
    gain_two = moe_norm_gain
    project = query_key_value[0].reshape(D, 3 * GW)
    output = attn_output[0]
    router = router_weight[0]
    first, second = expert_in[0], expert_down[0]
    stage = lax.axis_index("pipe")
    early = stage == 0
    counts = image_counts[:, lax.axis_index("dp")].reshape(2, 1, 1)
    plain = pad_rows(tokens)
    upstream = pad_rows(cotangent)
    paths = pad_rows(routes)

    def chosen(one, other):
        return jax.tree.map(lambda a, b: jnp.where(early, a, b), one, other)

    def attend(mode, inputs):
        return attention_part(mode, inputs, gain_one, project, output)

    def layer_inputs(packed, dpicks, delta, saved):
        state, qkv, ctx, x1, meta, arrived, pieces = saved
        return [
            packed, dpicks, delta, x1, meta, gain_two, router, state, gain_one, qkv, ctx, project,
            output,
        ]

    saved = []
    packed_list = []
    states = []
    arriving = None
    for moment in range(2):
        if moment == 0:
            mode, inputs = "plain", (plain[0],)
            count, path = counts[0], paths[0]
        else:
            mode, inputs = "mixed", (plain[1], arriving)
            count, path = chosen((counts[1], paths[1]), (counts[0], paths[0]))
        (results,) = run(
            "attention_" + mode, 1 + moment, ("tensor",), [attend(mode, inputs)]
        )
        summed, qkv, ctx = results[:3]
        state = inputs[0] if mode == "plain" else results[3]
        ((arrived, x1, meta),) = run(
            "dispatch", 3, ("tensor", "dp"),
            [dispatch_part(True, count, state, summed, gain_two, router, path)],
        )
        ((returned,),) = run(
            "experts_forward", 4, ("tensor", "dp"), [experts_forward_part(arrived, first, second)]
        )
        ((packed, pieces, arriving),) = run(
            "combine", 5, ("tensor", "pipe"), [combine_part(True, returned, x1, meta)]
        )
        packed_list.append(packed)
        states.append(arriving)
        saved.append((state, qkv, ctx, x1, meta, arrived, pieces))

    late = saved[1]
    delta = upstream[0]
    (summed, qkv, ctx, state), (delta_arrived,) = run(
        "attention_and_spread", 6, ("tensor", "dp"),
        [attend("packed", (arriving,)), spread_part(False, delta, late[4])],
    )
    (arrived, x1, meta), (returned, hidden, dpre) = run(
        "dispatch_and_experts_backward", 7, ("tensor", "dp"),
        [
            dispatch_part(False, counts[1], state, summed, gain_two, router, paths[1]),
            experts_backward_part(late[5], delta_arrived, first, second),
        ],
    )
    terms = [(late[5], dpre, hidden, delta_arrived)]
    (returned_forward,), (packed, dpicks) = run(
        "experts_forward_and_collect", 8, ("tensor", "dp"),
        [
            experts_forward_part(arrived, first, second),
            collect_part(returned, late[4], late[6], delta),
        ],
    )
    (packed_last, pieces), (grad_state, chunk, grads) = run(
        "combine_and_layer_backward", 9, ("tensor", "pipe"),
        [
            combine_part(False, returned_forward, x1, meta),
            layer_part(False, layer_inputs(packed, dpicks, delta, late)),
        ],
    )
    packed_list.append(packed_last)
    saved.append((state, qkv, ctx, x1, meta, arrived, pieces))
    grad_list = [grads]
    grad_states = [grad_state.reshape(NR, D)]

    for moment in range(1, 3):
        if moment == 1:
            late = chosen(saved[0], saved[2])
            delta = jnp.where(early, grad_states[0], upstream[1])
        else:
            late = saved[1]
            delta = grad_states[1]
        meta, arrived, pieces = late[4:]
        ((delta_arrived,),) = run("spread", 10, ("tensor", "dp"), [spread_part(True, delta, meta)])
        ((returned, hidden, dpre),) = run(
            "experts_backward", 11, ("tensor", "dp"),
            [experts_backward_part(arrived, delta_arrived, first, second)],
        )
        terms.append((arrived, dpre, hidden, delta_arrived))
        ((packed, dpicks),) = run(
            "collect", 12, ("tensor",), [collect_part(returned, meta, pieces, delta)]
        )
        inputs = layer_inputs(packed, dpicks, delta, late)
        if moment == 1:
            ((grad_state, chunk, grads),) = run(
                "layer_backward", 13, ("tensor", "pipe"), [layer_part(False, inputs)]
            )
            grad_list.append(grads)
            grad_states.append(grad_state.reshape(NR, D))
        else:
            finals = [grad_list[1], grad_list[0], chunk, packed_list[1], packed_list[2]]
            ((grad_state, whole, own, wide_one, wide_two),) = run(
                "layer_backward_last", 14, ("tensor", "dp"), [layer_part(True, inputs, finals)]
            )
            grad_states.append(grad_state.reshape(NR, D))

    grad_first, grad_second = expert_grads(
        stage.reshape(1).astype(jnp.int32), terms[1], terms[2], terms[0]
    )
    section_out, input_grad, project_grad, output_grad, router_grad, gains = finish(
        stage.reshape(1, 1).astype(jnp.int32),
        [states[0], states[1], wide_one, wide_two],
        [own.reshape(NR, D), grad_states[2], grad_states[0], grad_states[1]],
        whole.reshape(D, GP),
    )
    return (
        section_out[None],
        input_grad[None],
        gains[1:2],
        project_grad.reshape(1, D, 3, GW),
        output_grad[None],
        gains[0:1],
        router_grad[None],
        grad_first[None],
        grad_second[None],
    )


def solution(mesh):
    placed = (
        P(None, "dp", None),
        P(None, "dp", None),
        P(),
        P(None, "dp", None),
        P("pipe", None),
        P("pipe", None, None, "tensor"),
        P("pipe", "tensor", None),
        P("pipe", None),
        P("pipe", None, None),
        P("pipe", "dp", None, "tensor"),
        P("pipe", "dp", "tensor", None),
    )
    return jax.shard_map(
        body,
        mesh=mesh,
        in_specs=placed,
        out_specs=(
            P("pipe", None, "dp", None),
            P("pipe", None, "dp", None),
            P("pipe", None),
            P("pipe", None, None, "tensor"),
            P("pipe", "tensor", None),
            P("pipe", None),
            P("pipe", None, None),
            P("pipe", "dp", None, "tensor"),
            P("pipe", "dp", "tensor", None),
        ),
        check_vma=False,
    )
```

```python
from types import SimpleNamespace

import jax
import jax.numpy as jnp
from jax import lax
from jax.experimental import pallas as pl
from jax.experimental.pallas import tpu as pltpu
from jax.sharding import PartitionSpec as P

TENSOR, PIPE, DP = "tensor", "pipe", "dp"
BF = jnp.bfloat16
F32 = jnp.float32
MESH = pl.DeviceIdType.MESH
D = 768
HD = 64
NH = 3
GW = NH * HD
IMG_LEN = 197
R = 224
NR = 2 * R
CH = NR // 4
EXPERTS = 32
SL = 32
NT = 4
NDP = 16
Q = D // NT
EPSILON = 1e-06
VMEM_BYTES = 58 * 1024 * 1024
GP = 896


def dot(a, b, ca=1, cb=0):
    return lax.dot_general(a, b, (((ca,), (cb,)), ((), ())), preferred_element_type=F32)


def params(**more):
    return pltpu.CompilerParams(vmem_limit_bytes=VMEM_BYTES, **more)


def norm_parts(values):
    mean = jnp.mean(values, axis=-1, keepdims=True)
    centred = values - mean
    inverse = lax.rsqrt(jnp.mean(centred * centred, axis=-1, keepdims=True) + EPSILON)
    return centred * inverse, inverse


def norm_back(delta, gain, normal, inverse):
    scaled = delta * gain
    return inverse * (
        scaled
        - jnp.mean(scaled, axis=-1, keepdims=True)
        - normal * jnp.mean(scaled * normal, axis=-1, keepdims=True)
    )


def pick(index, options):
    result = options[0]
    for number in range(1, len(options)):
        result = jnp.where(index == number, options[number], result)
    return result


def column_quarter(values, member):
    return pick(member, [values[:, Q * q : Q * (q + 1)] for q in range(NT)])


def unpack(packed):
    images = [
        jnp.concatenate([packed[q][:, Q * i : Q * (i + 1)] for q in range(NT)], axis=1)
        for i in range(2)
    ]
    return jnp.concatenate(images, axis=0)


def head_parts(projected, image, head):
    rows = slice(image * R, (image + 1) * R)
    return [
        projected[rows, part * GW + head * HD : part * GW + (head + 1) * HD] for part in range(3)
    ]


def probabilities(queries, keys):
    scores = dot(queries, keys, 1, 1) * (HD**-0.5)
    held = lax.broadcasted_iota(jnp.int32, scores.shape, 1) < IMG_LEN
    scores = jnp.where(held, scores, -1e30)
    exponent = jnp.exp(scores - jnp.max(scores, axis=-1, keepdims=True))
    return exponent / jnp.sum(exponent, axis=-1, keepdims=True)


VMEM = pl.BlockSpec(memory_space=pltpu.VMEM)
SMEM = pl.BlockSpec(memory_space=pltpu.SMEM)
ANYWHERE = pl.BlockSpec(memory_space=pl.ANY)


def drive(*running):
    running = list(running)
    while running:
        for steps in list(running):
            if next(steps, StopIteration) is StopIteration:
                running.remove(steps)


OUT, SEM, SOURCE = "out ", "sem ", ("/0", "/1")


def prefixed(prefix, items):
    return {prefix + name: item for name, item in items.items()}


class Frame:
    def __init__(self, barrier, count):
        self.barrier = barrier
        self.count = count
        self.met = False
        self.loading = {}
        self.storing = []
        self.refs = {}

    def meet(self):
        if not self.met:
            pl.semaphore_wait(self.barrier, self.count)
            self.met = True

    def __getattr__(self, name):
        if name in self.loading:
            self.loading.pop(name).wait()
        return self.refs[name]

    def group(self, prefix):
        size = len(prefix)
        return SimpleNamespace(
            **{name[size:]: ref for name, ref in self.refs.items() if name[:size] == prefix}
        )

    def flush(self, *refs):
        for ref in refs:
            name = next(name for name, known in self.refs.items() if known is ref)
            copy = pltpu.make_async_copy(ref, self.refs[OUT + name], self.refs[SEM + name])
            copy.start()
            self.storing.append(copy)


def greet(axes):
    barrier = pltpu.get_barrier_semaphore()
    count = 0
    for axis in axes:
        size = lax.axis_size(axis)
        me = lax.axis_index(axis)
        for step in range(1, size):
            pl.semaphore_signal(
                barrier, inc=1, device_id={axis: (me + step) % size}, device_id_type=MESH
            )
        count += size - 1
    return barrier, count


def launch(name, number, axes, plain, lazy, outs, scratch, program):
    arrays, specs, places = [], [], []
    for key, (array, spec) in plain.items():
        arrays.append(array)
        specs.append(spec)
        places.append(key)
    for key, item in lazy.items():
        for position, array in enumerate(item if isinstance(item, tuple) else (item,)):
            arrays.append(array)
            specs.append(ANYWHERE)
            places.append(key + SOURCE[position])
    held = dict(scratch)
    for key, item in lazy.items():
        array = item[0] if isinstance(item, tuple) else item
        held[key] = pltpu.VMEM(array.shape, array.dtype)
        held[SEM + key] = pltpu.SemaphoreType.DMA
    for key, (shape, dtype) in outs.items():
        held[key] = pltpu.VMEM(shape, dtype)
        held[SEM + key] = pltpu.SemaphoreType.DMA

    def kernel(*refs):
        frame = Frame(*greet(axes))
        names = places + [OUT + key for key in outs] + list(held)
        frame.refs = dict(zip(names, refs))
        stage = lax.axis_index(PIPE)
        for key, item in lazy.items():
            target, sem = frame.refs[key], frame.refs[SEM + key]
            copy = pltpu.make_async_copy(frame.refs[key + SOURCE[0]], target, sem)
            if isinstance(item, tuple):
                other = pltpu.make_async_copy(frame.refs[key + SOURCE[1]], target, sem)
                pl.when(stage == 0)(copy.start)
                pl.when(stage != 0)(other.start)
            else:
                copy.start()
            frame.loading[key] = copy
        program(frame)
        for copy in list(frame.loading.values()) + frame.storing:
            copy.wait()

    results = pl.pallas_call(
        kernel,
        in_specs=specs,
        out_specs=[ANYWHERE] * len(outs),
        out_shape=[jax.ShapeDtypeStruct(*out) for out in outs.values()],
        scratch_shapes=list(held.values()),
        compiler_params=params(collective_id=number, has_side_effects=True),
        name=name,
    )(*arrays)
    return SimpleNamespace(**dict(zip(outs, results)))


def send(source, target, send_sem, recv_sem, axis, peer):
    copy = pltpu.make_async_remote_copy(
        src_ref=source,
        dst_ref=target,
        send_sem=send_sem,
        recv_sem=recv_sem,
        device_id={axis: peer},
        device_id_type=MESH,
    )
    copy.start()
    return copy


def sems(*shape):
    return pltpu.SemaphoreType.DMA(shape)


def spread_over_tensor(source, target_of, pairs, row):
    me = lax.axis_index(TENSOR)
    return [
        send(
            source, target_of(me), pairs.at[row, step], pairs.at[row + 1, step], TENSOR,
            (me + step) % NT,
        )
        for step in range(1, NT)
    ]


def padded(values):
    kind = values.dtype
    values = values if kind == jnp.int32 else values.astype(F32)
    blank = jnp.zeros((R - IMG_LEN, values.shape[1]), values.dtype)
    return jnp.concatenate(
        [values[:IMG_LEN], blank, values[IMG_LEN:], blank], axis=0
    ).astype(kind)


def forward_scratch():
    return dict(
        a_part=pltpu.VMEM((NT, CH, D), BF),
        a_held=pltpu.VMEM((NT, CH, D), BF),
        a_mine=pltpu.VMEM((CH, D), BF),
        a_pairs=sems(4, NT),
        d_hot=pltpu.VMEM((NR, EXPERTS * SL), BF),
        d_match=pltpu.VMEM((2, NR, EXPERTS), F32),
    )


FORWARD_OUTS = dict(
    state=((NR, D), BF),
    qkv=((NR, 3 * GW), BF),
    ctx=((NR, GW), BF),
    summed=((NT, CH, D), BF),
    meta=((NR, 128), F32),
    arrived=((NDP, 2 * SL, D), BF),
)


def attention_steps(f, state):
    part, held, mine, pairs = (f.a_part, f.a_held, f.a_mine, f.a_pairs)
    qkv, ctx, summed = f.qkv, f.ctx, f.summed
    f.state[...] = state
    normal, _ = norm_parts(state.astype(F32))
    normed = (normal * f.gain_one[...]).astype(BF)
    projected = dot(normed, f.project[...], 1, 1).astype(BF)
    qkv[...] = projected
    for image in range(2):
        for head in range(NH):
            queries, keys, values = head_parts(projected, image, head)
            weights = probabilities(queries, keys).astype(BF)
            ctx[image * R : (image + 1) * R, head * HD : (head + 1) * HD] = dot(
                weights, values
            ).astype(BF)
    part[...] = dot(ctx[...], f.output[...]).astype(BF).reshape(NT, CH, D)
    f.meet()
    me = lax.axis_index(TENSOR)
    copies = [
        send(
            part.at[(me + step) % NT], held.at[me], pairs.at[0, step], pairs.at[1, step],
            TENSOR, (me + step) % NT,
        )
        for step in range(1, NT)
    ]
    f.flush(f.state, f.qkv, f.ctx)
    yield
    for copy in copies:
        copy.wait()
    total = part[me].astype(F32)
    for step in range(1, NT):
        total = total + held[(me + step) % NT].astype(F32)
    mine[...] = total.astype(BF)
    copies = spread_over_tensor(mine, lambda me: summed.at[me], pairs, 2)
    summed[me] = mine[...]
    yield
    for copy in copies:
        copy.wait()
    f.flush(f.summed)


RELATIVE = [(dy, dx, dc) for dy in (2, 1, 3, 0) for dx in (1, 0) for dc in (0, 1)]
RELATIVE.remove((0, 0, 0))


def peer_at(relative, sign):
    dy, dx, dc = relative
    me = lax.axis_index(DP)
    row = (me // 4 + sign * dy + 4) % 4
    return row * 4 + ((me // 2 + dx) % 2) * 2 + (me + dc) % 2


def quartered(relative):
    return relative[0] != 0 and relative[1] == 1


SHORT = [relative for relative in RELATIVE if quartered(relative)]


def to_experts(outbox, arrived, pairs, relayed, hybrid):
    me = lax.axis_index(DP)
    member = lax.axis_index(TENSOR)
    rows = pl.ds(pl.multiple_of(member * 16, 16), 16)
    direct, relays, order = [], [], []
    for number, relative in enumerate(RELATIVE):
        peer = peer_at(relative, 1)
        short = hybrid and quartered(relative)
        copy = send(
            outbox.at[peer, rows] if short else outbox.at[peer],
            arrived.at[me, rows] if short else arrived.at[me],
            pairs.at[0, number],
            pairs.at[1, number],
            DP,
            peer,
        )
        if short:
            order.append((number, relative, copy))
        else:
            direct.append(copy)
    arrived[me] = outbox[me]
    yield
    order.sort(key=lambda item: item[1][0] == 2)
    for _, relative, copy in order:
        number = SHORT.index(relative)
        copy.wait_recv()
        source = peer_at(relative, -1)
        for step in range(1, NT):
            relays.append(
                send(
                    arrived.at[source, rows],
                    arrived.at[source, rows],
                    relayed.at[0, number, step],
                    relayed.at[1, number, step],
                    TENSOR,
                    (member + step) % NT,
                )
            )
    for _ in range(6):
        yield
    for copy in direct:
        copy.wait()
    for _, _, copy in order:
        copy.wait_send()
    for copy in relays:
        copy.wait()


def to_experts_scratch(hybrid):
    return dict(
        outbox=pltpu.VMEM((NDP, 2 * SL, D), BF),
        pairs=sems(2, NDP),
        relayed=sems(2, len(SHORT), NT) if hybrid else sems(2, 1, 1),
    )


def live_rows(count):
    row = lax.broadcasted_iota(jnp.int32, (NR, 1), 0)
    image = (row >= R).astype(jnp.int32)
    return (image < count) & (row - image * R < IMG_LEN)


def places_steps(f, count, routes):
    meta = f.meta
    live = live_rows(count)
    experts = lax.broadcasted_iota(jnp.int32, (NR, EXPERTS), 1)
    route = [routes[:, k : k + 1] for k in range(2)]
    match = [jnp.where(live & (route[k] == experts), 1.0, 0.0) for k in range(2)]
    above = lax.broadcasted_iota(jnp.int32, (NR, NR), 1) < lax.broadcasted_iota(
        jnp.int32, (NR, NR), 0
    )
    before = dot(jnp.where(above, 1.0, 0.0).astype(BF), (match[0] + match[1]).astype(BF))
    hot = None
    slots = lax.broadcasted_iota(jnp.int32, (NR, EXPERTS * SL), 1)
    for k in range(2):
        slot = jnp.sum(match[k] * before, axis=1, keepdims=True).astype(jnp.int32)
        position = jnp.where(live, route[k] * SL + slot, -1)
        meta[:, 34 + k : 35 + k] = position.astype(F32)
        meta[:, 36 + k : 37 + k] = route[k].astype(F32)
        f.d_match[k] = match[k]
        same = slots == position
        hot = same if hot is None else hot | same
    meta[:, 38:39] = jnp.where(live, 1.0, 0.0)
    f.d_hot[...] = jnp.where(hot, 1.0, 0.0).astype(BF)
    yield


def dispatch_steps(f, hybrid):
    state, summed, meta = f.state, f.summed, f.meta
    outbox, arrived = f.d_outbox, f.arrived
    values = state[...].astype(F32) + summed[...].reshape(NR, D).astype(F32)
    normal, _ = norm_parts(values)
    normed = (normal * f.gain_two[...]).astype(BF)
    outbox[...] = dot(f.d_hot[...], normed, 0, 0).astype(BF).reshape(NDP, 2 * SL, D)
    f.meet()
    sending = to_experts(outbox, arrived, f.d_pairs, f.d_relayed, hybrid)
    next(sending)
    logits = dot(normed, f.router[...], 1, 1)
    exponent = jnp.exp(logits - jnp.max(logits, axis=-1, keepdims=True))
    gate = exponent / jnp.sum(exponent, axis=-1, keepdims=True)
    meta[:, 0:EXPERTS] = gate
    for k in range(2):
        meta[:, 32 + k : 33 + k] = jnp.sum(f.d_match[k] * gate, axis=1, keepdims=True)
    f.flush(f.meta)
    yield
    yield from sending
    f.flush(f.arrived)


def spread_steps(f, hybrid, delta, meta):
    outbox, arrived = f.s_outbox, f.delta_arrived
    values = delta[...].astype(F32) * meta[:, 38:39]
    slots = lax.broadcasted_iota(jnp.int32, (NR, EXPERTS * SL), 1)
    total = None
    for k in range(2):
        position = meta[:, 34 + k : 35 + k].astype(jnp.int32)
        hot = jnp.where(slots == position, 1.0, 0.0).astype(BF)
        scaled = (values * meta[:, 32 + k : 33 + k]).astype(BF)
        term = dot(hot, scaled, 0, 0)
        total = term if total is None else total + term
    outbox[...] = total.astype(BF).reshape(NDP, 2 * SL, D)
    f.meet()
    yield from to_experts(outbox, arrived, f.s_pairs, f.s_relayed, hybrid)
    f.flush(f.delta_arrived)


CUBE = 0.044715
ROOT = 0.7978845608028654


def gelu_parts(pre):
    squared = pre * pre
    inner = jnp.tanh(ROOT * (pre + CUBE * pre * squared))
    return 0.5 * pre * (1.0 + inner), inner, squared


def store_quarters(target, expert, values):
    values = values.astype(BF).reshape(NDP, 2, 16, D)
    for q in range(NT):
        for half in range(2):
            target[q, expert, :, :, half * Q : (half + 1) * Q] = values[
                :, half, :, q * Q : (q + 1) * Q
            ]


def expert_steps(f, key, compute):
    part, held, mine, sums, pairs = (key.part, key.held, key.mine, key.sums, key.pairs)
    store_quarters(part, 0, compute(0))
    f.meet()
    me = lax.axis_index(TENSOR)
    home = lax.axis_index(DP)
    whole = [
        send(
            part.at[(me + step) % NT, 0], held.at[me, 0], sums.at[0, 4, step], sums.at[1, 4, step],
            TENSOR, (me + step) % NT,
        )
        for step in range(1, NT)
    ]
    yield
    store_quarters(part, 1, compute(1))
    group = home // 4
    scattered = []
    for turn in range(4):
        block = ((group + turn + 1) % 4) * 4
        for step in range(1, NT):
            peer = (me + step) % NT
            scattered.append(
                send(
                    part.at[peer, 1, pl.ds(block, 4)],
                    held.at[me, 1, pl.ds(block, 4)],
                    sums.at[0, turn, step],
                    sums.at[1, turn, step],
                    TENSOR,
                    peer,
                )
            )
    yield
    for copy in whole:
        copy.wait()
    total = part[me, 0].astype(F32)
    for step in range(1, NT):
        total = total + held[(me + step) % NT, 0].astype(F32)
    mine[:, 0] = total.astype(BF)
    returned = []
    for turn in range(4):
        block = ((group + turn + 1) % 4) * 4
        for step in range(1, NT):
            scattered[turn * 3 + step - 1].wait_recv()
        total = part[me, 1, pl.ds(block, 4)].astype(F32)
        for step in range(1, NT):
            total = total + held[(me + step) % NT, 1, pl.ds(block, 4)].astype(F32)
        mine[pl.ds(block, 4), 1] = total.astype(BF)
        for number in range(4):
            if turn == 3 and number == 0:
                key.returned[home] = mine[home]
                continue
            offset = (turn + 1) % 4 * 4 + number
            peer = block + (home + number) % 4
            returned.append(
                send(
                    mine.at[peer], key.returned.at[home], pairs.at[0, offset], pairs.at[1, offset], DP,
                    peer,
                )
            )
        yield
    for copy in returned:
        copy.wait()
    for copy in scattered:
        copy.wait_send()


def expert_scratch():
    return dict(
        part=pltpu.VMEM((NT, 2, NDP, 16, 2 * Q), BF),
        held=pltpu.VMEM((NT, 2, NDP, 16, 2 * Q), BF),
        mine=pltpu.VMEM((NDP, 2, 16, 2 * Q), BF),
        sums=sems(2, 5, NT),
        pairs=sems(2, NDP),
        returned=pltpu.VMEM((NDP, 2, 16, 2 * Q), BF),
    )


def expert_rows(ref, expert):
    return ref[:, expert * SL : (expert + 1) * SL].reshape(NDP * SL, D)


def experts_forward_steps(f, arrived):
    def compute(expert):
        hidden = gelu_parts(dot(expert_rows(arrived, expert), f.first[expert]))[0].astype(BF)
        return dot(hidden, f.second[expert])

    yield from expert_steps(f, f.group("f_"), compute)


def experts_backward_steps(f, arrived):
    delta, hidden_out, dpre_out = f.delta_arrived, f.hidden, f.dpre

    def compute(expert):
        place = slice(expert * SL, (expert + 1) * SL)
        pre = dot(expert_rows(arrived, expert), f.first[expert])
        hidden, inner, squared = gelu_parts(pre)
        hidden_out[:, place] = hidden.astype(BF).reshape(NDP, SL, D)
        slope = 0.5 * (1.0 + inner) + (0.5 * ROOT) * pre * (1.0 - inner * inner) * (
            1.0 + 3.0 * CUBE * squared
        )
        dhidden = dot(expert_rows(delta, expert), f.second[expert], 1, 1)
        dpre = (dhidden.astype(BF).astype(F32) * slope).astype(BF)
        dpre_out[:, place] = dpre.reshape(NDP, SL, D)
        result = dot(dpre, f.first[expert], 1, 1)
        if expert == 1:
            f.flush(f.hidden, f.dpre)
        return result

    yield from expert_steps(f, f.group("b_"), compute)


def expert_grads_kernel(stage, *refs):
    grad_first, grad_second = refs[12:]

    def flat(ref):
        return ref[...].reshape(NDP * SL, D)

    def pairs(a, b):
        grad_first[0] = dot(flat(a[0]), flat(a[1]), 0, 0) + dot(flat(b[0]), flat(b[1]), 0, 0)
        grad_second[0] = dot(flat(a[2]), flat(a[3]), 0, 0) + dot(flat(b[2]), flat(b[3]), 0, 0)

    @pl.when(stage[0] == 0)
    def _():
        pairs(refs[0:4], refs[4:8])

    @pl.when(stage[0] != 0)
    def _():
        pairs(refs[0:4], refs[8:12])


def expert_grads(stage, both, first_only, last_only):
    shape = (NDP, SL, D)
    weights = pl.BlockSpec((1, D, D), lambda p, s: (p, 0, 0))
    return pl.pallas_call(
        expert_grads_kernel,
        grid_spec=pltpu.PrefetchScalarGridSpec(
            num_scalar_prefetch=1,
            grid=(2,),
            in_specs=[pl.BlockSpec(shape, lambda p, s: (0, p, 0))] * 4
            + [pl.BlockSpec(shape, lambda p, s: (0, p * (1 - s[0]), 0))] * 4
            + [pl.BlockSpec(shape, lambda p, s: (0, p * s[0], 0))] * 4,
            out_specs=[weights, weights],
        ),
        out_shape=[jax.ShapeDtypeStruct((2, D, D), F32)] * 2,
        compiler_params=params(),
        name="expert_grads",
    )(stage, *both, *first_only, *last_only)


def hot_steps(meta, hots):
    yield
    for k in range(2):
        position = meta[:, 34 + k : 35 + k].astype(jnp.int32)
        place = jnp.where(position >= 0, (position // SL) * 16 + position % 16, -1)
        hot = lax.broadcasted_iota(jnp.int32, (NR, NDP * SL), 1) == place
        hots[k] = jnp.where(hot, 1.0, 0.0).astype(BF)


def gathered(returned, meta, k, hots):
    position = meta[:, 34 + k : 35 + k].astype(jnp.int32)
    odd = (position // 16) % 2 == 1
    both = dot(hots[k], returned)
    return jnp.where(odd, both[:, Q:], both[:, :Q])


HOTS = pltpu.VMEM((2, NR, NDP * SL), BF)
HALVES = (slice(0, CH), slice(CH, R))


def combine_steps(f, onward, meta, hots):
    packed, pieces, returned = f.packed, f.pieces, f.f_returned
    member = lax.axis_index(TENSOR)
    live = meta[:, 38:39]
    total = column_quarter(f.state[...], member).astype(F32) + column_quarter(
        f.summed[...].reshape(NR, D), member
    ).astype(F32)
    rows = returned[...].reshape(NDP * SL, 2 * Q)
    for k in range(2):
        piece = gathered(rows, meta, k, hots)
        pieces[k] = piece.astype(BF)
        total = total + meta[:, 32 + k : 33 + k] * piece
    total = (total * live).astype(BF)
    packed[:, :Q] = total[:R]
    packed[:, Q:] = total[R:]
    f.flush(f.packed)
    if not onward:
        return
    f.flush(f.pieces)
    result = f.onward
    near, chosen, across_sems, pairs = (f.c_near, f.c_chosen, f.c_across, f.c_pairs)
    stage = lax.axis_index(PIPE)
    across = [
        send(
            packed.at[half], near.at[half], across_sems.at[0, i], across_sems.at[1, i], PIPE,
            1 - stage,
        )
        for i, half in enumerate(HALVES)
    ]
    copies = []
    for i, half in enumerate(HALVES):
        across[i].wait_recv()
        chosen[half] = jnp.where(stage == 0, packed[half], near[half])
        copies += spread_over_tensor(
            chosen.at[half], lambda me: result.at[me, half], pairs, 2 * i
        )
    result[member] = chosen[...]
    yield
    for copy in copies:
        copy.wait()
    for copy in across:
        copy.wait_send()
    f.flush(f.onward)


def combine_scratch():
    return dict(
        c_near=pltpu.VMEM((R, 2 * Q), BF),
        c_chosen=pltpu.VMEM((R, 2 * Q), BF),
        c_across=sems(2, 2),
        c_pairs=sems(4, NT),
        h_hot=HOTS,
    )


def collect_steps(f, meta, pieces, delta):
    returned, result, dpicks_all = f.b_returned, f.g_result, f.g_dpicks_all
    packed, dpicks, pairs = f.g_packed, f.g_dpicks, f.g_pairs
    member = lax.axis_index(TENSOR)
    total = None
    rows = returned[...].reshape(NDP * SL, 2 * Q)
    lanes = lax.broadcasted_iota(jnp.int32, (NR, 128), 1)
    columns = jnp.zeros((NR, 128), F32)
    part = column_quarter(delta[...], member).astype(F32) * meta[:, 38:39]
    for k in range(2):
        piece = gathered(rows, meta, k, f.h_hot)
        total = piece if total is None else total + piece
        dots = jnp.sum(pieces(k).astype(F32) * part, axis=1, keepdims=True)
        columns = jnp.where(lanes == k, dots, columns)
    total = total.astype(BF)
    packed[:, :Q] = total[:R]
    packed[:, Q:] = total[R:]
    dpicks[:, :NR] = jnp.transpose(columns)[:8]
    dpicks[:, NR:] = jnp.zeros((8, 512 - NR), F32)
    copies = spread_over_tensor(packed, lambda me: result.at[me], pairs, 0)
    copies += spread_over_tensor(dpicks, lambda me: dpicks_all.at[me], pairs, 2)
    result[member] = packed[...]
    dpicks_all[member] = dpicks[...]
    yield
    for copy in copies:
        copy.wait()


def collect_scratch():
    return dict(
        g_packed=pltpu.VMEM((R, 2 * Q), BF),
        g_dpicks=pltpu.VMEM((8, 512), F32),
        g_pairs=sems(4, NT),
        g_result=pltpu.VMEM((NT, R, 2 * Q), BF),
        g_dpicks_all=pltpu.VMEM((NT, 8, 512), F32),
    )


def halves(values):
    high = values.astype(BF)
    return high, (values - high.astype(F32)).astype(BF)


RS_ROWS = ((0, 64), (64, 48))
GR = D // NDP


def sum_dp(pack, result, near, half, held, mine, tile, tiles, core_sems, chip_sems, tile_sems):
    home = lax.axis_index(DP)
    core = home % 2
    chip = home // 2
    partner = home + 1 - 2 * core
    copy = send(pack.at[1 - core], near, core_sems.at[0, 0], core_sems.at[1, 0], DP, partner)
    yield
    copy.wait()
    half[...] = (pack[core].astype(F32) + near[...].astype(F32)).astype(BF)
    chips = [(dy, dx) for dy in (2, 1, 3, 0) for dx in (1, 0) if (dy, dx) != (0, 0)]

    def chip_at(dy, dx):
        return ((chip // 2 + dy) % 4) * 2 + (chip + dx) % 2

    copies = []
    for number, (dy, dx) in enumerate(chips):
        other = chip_at(dy, dx)
        copies.append(
            send(
                half.at[other], held.at[chip], chip_sems.at[0, number], chip_sems.at[1, number],
                DP, other * 2 + core,
            )
        )
    yield
    for copy in copies:
        copy.wait()
    total = half[chip].astype(F32)
    for step in range(1, 8):
        total = total + held[(chip + step) % 8].astype(F32)
    mine[...] = total[:, :768].astype(BF)
    tile[...] = total[:, 768:]
    small = spread_over_tensor(tile, lambda me: tiles.at[me], tile_sems, 0)
    copies = []
    for number, (dy, dx) in enumerate(chips):
        other = chip_at(dy, dx)
        copies.append(
            send(
                mine, result.at[core, chip, :, pl.ds(0, 768)], chip_sems.at[2, number],
                chip_sems.at[3, number], DP, other * 2 + core,
            )
        )
    result[core, chip, :, 0:768] = mine[...]
    yield
    for copy in small:
        copy.wait()
    me = lax.axis_index(TENSOR)
    others = tile[...]
    for step in range(1, NT):
        others = others + tiles[(me + step) % NT]
    lanes = lax.broadcasted_iota(jnp.int32, (GR, 128), 1)
    result[core, chip, :, 768:] = jnp.where(lanes == 33, others, tile[...]).astype(BF)
    for number, (dy, dx) in enumerate(chips):
        other = chip_at(dy, dx)
        place = result.at[core, chip, :, pl.ds(768, 128)]
        copies.append(
            send(
                place, place, chip_sems.at[4, number], chip_sems.at[5, number], DP,
                other * 2 + core,
            )
        )
    yield
    for copy in copies:
        copy.wait()
    copy = send(
        result.at[core], result.at[core], core_sems.at[0, 1], core_sems.at[1, 1], DP, partner
    )
    yield
    copy.wait()


SUM_SCRATCH = dict(
    t_near=pltpu.VMEM((8, GR, GP), BF),
    t_half=pltpu.VMEM((8, GR, GP), BF),
    t_held=pltpu.VMEM((8, GR, GP), BF),
    t_mine=pltpu.VMEM((GR, D), BF),
    t_tile=pltpu.VMEM((GR, 128), F32),
    t_tiles=pltpu.VMEM((NT, GR, 128), F32),
    t_core=sems(2, 2),
    t_chip=sems(6, 8),
    t_tile_sems=sems(2, NT),
    t_pack=pltpu.VMEM((2, 8, GR, GP), BF),
    t_gathers=sems(6, NT),
)


def gathers(sources, targets, pairs, begin):
    def handle(chosen):
        me = lax.axis_index(TENSOR)
        for number in chosen:
            for step in range(1, NT):
                copy = pltpu.make_async_remote_copy(
                    src_ref=sources[number],
                    dst_ref=targets[number].at[me],
                    send_sem=pairs.at[2 * number, step],
                    recv_sem=pairs.at[2 * number + 1, step],
                    device_id={TENSOR: (me + step) % NT},
                    device_id_type=MESH,
                )
                if begin:
                    copy.start()
                else:
                    copy.wait()

    @pl.when(lax.axis_index(PIPE) == 0)
    def _():
        handle((0,))

    @pl.when(lax.axis_index(PIPE) == 1)
    def _():
        handle((1, 2))


def weights_steps(f):
    yield
    projected = f.qkv_in[...]
    for image in range(2):
        for head in range(NH):
            queries, keys, _ = head_parts(projected, image, head)
            f.l_weights[image * NH + head] = probabilities(queries, keys)


def layer_steps(f, last, meta, delta):
    packed, dpicks, state = f.g_result, f.g_dpicks_all, f.state_in
    dqkv, part, dx1_kept, held, near, chosen, pairs, across_sems = (
        f.l_dqkv, f.l_part, f.l_dx1, f.l_held, f.l_near, f.l_chosen, f.l_pairs, f.l_across
    )
    x1 = state[...].astype(F32) + f.summed_in[...].reshape(NR, D).astype(F32)
    live = meta[:, 38:39]
    gate = meta[:, 0:EXPERTS]
    dx2 = delta[...].astype(F32) * live
    total = dpicks[0] + dpicks[1] + dpicks[2] + dpicks[3]
    total = jnp.concatenate([total, jnp.zeros((120, 512), F32)], axis=0)
    columns = jnp.transpose(total)[:NR]
    experts = lax.broadcasted_iota(jnp.int32, (NR, EXPERTS), 1)
    dgate = jnp.zeros((NR, EXPERTS), F32)
    for k in range(2):
        route = meta[:, 36 + k : 37 + k].astype(jnp.int32)
        dgate = dgate + jnp.where(route == experts, columns[:, k : k + 1] * live, 0.0)
    dlogits = gate * (dgate - jnp.sum(gate * dgate, axis=-1, keepdims=True))
    normal, inverse = norm_parts(x1)
    high, low = halves(dlogits)
    dz2 = (
        unpack(packed).astype(F32) + dot(high, f.router[...]) + dot(low, f.router[...])
    )
    dx1 = dx2 + norm_back(dz2, f.gain_two[...], normal, inverse)
    dx1_kept[...] = dx1.reshape(NT, CH, D)
    dattn = dx1.astype(BF)
    if last:
        sources = [f.own_in, f.wide_one_in, f.wide_two_in]
        targets = [f.own, f.wide_one, f.wide_two]
        gathers(sources, targets, f.t_gathers, True)
        for source, target in zip(sources, targets):
            target[lax.axis_index(TENSOR)] = source[...]
    dctx = dot(dattn, f.output[...], 1, 1).astype(BF)
    scale = HD**-0.5
    projected = f.qkv_in[...]
    for image in range(2):
        rows = slice(image * R, (image + 1) * R)
        for head in range(NH):
            queries, keys, values = head_parts(projected, image, head)
            dc = dctx[rows, head * HD : (head + 1) * HD]
            weights = f.l_weights[image * NH + head]
            dweights = dot(dc, values, 1, 1)
            dvalues = dot(weights.astype(BF), dc, 0, 0)
            dscores = weights * (dweights - jnp.sum(weights * dweights, axis=-1, keepdims=True))
            dscores = dscores.astype(BF)
            dqueries = dot(dscores, keys) * scale
            dkeys = dot(dscores, queries, 0, 0) * scale
            for number, value in enumerate((dqueries, dkeys, dvalues)):
                start = number * GW + head * HD
                dqkv[rows, start : start + HD] = value.astype(BF)
    own_part = dot(dqkv[...], f.project[...]).astype(BF)
    part[...] = own_part.reshape(NT, CH, D)
    me = lax.axis_index(TENSOR)
    stage = lax.axis_index(PIPE)
    scattered = [
        [
            send(
                part.at[(me + step) % NT, pl.ds(start, size)],
                held.at[me, pl.ds(start, size)],
                pairs.at[2 * i, step],
                pairs.at[2 * i + 1, step],
                TENSOR,
                (me + step) % NT,
            )
            for step in range(1, NT)
        ]
        for i, (start, size) in enumerate(RS_ROWS)
    ]
    normal_one, _ = norm_parts(state[...].astype(F32))
    normed_one = (normal_one * f.gain_one[...]).astype(BF)
    normed = (normal * f.gain_two[...]).astype(BF)
    gain_rows = [
        jnp.sum(dz2 * normal, axis=0, keepdims=True),
        jnp.sum(own_part.astype(F32) * normal_one, axis=0, keepdims=True),
    ]
    places = lax.broadcasted_iota(jnp.int32, (128, D), 0)
    tall = jnp.where(places == 32, gain_rows[0], 0.0)
    tall = jnp.where(places == 33, gain_rows[1], tall)
    terms = [
        (0, 576, dot(normed_one, dqkv[...], 0, 0)),
        (576, 768, dot(dattn, f.ctx_in[...], 0, 0)),
    ]
    side = jnp.transpose(tall)
    router_term = dot(normed, high, 0, 0) + dot(normed, low, 0, 0)
    side = side + jnp.concatenate([router_term, jnp.zeros((D, 96), F32)], axis=1)
    terms.append((768, GP, side))
    if last:
        one, first, pack = f.grads_one, f.grads_first, f.t_pack
        for low_end, high_end, term in terms:
            term = jnp.where(stage == 0, term, first[:, low_end:high_end])
            term = term + one[:, low_end:high_end]
            pack[:, :, :, low_end:high_end] = term.astype(BF).reshape(
                2, 8, GR, high_end - low_end
            )
        summing = sum_dp(
            pack,
            f.whole,
            f.t_near, f.t_half, f.t_held, f.t_mine, f.t_tile, f.t_tiles, f.t_core, f.t_chip,
            f.t_tile_sems,
        )
        next(summing)
        next(summing)
    else:
        for low_end, high_end, term in terms:
            f.grads[:, low_end:high_end] = term
        f.flush(f.grads)
        summing = iter(())
    waiting = []
    result = f.result
    chunk = chosen if last else f.chunk
    across = []
    for i, (start, size) in enumerate(RS_ROWS):
        rows = pl.ds(start, size)
        for copy in scattered[i]:
            copy.wait_recv()
        dz1 = part[me, rows].astype(F32)
        for step in range(1, NT):
            dz1 = dz1 + held[(me + step) % NT, rows].astype(F32)
        here = pl.ds(pl.multiple_of(me * CH + start, 16), size)
        normal_here, inverse_here = norm_parts(state[here].astype(F32))
        delta_here = norm_back(dz1, f.gain_one[...], normal_here, inverse_here)
        chunk[rows] = (dx1_kept[me, rows] + delta_here).astype(BF)
        if not last:
            across.append(
                send(
                    chunk.at[rows], near.at[rows], across_sems.at[0, i], across_sems.at[1, i],
                    PIPE, 1 - stage,
                )
            )
    for i, (start, size) in enumerate(RS_ROWS):
        rows = pl.ds(start, size)
        if not last:
            across[i].wait_recv()
            chosen[rows] = jnp.where(stage == 1, chunk[rows], near[rows])
        waiting += spread_over_tensor(
            chosen.at[rows], lambda me: result.at[me, rows], pairs, 4 + 2 * i
        )
    result[me] = chosen[...]
    yield
    for _ in summing:
        yield
    if last:
        gathers(sources, targets, f.t_gathers, False)
        f.flush(f.own, f.wide_one, f.wide_two, f.whole)
    for copy in waiting:
        copy.wait()
    for group in scattered:
        for copy in group:
            copy.wait_send()
    for copy in across:
        copy.wait_send()
    f.flush(f.result)
    if not last:
        f.flush(f.chunk)


LAYER_SCRATCH = dict(
    l_dqkv=pltpu.VMEM((NR, 3 * GW), BF),
    l_part=pltpu.VMEM((NT, CH, D), BF),
    l_dx1=pltpu.VMEM((NT, CH, D), F32),
    l_held=pltpu.VMEM((NT, CH, D), BF),
    l_near=pltpu.VMEM((CH, D), BF),
    l_chosen=pltpu.VMEM((CH, D), BF),
    l_pairs=sems(8, NT),
    l_across=sems(2, 2),
    l_weights=pltpu.VMEM((2 * NH, R, R), F32),
    h_hot=HOTS,
)
ROWS_OUT = ((NDP, 2 * SL, D), BF)
BACKWARD_OUTS = dict(
    delta_arrived=ROWS_OUT,
    hidden=ROWS_OUT,
    dpre=ROWS_OUT,
    result=((NT, CH, D), BF),
)
LINEAR_OUTS = dict(chunk=((CH, D), BF), grads=((D, GP), F32))


def finish_kernel(stage, *refs):
    states, grads, whole = refs[:4], refs[4:8], refs[8]
    section_out, input_grad, project_grad, output_grad, router_grad, gains = refs[9:]

    def rows(values):
        values = values.astype(F32)
        return jnp.concatenate([values[:IMG_LEN], values[R : R + IMG_LEN]], axis=0).astype(BF)

    def place(base):
        for micro in range(2):
            section_out[micro] = rows(unpack(states[base + micro]))
            input_grad[micro] = rows(grads[base + micro][...])

    @pl.when(stage[0, 0] == 0)
    def _():
        place(0)

    @pl.when(stage[0, 0] != 0)
    def _():
        place(2)

    project_grad[...] = jnp.transpose(whole[:, :576].astype(F32))
    output_grad[...] = jnp.transpose(whole[:, 576:768].astype(F32))
    side = whole[:, 768:].astype(F32)
    side = jnp.transpose(side)
    router_grad[...] = side[:EXPERTS]
    gains[...] = side[EXPERTS : EXPERTS + 8]


def finish(stage, states, grads, whole):
    return pl.pallas_call(
        finish_kernel,
        in_specs=[SMEM] + [VMEM] * 9,
        out_shape=[
            jax.ShapeDtypeStruct((2, 2 * IMG_LEN, D), BF),
            jax.ShapeDtypeStruct((2, 2 * IMG_LEN, D), BF),
            jax.ShapeDtypeStruct((3 * GW, D), F32),
            jax.ShapeDtypeStruct((GW, D), F32),
            jax.ShapeDtypeStruct((EXPERTS, D), F32),
            jax.ShapeDtypeStruct((8, D), F32),
        ],
        compiler_params=params(),
        name="finish",
    )(stage, *states, *grads, whole)


def body(
    tokens,
    cotangent,
    image_counts,
    routes,
    attn_norm_gain,
    query_key_value,
    attn_output,
    moe_norm_gain,
    router_weight,
    expert_in,
    expert_down,
):
    project = query_key_value[0].transpose(1, 2, 0).reshape(3 * GW, D)
    stage = lax.axis_index(PIPE)
    all_axes = (TENSOR, DP, PIPE)
    gains = dict(gain_one=(attn_norm_gain, VMEM), gain_two=(moe_norm_gain, VMEM))
    small = dict(project=project, output=attn_output[0], router=router_weight[0].T)
    heavy = dict(first=expert_in[0], second=expert_down[0])
    placing = dict(counts=(image_counts, SMEM), routes=(routes, VMEM))

    def place_of(f, moment):
        home = lax.axis_index(DP)
        one, other = min(moment, 1), max(moment - 1, 0)
        early = lax.axis_index(PIPE) == 0
        count = jnp.where(early, f.counts[one, home], f.counts[other, home])
        path = jnp.where(early, f.routes[one], f.routes[other])
        return count, padded(path)

    def forward(moment, arriving):
        def program(f):
            if moment == 0:
                state = padded(f.tokens[0])
            else:
                early = lax.axis_index(PIPE) == 0
                state = jnp.where(early, padded(f.tokens[1]), unpack(f.arriving))
            drive(attention_steps(f, state), places_steps(f, *place_of(f, moment)))
            drive(dispatch_steps(f, True))
            drive(experts_forward_steps(f, f.arrived), hot_steps(f.meta, f.h_hot))
            drive(combine_steps(f, True, f.meta, f.h_hot))

        outs = dict(FORWARD_OUTS)
        outs["packed"] = ((R, 2 * Q), BF)
        outs["pieces"] = ((2, NR, Q), BF)
        outs["onward"] = ((NT, R, 2 * Q), BF)
        plain = dict(**gains, **placing, tokens=(tokens, VMEM))
        if moment > 0:
            plain["arriving"] = (arriving, VMEM)
        return launch(
            "forward_%d" % moment, 1 + moment, all_axes, plain, dict(**small, **heavy), outs,
            dict(
                **forward_scratch(), **prefixed("d_", to_experts_scratch(True)), **prefixed("f_", expert_scratch()),
                **combine_scratch(),
            ),
            program,
        )

    def kept(saved):
        return dict(
            state_in=saved.state,
            summed_in=saved.summed,
            qkv_in=saved.qkv,
            ctx_in=saved.ctx,
            meta_in=saved.meta,
            arrived_in=saved.arrived,
        )

    def either(one, other):
        return {key: (one[key], other[key]) for key in one}

    backward_scratch = dict(**prefixed("b_", expert_scratch()), **collect_scratch(), **LAYER_SCRATCH)
    zero = forward(0, None)
    one = forward(1, zero.onward)

    def turning(f):
        state = unpack(f.arriving)
        delta = padded(f.delta[0])
        f.delta_kept[...] = delta
        drive(
            spread_steps(f, False, delta, f.meta_in),
            attention_steps(f, state),
            places_steps(f, *place_of(f, 2)),
        )
        drive(
            experts_backward_steps(f, f.arrived_in),
            dispatch_steps(f, False),
            hot_steps(f.meta_in, f.h_hot),
            weights_steps(f),
        )
        drive(
            collect_steps(f, f.meta_in, lambda k: f.pieces_in[k], f.delta_kept)
        )
        drive(layer_steps(f, False, f.meta_in, f.delta_kept))

    two = launch(
        "turning", 3, all_axes,
        dict(**gains, **placing, delta=(cotangent, VMEM), arriving=(one.onward, VMEM)),
        dict(**small, **kept(one), pieces_in=one.pieces, **heavy),
        dict(**FORWARD_OUTS, **BACKWARD_OUTS, **LINEAR_OUTS),
        dict(
            **forward_scratch(), **prefixed("d_", to_experts_scratch(False)),
            **prefixed("s_", to_experts_scratch(False)), **backward_scratch,
            delta_kept=pltpu.VMEM((NR, D), BF),
        ),
        turning,
    )

    def middle(f):
        early = lax.axis_index(PIPE) == 0
        delta = jnp.where(early, f.arriving[...].reshape(NR, D), padded(f.delta[1]))
        f.delta_kept[...] = delta
        drive(
            spread_steps(f, False, delta, f.meta_in),
            experts_forward_steps(f, f.late_arrived),
            hot_steps(f.late_meta, f.k_hot),
        )

        def combining():
            yield
            yield from combine_steps(f, False, f.late_meta, f.k_hot)

        drive(
            experts_backward_steps(f, f.arrived_in),
            combining(),
            hot_steps(f.meta_in, f.h_hot),
            weights_steps(f),
        )
        drive(
            collect_steps(
                f,
                f.meta_in,
                lambda k: jnp.where(early, f.pieces_in[k], f.pieces[k]),
                f.delta_kept,
            )
        )
        drive(layer_steps(f, False, f.meta_in, f.delta_kept))

    three = launch(
        "middle", 4, all_axes,
        dict(**gains, delta=(cotangent, VMEM), arriving=(two.result, VMEM)),
        dict(
            **either(kept(zero), kept(two)), **heavy, late_arrived=two.arrived,
            late_meta=two.meta, state=two.state, summed=two.summed,
            pieces_in=zero.pieces, **small,
        ),
        dict(**BACKWARD_OUTS, **LINEAR_OUTS, packed=((R, 2 * Q), BF)),
        dict(
            **prefixed("s_", to_experts_scratch(False)), **prefixed("f_", expert_scratch()), **backward_scratch,
            pieces=pltpu.VMEM((2, NR, Q), BF), k_hot=HOTS, delta_kept=pltpu.VMEM((NR, D), BF),
        ),
        middle,
    )

    def ending(f):
        delta = f.arriving[...].reshape(NR, D)
        f.delta_kept[...] = delta
        drive(spread_steps(f, True, delta, f.meta_in))
        drive(
            experts_backward_steps(f, f.arrived_in),
            hot_steps(f.meta_in, f.h_hot),
            weights_steps(f),
        )
        drive(
            collect_steps(f, f.meta_in, lambda k: f.pieces_in[k], f.delta_kept)
        )
        drive(layer_steps(f, True, f.meta_in, f.delta_kept))

    wide = ((NT, R, 2 * Q), BF)
    four = launch(
        "ending", 5, (TENSOR, DP),
        dict(**gains, arriving=(three.result, VMEM)),
        dict(
            **kept(one), **heavy, pieces_in=one.pieces, **small,
            own_in=three.chunk, wide_one_in=one.packed,
            wide_two_in=three.packed, grads_one=three.grads,
            grads_first=two.grads,
        ),
        dict(
            **BACKWARD_OUTS, whole=((2, 8, GR, GP), BF), own=((NT, CH, D), BF),
            wide_one=wide, wide_two=wide,
        ),
        dict(
            **prefixed("s_", to_experts_scratch(True)), **backward_scratch, **SUM_SCRATCH,
            delta_kept=pltpu.VMEM((NR, D), BF),
        ),
        ending,
    )

    def outer(saved, results):
        return (saved.arrived, results.dpre, results.hidden, results.delta_arrived)

    early = stage == 0
    middle_arrived = jnp.where(early, zero.arrived, two.arrived)
    grad_first, grad_second = expert_grads(
        stage.reshape(1).astype(jnp.int32),
        outer(SimpleNamespace(arrived=middle_arrived), three),
        outer(one, four),
        outer(one, two),
    )
    section_out, input_grad, project_grad, output_grad, router_grad, gain_grads = finish(
        stage.reshape(1, 1).astype(jnp.int32),
        [zero.onward, one.onward, four.wide_one, four.wide_two],
        [
            array.reshape(NR, D)
            for array in (four.own, four.result, two.result, three.result)
        ],
        four.whole.reshape(D, GP),
    )
    return (
        section_out[None],
        input_grad[None],
        gain_grads[1:2],
        project_grad.reshape(1, 3, GW, D).transpose(0, 3, 1, 2),
        output_grad[None],
        gain_grads[0:1],
        router_grad.T[None],
        grad_first[None],
        grad_second[None],
    )


def solution(mesh):
    placed = (
        P(None, DP, None),
        P(None, DP, None),
        P(),
        P(None, DP, None),
        P(PIPE, None),
        P(PIPE, None, None, TENSOR),
        P(PIPE, TENSOR, None),
        P(PIPE, None),
        P(PIPE, None, None),
        P(PIPE, DP, None, TENSOR),
        P(PIPE, DP, TENSOR, None),
    )
    return jax.shard_map(
        body,
        mesh=mesh,
        in_specs=placed,
        out_specs=(
            P(PIPE, None, DP, None),
            P(PIPE, None, DP, None),
            P(PIPE, None),
            P(PIPE, None, None, TENSOR),
            P(PIPE, TENSOR, None),
            P(PIPE, None),
            P(PIPE, None, None),
            P(PIPE, DP, None, TENSOR),
            P(PIPE, DP, TENSOR, None),
        ),
        check_vma=False,
    )
```

```python
from types import SimpleNamespace

import jax
import jax.numpy as jnp
from jax import lax
from jax.experimental import pallas as pl
from jax.experimental.pallas import tpu as pltpu
from jax.sharding import PartitionSpec as P

TENSOR, PIPE, DP = "tensor", "pipe", "dp"
BF = jnp.bfloat16
F32 = jnp.float32
MESH = pl.DeviceIdType.MESH
D = 768
HD = 64
NH = 3
GW = NH * HD
IMG_LEN = 197
R = 224
NR = 2 * R
CH = NR // 4
EXPERTS = 32
SL = 32
NT = 4
NDP = 16
Q = D // NT
EPSILON = 1e-06
VMEM_BYTES = 58 * 1024 * 1024
GP = 896


def dot(a, b, ca=1, cb=0):
    return lax.dot_general(a, b, (((ca,), (cb,)), ((), ())), preferred_element_type=F32)


def params(**more):
    return pltpu.CompilerParams(vmem_limit_bytes=VMEM_BYTES, **more)


def norm_parts(values):
    mean = jnp.mean(values, axis=-1, keepdims=True)
    centred = values - mean
    inverse = lax.rsqrt(jnp.mean(centred * centred, axis=-1, keepdims=True) + EPSILON)
    return centred * inverse, inverse


def norm_back(delta, gain, normal, inverse):
    scaled = delta * gain
    return inverse * (
        scaled
        - jnp.mean(scaled, axis=-1, keepdims=True)
        - normal * jnp.mean(scaled * normal, axis=-1, keepdims=True)
    )


def pick(index, options):
    result = options[0]
    for number in range(1, len(options)):
        result = jnp.where(index == number, options[number], result)
    return result


def column_quarter(values, member):
    return pick(member, [values[:, Q * q : Q * (q + 1)] for q in range(NT)])


def unpack(packed):
    images = [
        jnp.concatenate([packed[q][:, Q * i : Q * (i + 1)] for q in range(NT)], axis=1)
        for i in range(2)
    ]
    return jnp.concatenate(images, axis=0)


def head_parts(projected, image, head):
    rows = slice(image * R, (image + 1) * R)
    return [
        projected[rows, part * GW + head * HD : part * GW + (head + 1) * HD] for part in range(3)
    ]


def probabilities(queries, keys):
    scores = dot(queries, keys, 1, 1) * (HD**-0.5)
    held = lax.broadcasted_iota(jnp.int32, scores.shape, 1) < IMG_LEN
    scores = jnp.where(held, scores, -1e30)
    exponent = jnp.exp(scores - jnp.max(scores, axis=-1, keepdims=True))
    return exponent / jnp.sum(exponent, axis=-1, keepdims=True)


VMEM = pl.BlockSpec(memory_space=pltpu.VMEM)
SMEM = pl.BlockSpec(memory_space=pltpu.SMEM)
ANYWHERE = pl.BlockSpec(memory_space=pl.ANY)


def drive(*running):
    running = list(running)
    while running:
        for steps in list(running):
            if next(steps, StopIteration) is StopIteration:
                running.remove(steps)


OUT, SEM, SOURCE = "out ", "sem ", ("/0", "/1")


def prefixed(prefix, items):
    return {prefix + name: item for name, item in items.items()}


def chain(*makers):
    for maker in makers:
        yield from maker()


class Frame:
    def __init__(self, barrier, count):
        self.barrier = barrier
        self.count = count
        self.met = False
        self.loading = {}
        self.storing = []
        self.refs = {}

    def meet(self):
        if not self.met:
            pl.semaphore_wait(self.barrier, self.count)
            self.met = True

    def __getattr__(self, name):
        if name in self.loading:
            self.loading.pop(name).wait()
        return self.refs[name]

    def group(self, prefix):
        size = len(prefix)
        return SimpleNamespace(
            **{name[size:]: ref for name, ref in self.refs.items() if name[:size] == prefix}
        )

    def flush(self, *refs):
        for ref in refs:
            name = next(name for name, known in self.refs.items() if known is ref)
            copy = pltpu.make_async_copy(ref, self.refs[OUT + name], self.refs[SEM + name])
            copy.start()
            self.storing.append(copy)


def greet(axes):
    barrier = pltpu.get_barrier_semaphore()
    count = 0
    for axis in axes:
        size = lax.axis_size(axis)
        me = lax.axis_index(axis)
        for step in range(1, size):
            pl.semaphore_signal(
                barrier, inc=1, device_id={axis: (me + step) % size}, device_id_type=MESH
            )
        count += size - 1
    return barrier, count


def launch(name, number, axes, plain, lazy, outs, scratch, program):
    arrays, specs, places = [], [], []
    for key, (array, spec) in plain.items():
        arrays.append(array)
        specs.append(spec)
        places.append(key)
    for key, item in lazy.items():
        for position, array in enumerate(item if isinstance(item, tuple) else (item,)):
            arrays.append(array)
            specs.append(ANYWHERE)
            places.append(key + SOURCE[position])
    held = dict(scratch)
    for key, item in lazy.items():
        array = item[0] if isinstance(item, tuple) else item
        held[key] = pltpu.VMEM(array.shape, array.dtype)
        held[SEM + key] = pltpu.SemaphoreType.DMA
    for key, (shape, dtype) in outs.items():
        held[key] = pltpu.VMEM(shape, dtype)
        held[SEM + key] = pltpu.SemaphoreType.DMA

    def kernel(*refs):
        frame = Frame(*greet(axes))
        names = places + [OUT + key for key in outs] + list(held)
        frame.refs = dict(zip(names, refs))
        stage = lax.axis_index(PIPE)
        for key, item in lazy.items():
            target, sem = frame.refs[key], frame.refs[SEM + key]
            copy = pltpu.make_async_copy(frame.refs[key + SOURCE[0]], target, sem)
            if isinstance(item, tuple):
                other = pltpu.make_async_copy(frame.refs[key + SOURCE[1]], target, sem)
                pl.when(stage == 0)(copy.start)
                pl.when(stage != 0)(other.start)
            else:
                copy.start()
            frame.loading[key] = copy
        program(frame)
        for copy in list(frame.loading.values()) + frame.storing:
            copy.wait()

    results = pl.pallas_call(
        kernel,
        in_specs=specs,
        out_specs=[ANYWHERE] * len(outs),
        out_shape=[jax.ShapeDtypeStruct(*out) for out in outs.values()],
        scratch_shapes=list(held.values()),
        compiler_params=params(collective_id=number, has_side_effects=True),
        name=name,
    )(*arrays)
    return SimpleNamespace(**dict(zip(outs, results)))


def send(source, target, send_sem, recv_sem, axis, peer):
    copy = pltpu.make_async_remote_copy(
        src_ref=source,
        dst_ref=target,
        send_sem=send_sem,
        recv_sem=recv_sem,
        device_id={axis: peer},
        device_id_type=MESH,
    )
    copy.start()
    return copy


def sems(*shape):
    return pltpu.SemaphoreType.DMA(shape)


def spread_over_tensor(source, target_of, pairs, row):
    me = lax.axis_index(TENSOR)
    return [
        send(
            source, target_of(me), pairs.at[row, step], pairs.at[row + 1, step], TENSOR,
            (me + step) % NT,
        )
        for step in range(1, NT)
    ]


def padded(values):
    kind = values.dtype
    values = values if kind == jnp.int32 else values.astype(F32)
    blank = jnp.zeros((R - IMG_LEN, values.shape[1]), values.dtype)
    return jnp.concatenate(
        [values[:IMG_LEN], blank, values[IMG_LEN:], blank], axis=0
    ).astype(kind)


def forward_scratch():
    return dict(
        a_part=pltpu.VMEM((NT, CH, D), BF),
        a_held=pltpu.VMEM((NT, CH, D), BF),
        a_mine=pltpu.VMEM((CH, D), BF),
        a_pairs=sems(8, NT),
        d_hot=pltpu.VMEM((NR, EXPERTS * SL), BF),
        d_match=pltpu.VMEM((2, NR, EXPERTS), F32),
    )


FORWARD_OUTS = dict(
    state=((NR, D), BF),
    qkv=((NR, 3 * GW), BF),
    ctx=((NR, GW), BF),
    summed=((NT, CH, D), BF),
    meta=((NR, 128), F32),
    arrived=((NDP, 2 * SL, D), BF),
)


def attention_steps(f, state):
    part, held, mine, pairs = (f.a_part, f.a_held, f.a_mine, f.a_pairs)
    qkv, ctx, summed = f.qkv, f.ctx, f.summed
    f.state[...] = state
    normal, _ = norm_parts(state.astype(F32))
    normed = (normal * f.gain_one[...]).astype(BF)
    projected = dot(normed, f.project[...], 1, 1).astype(BF)
    qkv[...] = projected
    for image in range(2):
        for head in range(NH):
            queries, keys, values = head_parts(projected, image, head)
            weights = probabilities(queries, keys).astype(BF)
            ctx[image * R : (image + 1) * R, head * HD : (head + 1) * HD] = dot(
                weights, values
            ).astype(BF)
    part[...] = dot(ctx[...], f.output[...]).astype(BF).reshape(NT, CH, D)
    f.meet()
    me = lax.axis_index(TENSOR)
    scattered = [
        [
            send(
                part.at[(me + step) % NT, pl.ds(start, size)], held.at[me, pl.ds(start, size)],
                pairs.at[4 * i, step], pairs.at[4 * i + 1, step], TENSOR, (me + step) % NT,
            )
            for step in range(1, NT)
        ]
        for i, (start, size) in enumerate(RS_ROWS)
    ]
    f.flush(f.state, f.qkv, f.ctx)
    yield
    copies = []
    for i, (start, size) in enumerate(RS_ROWS):
        rows = pl.ds(start, size)
        for copy in scattered[i]:
            copy.wait()
        total = part[me, rows].astype(F32)
        for step in range(1, NT):
            total = total + held[(me + step) % NT, rows].astype(F32)
        mine[rows] = total.astype(BF)
        copies += spread_over_tensor(
            mine.at[rows], lambda me: summed.at[me, rows], pairs, 4 * i + 2
        )
    summed[me] = mine[...]
    yield
    for copy in copies:
        copy.wait()
    f.flush(f.summed)


RELATIVE = [(dy, dx, dc) for dy in (2, 1, 3, 0) for dx in (1, 0) for dc in (0, 1)]
RELATIVE.remove((0, 0, 0))


def peer_at(relative, sign):
    dy, dx, dc = relative
    me = lax.axis_index(DP)
    row = (me // 4 + sign * dy + 4) % 4
    return row * 4 + ((me // 2 + dx) % 2) * 2 + (me + dc) % 2


def quartered(relative):
    return relative[0] != 0 and relative[1] == 1


SHORT = [relative for relative in RELATIVE if quartered(relative)]


def to_experts(outbox, arrived, pairs, relayed, hybrid):
    me = lax.axis_index(DP)
    member = lax.axis_index(TENSOR)
    rows = pl.ds(pl.multiple_of(member * 16, 16), 16)
    direct, relays, order = [], [], []
    for number, relative in enumerate(RELATIVE):
        peer = peer_at(relative, 1)
        short = hybrid and quartered(relative)
        copy = send(
            outbox.at[peer, rows] if short else outbox.at[peer],
            arrived.at[me, rows] if short else arrived.at[me],
            pairs.at[0, number],
            pairs.at[1, number],
            DP,
            peer,
        )
        if short:
            order.append((number, relative, copy))
        else:
            direct.append(copy)
    arrived[me] = outbox[me]
    yield
    order.sort(key=lambda item: item[1][0] == 2)
    for _, relative, copy in order:
        number = SHORT.index(relative)
        copy.wait_recv()
        source = peer_at(relative, -1)
        for step in range(1, NT):
            relays.append(
                send(
                    arrived.at[source, rows],
                    arrived.at[source, rows],
                    relayed.at[0, number, step],
                    relayed.at[1, number, step],
                    TENSOR,
                    (member + step) % NT,
                )
            )
    for _ in range(6):
        yield
    for copy in direct:
        copy.wait()
    for _, _, copy in order:
        copy.wait_send()
    for copy in relays:
        copy.wait()


def to_experts_scratch(hybrid):
    return dict(
        outbox=pltpu.VMEM((NDP, 2 * SL, D), BF),
        pairs=sems(2, NDP),
        relayed=sems(2, len(SHORT), NT) if hybrid else sems(2, 1, 1),
    )


def live_rows(count):
    row = lax.broadcasted_iota(jnp.int32, (NR, 1), 0)
    image = (row >= R).astype(jnp.int32)
    return (image < count) & (row - image * R < IMG_LEN)


def places_steps(f, count, routes):
    meta = f.meta
    live = live_rows(count)
    experts = lax.broadcasted_iota(jnp.int32, (NR, EXPERTS), 1)
    route = [routes[:, k : k + 1] for k in range(2)]
    match = [jnp.where(live & (route[k] == experts), 1.0, 0.0) for k in range(2)]
    above = lax.broadcasted_iota(jnp.int32, (NR, NR), 1) < lax.broadcasted_iota(
        jnp.int32, (NR, NR), 0
    )
    before = dot(jnp.where(above, 1.0, 0.0).astype(BF), (match[0] + match[1]).astype(BF))
    hot = None
    slots = lax.broadcasted_iota(jnp.int32, (NR, EXPERTS * SL), 1)
    for k in range(2):
        slot = jnp.sum(match[k] * before, axis=1, keepdims=True).astype(jnp.int32)
        position = jnp.where(live, route[k] * SL + slot, -1)
        meta[:, 34 + k : 35 + k] = position.astype(F32)
        meta[:, 36 + k : 37 + k] = route[k].astype(F32)
        f.d_match[k] = match[k]
        same = slots == position
        hot = same if hot is None else hot | same
    meta[:, 38:39] = jnp.where(live, 1.0, 0.0)
    f.d_hot[...] = jnp.where(hot, 1.0, 0.0).astype(BF)
    yield


def dispatch_steps(f, hybrid):
    state, summed, meta = f.state, f.summed, f.meta
    outbox, arrived = f.d_outbox, f.arrived
    values = state[...].astype(F32) + summed[...].reshape(NR, D).astype(F32)
    normal, _ = norm_parts(values)
    normed = (normal * f.gain_two[...]).astype(BF)
    outbox[...] = dot(f.d_hot[...], normed, 0, 0).astype(BF).reshape(NDP, 2 * SL, D)
    f.meet()
    sending = to_experts(outbox, arrived, f.d_pairs, f.d_relayed, hybrid)
    next(sending)
    logits = dot(normed, f.router[...], 1, 1)
    exponent = jnp.exp(logits - jnp.max(logits, axis=-1, keepdims=True))
    gate = exponent / jnp.sum(exponent, axis=-1, keepdims=True)
    meta[:, 0:EXPERTS] = gate
    for k in range(2):
        meta[:, 32 + k : 33 + k] = jnp.sum(f.d_match[k] * gate, axis=1, keepdims=True)
    f.flush(f.meta)
    yield
    yield from sending
    f.flush(f.arrived)


def spread_steps(f, hybrid, delta, meta):
    outbox, arrived = f.s_outbox, f.delta_arrived
    values = delta[...].astype(F32) * meta[:, 38:39]
    slots = lax.broadcasted_iota(jnp.int32, (NR, EXPERTS * SL), 1)
    total = None
    for k in range(2):
        position = meta[:, 34 + k : 35 + k].astype(jnp.int32)
        hot = jnp.where(slots == position, 1.0, 0.0).astype(BF)
        scaled = (values * meta[:, 32 + k : 33 + k]).astype(BF)
        term = dot(hot, scaled, 0, 0)
        total = term if total is None else total + term
    outbox[...] = total.astype(BF).reshape(NDP, 2 * SL, D)
    f.meet()
    yield from to_experts(outbox, arrived, f.s_pairs, f.s_relayed, hybrid)
    f.flush(f.delta_arrived)


CUBE = 0.044715
ROOT = 0.7978845608028654


def gelu_parts(pre):
    squared = pre * pre
    inner = jnp.tanh(ROOT * (pre + CUBE * pre * squared))
    return 0.5 * pre * (1.0 + inner), inner, squared


def store_quarters(target, expert, values):
    values = values.astype(BF).reshape(NDP, 2, 16, D)
    for q in range(NT):
        for half in range(2):
            target[q, expert, :, :, half * Q : (half + 1) * Q] = values[
                :, half, :, q * Q : (q + 1) * Q
            ]


def expert_steps(f, key, compute):
    part, held, mine, passing, pairs = (key.part, key.held, key.mine, key.passing, key.pairs)
    me = lax.axis_index(TENSOR)
    home = lax.axis_index(DP)
    group = home // 4
    near = ((me + 1) % NT, (me + 3) % NT)
    far = (me + 2) % NT
    half = (pl.ds(0, 8), pl.ds(8, 8))

    def begin(expert):
        return [
            send(
                part.at[far, expert, half[way]], passing.at[way, expert],
                key.pass_sems.at[0, way, expert], key.pass_sems.at[1, way, expert],
                TENSOR, near[way],
            )
            for way in range(2)
        ]

    def add_passing(expert, copies):
        for way in range(2):
            copies[way].wait()
            rows = (near[way], expert, half[way])
            part[rows] = (part[rows].astype(F32) + passing[way, expert].astype(F32)).astype(BF)

    store_quarters(part, 0, compute(0))
    f.meet()
    one = begin(0)
    yield
    store_quarters(part, 1, compute(1))
    two = begin(1)
    add_passing(0, one)
    whole = [
        send(
            part.at[near[way], 0], held.at[way, 0], key.sums.at[0, 4, way],
            key.sums.at[1, 4, way], TENSOR, near[way],
        )
        for way in range(2)
    ]
    yield
    add_passing(1, two)
    scattered = []
    for turn in range(4):
        block = ((group + turn + 1) % 4) * 4
        for way in range(2):
            scattered.append(
                send(
                    part.at[near[way], 1, pl.ds(block, 4)],
                    held.at[way, 1, pl.ds(block, 4)],
                    key.sums.at[0, turn, way],
                    key.sums.at[1, turn, way],
                    TENSOR,
                    near[way],
                )
            )
    yield
    for copy in whole:
        copy.wait()
    total = part[me, 0].astype(F32) + held[0, 0].astype(F32) + held[1, 0].astype(F32)
    mine[:, 0] = total.astype(BF)
    returned = []
    for turn in range(4):
        block = ((group + turn + 1) % 4) * 4
        for way in range(2):
            scattered[turn * 2 + way].wait_recv()
        rows = pl.ds(block, 4)
        total = part[me, 1, rows].astype(F32)
        for way in range(2):
            total = total + held[way, 1, rows].astype(F32)
        mine[rows, 1] = total.astype(BF)
        for number in range(4):
            if turn == 3 and number == 0:
                key.returned[home] = mine[home]
                continue
            offset = (turn + 1) % 4 * 4 + number
            peer = block + (home + number) % 4
            returned.append(
                send(
                    mine.at[peer], key.returned.at[home], pairs.at[0, offset],
                    pairs.at[1, offset], DP, peer,
                )
            )
        yield
    for copy in returned:
        copy.wait()
    for copy in scattered:
        copy.wait_send()


def expert_scratch():
    return dict(
        part=pltpu.VMEM((NT, 2, NDP, 16, 2 * Q), BF),
        held=pltpu.VMEM((2, 2, NDP, 16, 2 * Q), BF),
        passing=pltpu.VMEM((2, 2, 8, 16, 2 * Q), BF),
        pass_sems=sems(2, 2, 2),
        mine=pltpu.VMEM((NDP, 2, 16, 2 * Q), BF),
        sums=sems(2, 5, 2),
        pairs=sems(2, NDP),
        returned=pltpu.VMEM((NDP, 2, 16, 2 * Q), BF),
    )


def expert_rows(ref, expert):
    return ref[:, expert * SL : (expert + 1) * SL].reshape(NDP * SL, D)


def experts_forward_steps(f, arrived):
    def compute(expert):
        hidden = gelu_parts(dot(expert_rows(arrived, expert), f.first[expert]))[0].astype(BF)
        return dot(hidden, f.second[expert])

    yield from expert_steps(f, f.group("f_"), compute)


def experts_backward_steps(f, arrived):
    delta, hidden_out, dpre_out = f.delta_arrived, f.hidden, f.dpre

    def compute(expert):
        place = slice(expert * SL, (expert + 1) * SL)
        pre = dot(expert_rows(arrived, expert), f.first[expert])
        hidden, inner, squared = gelu_parts(pre)
        hidden_out[:, place] = hidden.astype(BF).reshape(NDP, SL, D)
        slope = 0.5 * (1.0 + inner) + (0.5 * ROOT) * pre * (1.0 - inner * inner) * (
            1.0 + 3.0 * CUBE * squared
        )
        dhidden = dot(expert_rows(delta, expert), f.second[expert], 1, 1)
        dpre = (dhidden.astype(BF).astype(F32) * slope).astype(BF)
        dpre_out[:, place] = dpre.reshape(NDP, SL, D)
        result = dot(dpre, f.first[expert], 1, 1)
        if expert == 1:
            f.flush(f.hidden, f.dpre)
        return result

    yield from expert_steps(f, f.group("b_"), compute)


def expert_grads_kernel(stage, *refs):
    grad_first, grad_second = refs[12:]

    def flat(ref):
        return ref[...].reshape(NDP * SL, D)

    def pairs(a, b):
        grad_first[0] = dot(flat(a[0]), flat(a[1]), 0, 0) + dot(flat(b[0]), flat(b[1]), 0, 0)
        grad_second[0] = dot(flat(a[2]), flat(a[3]), 0, 0) + dot(flat(b[2]), flat(b[3]), 0, 0)

    @pl.when(stage[0] == 0)
    def _():
        pairs(refs[0:4], refs[4:8])

    @pl.when(stage[0] != 0)
    def _():
        pairs(refs[0:4], refs[8:12])


def expert_grads(stage, both, first_only, last_only):
    shape = (NDP, SL, D)
    weights = pl.BlockSpec((1, D, D), lambda p, s: (p, 0, 0))
    return pl.pallas_call(
        expert_grads_kernel,
        grid_spec=pltpu.PrefetchScalarGridSpec(
            num_scalar_prefetch=1,
            grid=(2,),
            in_specs=[pl.BlockSpec(shape, lambda p, s: (0, p, 0))] * 4
            + [pl.BlockSpec(shape, lambda p, s: (0, p * (1 - s[0]), 0))] * 4
            + [pl.BlockSpec(shape, lambda p, s: (0, p * s[0], 0))] * 4,
            out_specs=[weights, weights],
        ),
        out_shape=[jax.ShapeDtypeStruct((2, D, D), F32)] * 2,
        compiler_params=params(),
        name="expert_grads",
    )(stage, *both, *first_only, *last_only)


def hot_steps(meta, hots):
    yield
    for k in range(2):
        position = meta[:, 34 + k : 35 + k].astype(jnp.int32)
        place = jnp.where(position >= 0, (position // SL) * 16 + position % 16, -1)
        hot = lax.broadcasted_iota(jnp.int32, (NR, NDP * SL), 1) == place
        hots[k] = jnp.where(hot, 1.0, 0.0).astype(BF)


def gathered(returned, meta, k, hots):
    position = meta[:, 34 + k : 35 + k].astype(jnp.int32)
    odd = (position // 16) % 2 == 1
    both = dot(hots[k], returned)
    return jnp.where(odd, both[:, Q:], both[:, :Q])


HOTS = pltpu.VMEM((2, NR, NDP * SL), BF)
HALVES = (slice(0, CH), slice(CH, R))


def combine_steps(f, onward, meta, hots):
    packed, pieces, returned = f.packed, f.pieces, f.f_returned
    member = lax.axis_index(TENSOR)
    live = meta[:, 38:39]
    total = column_quarter(f.state[...], member).astype(F32) + column_quarter(
        f.summed[...].reshape(NR, D), member
    ).astype(F32)
    rows = returned[...].reshape(NDP * SL, 2 * Q)
    for k in range(2):
        piece = gathered(rows, meta, k, hots)
        pieces[k] = piece.astype(BF)
        total = total + meta[:, 32 + k : 33 + k] * piece
    total = (total * live).astype(BF)
    packed[:, :Q] = total[:R]
    packed[:, Q:] = total[R:]
    f.flush(f.packed)
    if not onward:
        return
    f.flush(f.pieces)
    result = f.onward
    near, chosen, across_sems, pairs = (f.c_near, f.c_chosen, f.c_across, f.c_pairs)
    stage = lax.axis_index(PIPE)
    across = [
        send(
            packed.at[half], near.at[half], across_sems.at[0, i], across_sems.at[1, i], PIPE,
            1 - stage,
        )
        for i, half in enumerate(HALVES)
    ]
    copies = []
    for i, half in enumerate(HALVES):
        across[i].wait_recv()
        chosen[half] = jnp.where(stage == 0, packed[half], near[half])
        copies += spread_over_tensor(
            chosen.at[half], lambda me: result.at[me, half], pairs, 2 * i
        )
    result[member] = chosen[...]
    yield
    for copy in copies:
        copy.wait()
    for copy in across:
        copy.wait_send()
    f.flush(f.onward)


def combine_scratch():
    return dict(
        c_near=pltpu.VMEM((R, 2 * Q), BF),
        c_chosen=pltpu.VMEM((R, 2 * Q), BF),
        c_across=sems(2, 2),
        c_pairs=sems(4, NT),
        h_hot=HOTS,
    )


def collect_steps(f, meta, pieces, delta):
    returned, result, dpicks_all = f.b_returned, f.g_result, f.g_dpicks_all
    packed, dpicks, pairs = f.g_packed, f.g_dpicks, f.g_pairs
    member = lax.axis_index(TENSOR)
    total = None
    rows = returned[...].reshape(NDP * SL, 2 * Q)
    lanes = lax.broadcasted_iota(jnp.int32, (NR, 128), 1)
    columns = jnp.zeros((NR, 128), F32)
    part = column_quarter(delta[...], member).astype(F32) * meta[:, 38:39]
    for k in range(2):
        piece = gathered(rows, meta, k, f.h_hot)
        total = piece if total is None else total + piece
        dots = jnp.sum(pieces(k).astype(F32) * part, axis=1, keepdims=True)
        columns = jnp.where(lanes == k, dots, columns)
    total = total.astype(BF)
    packed[:, :Q] = total[:R]
    packed[:, Q:] = total[R:]
    dpicks[:, :NR] = jnp.transpose(columns)[:8]
    dpicks[:, NR:] = jnp.zeros((8, 512 - NR), F32)
    copies = spread_over_tensor(packed, lambda me: result.at[me], pairs, 0)
    copies += spread_over_tensor(dpicks, lambda me: dpicks_all.at[me], pairs, 2)
    result[member] = packed[...]
    dpicks_all[member] = dpicks[...]
    yield
    for copy in copies:
        copy.wait()


def collect_scratch():
    return dict(
        g_packed=pltpu.VMEM((R, 2 * Q), BF),
        g_dpicks=pltpu.VMEM((8, 512), F32),
        g_pairs=sems(4, NT),
        g_result=pltpu.VMEM((NT, R, 2 * Q), BF),
        g_dpicks_all=pltpu.VMEM((NT, 8, 512), F32),
    )


def halves(values):
    high = values.astype(BF)
    return high, (values - high.astype(F32)).astype(BF)


RS_ROWS = ((0, 64), (64, 48))
GR = D // NDP


def sum_dp(pack, result, near, half, held, mine, tile, tiles, core_sems, chip_sems, tile_sems):
    home = lax.axis_index(DP)
    core = home % 2
    chip = home // 2
    partner = home + 1 - 2 * core
    copy = send(pack.at[1 - core], near, core_sems.at[0, 0], core_sems.at[1, 0], DP, partner)
    yield
    copy.wait()
    half[...] = (pack[core].astype(F32) + near[...].astype(F32)).astype(BF)
    chips = [(dy, dx) for dy in (2, 1, 3, 0) for dx in (1, 0) if (dy, dx) != (0, 0)]

    def chip_at(dy, dx):
        return ((chip // 2 + dy) % 4) * 2 + (chip + dx) % 2

    copies = []
    for number, (dy, dx) in enumerate(chips):
        other = chip_at(dy, dx)
        copies.append(
            send(
                half.at[other], held.at[chip], chip_sems.at[0, number], chip_sems.at[1, number],
                DP, other * 2 + core,
            )
        )
    yield
    for copy in copies:
        copy.wait()
    total = half[chip].astype(F32)
    for step in range(1, 8):
        total = total + held[(chip + step) % 8].astype(F32)
    mine[...] = total[:, :768].astype(BF)
    tile[...] = total[:, 768:]
    small = spread_over_tensor(tile, lambda me: tiles.at[me], tile_sems, 0)
    copies = []
    for number, (dy, dx) in enumerate(chips):
        other = chip_at(dy, dx)
        copies.append(
            send(
                mine, result.at[core, chip, :, pl.ds(0, 768)], chip_sems.at[2, number],
                chip_sems.at[3, number], DP, other * 2 + core,
            )
        )
    result[core, chip, :, 0:768] = mine[...]
    yield
    for copy in small:
        copy.wait()
    me = lax.axis_index(TENSOR)
    others = tile[...]
    for step in range(1, NT):
        others = others + tiles[(me + step) % NT]
    lanes = lax.broadcasted_iota(jnp.int32, (GR, 128), 1)
    result[core, chip, :, 768:] = jnp.where(lanes == 33, others, tile[...]).astype(BF)
    for number, (dy, dx) in enumerate(chips):
        other = chip_at(dy, dx)
        place = result.at[core, chip, :, pl.ds(768, 128)]
        copies.append(
            send(
                place, place, chip_sems.at[4, number], chip_sems.at[5, number], DP,
                other * 2 + core,
            )
        )
    yield
    for copy in copies:
        copy.wait()
    copy = send(
        result.at[core], result.at[core], core_sems.at[0, 1], core_sems.at[1, 1], DP, partner
    )
    yield
    copy.wait()


SUM_SCRATCH = dict(
    t_near=pltpu.VMEM((8, GR, GP), BF),
    t_half=pltpu.VMEM((8, GR, GP), BF),
    t_held=pltpu.VMEM((8, GR, GP), BF),
    t_mine=pltpu.VMEM((GR, D), BF),
    t_tile=pltpu.VMEM((GR, 128), F32),
    t_tiles=pltpu.VMEM((NT, GR, 128), F32),
    t_core=sems(2, 2),
    t_chip=sems(6, 8),
    t_tile_sems=sems(2, NT),
    t_pack=pltpu.VMEM((2, 8, GR, GP), BF),
    t_gathers=sems(6, NT),
)


def gathers(sources, targets, pairs, begin):
    def handle(chosen):
        me = lax.axis_index(TENSOR)
        for number in chosen:
            for step in range(1, NT):
                copy = pltpu.make_async_remote_copy(
                    src_ref=sources[number],
                    dst_ref=targets[number].at[me],
                    send_sem=pairs.at[2 * number, step],
                    recv_sem=pairs.at[2 * number + 1, step],
                    device_id={TENSOR: (me + step) % NT},
                    device_id_type=MESH,
                )
                if begin:
                    copy.start()
                else:
                    copy.wait()

    @pl.when(lax.axis_index(PIPE) == 0)
    def _():
        handle((0,))

    @pl.when(lax.axis_index(PIPE) == 1)
    def _():
        handle((1, 2))


def weights_steps(f):
    yield
    projected = f.qkv_in[...]
    for image in range(2):
        for head in range(NH):
            queries, keys, _ = head_parts(projected, image, head)
            f.l_weights[image * NH + head] = probabilities(queries, keys)


def layer_steps(f, last, meta, delta):
    packed, dpicks, state = f.g_result, f.g_dpicks_all, f.state_in
    dqkv, part, dx1_kept, held, near, chosen, pairs, across_sems = (
        f.l_dqkv, f.l_part, f.l_dx1, f.l_held, f.l_near, f.l_chosen, f.l_pairs, f.l_across
    )
    x1 = state[...].astype(F32) + f.summed_in[...].reshape(NR, D).astype(F32)
    live = meta[:, 38:39]
    gate = meta[:, 0:EXPERTS]
    dx2 = delta[...].astype(F32) * live
    total = dpicks[0] + dpicks[1] + dpicks[2] + dpicks[3]
    total = jnp.concatenate([total, jnp.zeros((120, 512), F32)], axis=0)
    columns = jnp.transpose(total)[:NR]
    experts = lax.broadcasted_iota(jnp.int32, (NR, EXPERTS), 1)
    dgate = jnp.zeros((NR, EXPERTS), F32)
    for k in range(2):
        route = meta[:, 36 + k : 37 + k].astype(jnp.int32)
        dgate = dgate + jnp.where(route == experts, columns[:, k : k + 1] * live, 0.0)
    dlogits = gate * (dgate - jnp.sum(gate * dgate, axis=-1, keepdims=True))
    normal, inverse = norm_parts(x1)
    high, low = halves(dlogits)
    dz2 = (
        unpack(packed).astype(F32) + dot(high, f.router[...]) + dot(low, f.router[...])
    )
    dx1 = dx2 + norm_back(dz2, f.gain_two[...], normal, inverse)
    dx1_kept[...] = dx1.reshape(NT, CH, D)
    dattn = dx1.astype(BF)
    if last:
        sources = [f.own_in, f.wide_one_in, f.wide_two_in]
        targets = [f.own, f.wide_one, f.wide_two]
        gathers(sources, targets, f.t_gathers, True)
        for source, target in zip(sources, targets):
            target[lax.axis_index(TENSOR)] = source[...]
    dctx = dot(dattn, f.output[...], 1, 1).astype(BF)
    scale = HD**-0.5
    projected = f.qkv_in[...]
    for image in range(2):
        rows = slice(image * R, (image + 1) * R)
        for head in range(NH):
            queries, keys, values = head_parts(projected, image, head)
            dc = dctx[rows, head * HD : (head + 1) * HD]
            weights = f.l_weights[image * NH + head]
            dweights = dot(dc, values, 1, 1)
            dvalues = dot(weights.astype(BF), dc, 0, 0)
            dscores = weights * (dweights - jnp.sum(weights * dweights, axis=-1, keepdims=True))
            dscores = dscores.astype(BF)
            dqueries = dot(dscores, keys) * scale
            dkeys = dot(dscores, queries, 0, 0) * scale
            for number, value in enumerate((dqueries, dkeys, dvalues)):
                start = number * GW + head * HD
                dqkv[rows, start : start + HD] = value.astype(BF)
    own_part = dot(dqkv[...], f.project[...]).astype(BF)
    part[...] = own_part.reshape(NT, CH, D)
    me = lax.axis_index(TENSOR)
    stage = lax.axis_index(PIPE)
    scattered = [
        [
            send(
                part.at[(me + step) % NT, pl.ds(start, size)],
                held.at[me, pl.ds(start, size)],
                pairs.at[2 * i, step],
                pairs.at[2 * i + 1, step],
                TENSOR,
                (me + step) % NT,
            )
            for step in range(1, NT)
        ]
        for i, (start, size) in enumerate(RS_ROWS)
    ]
    normal_one, _ = norm_parts(state[...].astype(F32))
    normed_one = (normal_one * f.gain_one[...]).astype(BF)
    normed = (normal * f.gain_two[...]).astype(BF)
    gain_rows = [
        jnp.sum(dz2 * normal, axis=0, keepdims=True),
        jnp.sum(own_part.astype(F32) * normal_one, axis=0, keepdims=True),
    ]
    places = lax.broadcasted_iota(jnp.int32, (128, D), 0)
    tall = jnp.where(places == 32, gain_rows[0], 0.0)
    tall = jnp.where(places == 33, gain_rows[1], tall)
    terms = [
        (0, 576, dot(normed_one, dqkv[...], 0, 0)),
        (576, 768, dot(dattn, f.ctx_in[...], 0, 0)),
    ]
    side = jnp.transpose(tall)
    router_term = dot(normed, high, 0, 0) + dot(normed, low, 0, 0)
    side = side + jnp.concatenate([router_term, jnp.zeros((D, 96), F32)], axis=1)
    terms.append((768, GP, side))
    if last:
        one, first, pack = f.grads_one, f.grads_first, f.t_pack
        for low_end, high_end, term in terms:
            term = jnp.where(stage == 0, term, first[:, low_end:high_end])
            term = term + one[:, low_end:high_end]
            pack[:, :, :, low_end:high_end] = term.astype(BF).reshape(
                2, 8, GR, high_end - low_end
            )
        summing = sum_dp(
            pack,
            f.whole,
            f.t_near, f.t_half, f.t_held, f.t_mine, f.t_tile, f.t_tiles, f.t_core, f.t_chip,
            f.t_tile_sems,
        )
        next(summing)
        next(summing)
    else:
        for low_end, high_end, term in terms:
            f.grads[:, low_end:high_end] = term
        f.flush(f.grads)
        summing = iter(())
    waiting = []
    result = f.result
    chunk = chosen if last else f.chunk
    across = []
    for i, (start, size) in enumerate(RS_ROWS):
        rows = pl.ds(start, size)
        for copy in scattered[i]:
            copy.wait_recv()
        dz1 = part[me, rows].astype(F32)
        for step in range(1, NT):
            dz1 = dz1 + held[(me + step) % NT, rows].astype(F32)
        here = pl.ds(pl.multiple_of(me * CH + start, 16), size)
        normal_here, inverse_here = norm_parts(state[here].astype(F32))
        delta_here = norm_back(dz1, f.gain_one[...], normal_here, inverse_here)
        chunk[rows] = (dx1_kept[me, rows] + delta_here).astype(BF)
        if not last:
            across.append(
                send(
                    chunk.at[rows], near.at[rows], across_sems.at[0, i], across_sems.at[1, i],
                    PIPE, 1 - stage,
                )
            )
    for i, (start, size) in enumerate(RS_ROWS):
        rows = pl.ds(start, size)
        if not last:
            across[i].wait_recv()
            chosen[rows] = jnp.where(stage == 1, chunk[rows], near[rows])
        waiting += spread_over_tensor(
            chosen.at[rows], lambda me: result.at[me, rows], pairs, 4 + 2 * i
        )
    result[me] = chosen[...]
    yield
    for _ in summing:
        yield
    if last:
        gathers(sources, targets, f.t_gathers, False)
        f.flush(f.own, f.wide_one, f.wide_two, f.whole)
    for copy in waiting:
        copy.wait()
    for group in scattered:
        for copy in group:
            copy.wait_send()
    for copy in across:
        copy.wait_send()
    f.flush(f.result)
    if not last:
        f.flush(f.chunk)


LAYER_SCRATCH = dict(
    l_dqkv=pltpu.VMEM((NR, 3 * GW), BF),
    l_part=pltpu.VMEM((NT, CH, D), BF),
    l_dx1=pltpu.VMEM((NT, CH, D), F32),
    l_held=pltpu.VMEM((NT, CH, D), BF),
    l_near=pltpu.VMEM((CH, D), BF),
    l_chosen=pltpu.VMEM((CH, D), BF),
    l_pairs=sems(8, NT),
    l_across=sems(2, 2),
    l_weights=pltpu.VMEM((2 * NH, R, R), F32),
    h_hot=HOTS,
)
ROWS_OUT = ((NDP, 2 * SL, D), BF)
BACKWARD_OUTS = dict(
    delta_arrived=ROWS_OUT,
    hidden=ROWS_OUT,
    dpre=ROWS_OUT,
    result=((NT, CH, D), BF),
)
LINEAR_OUTS = dict(chunk=((CH, D), BF), grads=((D, GP), F32))


def finish_kernel(stage, *refs):
    states, grads, whole = refs[:4], refs[4:8], refs[8]
    section_out, input_grad, project_grad, output_grad, router_grad, gains = refs[9:]

    def rows(values):
        values = values.astype(F32)
        return jnp.concatenate([values[:IMG_LEN], values[R : R + IMG_LEN]], axis=0).astype(BF)

    def place(base):
        for micro in range(2):
            section_out[micro] = rows(unpack(states[base + micro]))
            input_grad[micro] = rows(grads[base + micro][...])

    @pl.when(stage[0, 0] == 0)
    def _():
        place(0)

    @pl.when(stage[0, 0] != 0)
    def _():
        place(2)

    project_grad[...] = jnp.transpose(whole[:, :576].astype(F32))
    output_grad[...] = jnp.transpose(whole[:, 576:768].astype(F32))
    side = whole[:, 768:].astype(F32)
    side = jnp.transpose(side)
    router_grad[...] = side[:EXPERTS]
    gains[...] = side[EXPERTS : EXPERTS + 8]


def finish(stage, states, grads, whole):
    return pl.pallas_call(
        finish_kernel,
        in_specs=[SMEM] + [VMEM] * 9,
        out_shape=[
            jax.ShapeDtypeStruct((2, 2 * IMG_LEN, D), BF),
            jax.ShapeDtypeStruct((2, 2 * IMG_LEN, D), BF),
            jax.ShapeDtypeStruct((3 * GW, D), F32),
            jax.ShapeDtypeStruct((GW, D), F32),
            jax.ShapeDtypeStruct((EXPERTS, D), F32),
            jax.ShapeDtypeStruct((8, D), F32),
        ],
        compiler_params=params(),
        name="finish",
    )(stage, *states, *grads, whole)


def body(
    tokens,
    cotangent,
    image_counts,
    routes,
    attn_norm_gain,
    query_key_value,
    attn_output,
    moe_norm_gain,
    router_weight,
    expert_in,
    expert_down,
):
    project = query_key_value[0].transpose(1, 2, 0).reshape(3 * GW, D)
    stage = lax.axis_index(PIPE)
    all_axes = (TENSOR, DP, PIPE)
    gains = dict(gain_one=(attn_norm_gain, VMEM), gain_two=(moe_norm_gain, VMEM))
    small = dict(project=project, output=attn_output[0], router=router_weight[0].T)
    heavy = dict(first=expert_in[0], second=expert_down[0])
    placing = dict(counts=(image_counts, SMEM), routes=(routes, VMEM))

    def place_of(f, moment):
        home = lax.axis_index(DP)
        one, other = min(moment, 1), max(moment - 1, 0)
        early = lax.axis_index(PIPE) == 0
        count = jnp.where(early, f.counts[one, home], f.counts[other, home])
        path = jnp.where(early, f.routes[one], f.routes[other])
        return count, padded(path)

    def forward(moment, arriving):
        def program(f):
            if moment == 0:
                state = padded(f.tokens[0])
            else:
                early = lax.axis_index(PIPE) == 0
                state = jnp.where(early, padded(f.tokens[1]), unpack(f.arriving))
            drive(attention_steps(f, state), places_steps(f, *place_of(f, moment)))
            drive(dispatch_steps(f, True))
            drive(experts_forward_steps(f, f.arrived), hot_steps(f.meta, f.h_hot))
            drive(combine_steps(f, True, f.meta, f.h_hot))

        outs = dict(FORWARD_OUTS)
        outs["packed"] = ((R, 2 * Q), BF)
        outs["pieces"] = ((2, NR, Q), BF)
        outs["onward"] = ((NT, R, 2 * Q), BF)
        plain = dict(**gains, **placing, tokens=(tokens, VMEM))
        if moment > 0:
            plain["arriving"] = (arriving, VMEM)
        return launch(
            "forward_%d" % moment, 1 + moment, all_axes, plain, dict(**small, **heavy), outs,
            dict(
                **forward_scratch(), **prefixed("d_", to_experts_scratch(True)), **prefixed("f_", expert_scratch()),
                **combine_scratch(),
            ),
            program,
        )

    def kept(saved):
        return dict(
            state_in=saved.state,
            summed_in=saved.summed,
            qkv_in=saved.qkv,
            ctx_in=saved.ctx,
            meta_in=saved.meta,
            arrived_in=saved.arrived,
        )

    def either(one, other):
        return {key: (one[key], other[key]) for key in one}

    backward_scratch = dict(**prefixed("b_", expert_scratch()), **collect_scratch(), **LAYER_SCRATCH)
    zero = forward(0, None)
    one = forward(1, zero.onward)

    def turning(f):
        state = unpack(f.arriving)
        delta = padded(f.delta[0])
        f.delta_kept[...] = delta
        drive(
            chain(
                lambda: spread_steps(f, False, delta, f.meta_in),
                lambda: experts_backward_steps(f, f.arrived_in),
                lambda: collect_steps(f, f.meta_in, lambda k: f.pieces_in[k], f.delta_kept),
                lambda: layer_steps(f, False, f.meta_in, f.delta_kept),
            ),
            chain(lambda: attention_steps(f, state), lambda: dispatch_steps(f, False)),
            places_steps(f, *place_of(f, 2)),
            hot_steps(f.meta_in, f.h_hot),
            weights_steps(f),
        )

    two = launch(
        "turning", 3, all_axes,
        dict(**gains, **placing, delta=(cotangent, VMEM), arriving=(one.onward, VMEM)),
        dict(**small, **kept(one), pieces_in=one.pieces, **heavy),
        dict(**FORWARD_OUTS, **BACKWARD_OUTS, **LINEAR_OUTS),
        dict(
            **forward_scratch(), **prefixed("d_", to_experts_scratch(False)),
            **prefixed("s_", to_experts_scratch(False)), **backward_scratch,
            delta_kept=pltpu.VMEM((NR, D), BF),
        ),
        turning,
    )

    def middle(f):
        early = lax.axis_index(PIPE) == 0
        delta = jnp.where(early, f.arriving[...].reshape(NR, D), padded(f.delta[1]))
        f.delta_kept[...] = delta
        drive(
            chain(
                lambda: spread_steps(f, False, delta, f.meta_in),
                lambda: experts_backward_steps(f, f.arrived_in),
                lambda: collect_steps(
                    f,
                    f.meta_in,
                    lambda k: jnp.where(early, f.pieces_in[k], f.pieces[k]),
                    f.delta_kept,
                ),
                lambda: layer_steps(f, False, f.meta_in, f.delta_kept),
            ),
            chain(
                lambda: experts_forward_steps(f, f.late_arrived),
                lambda: combine_steps(f, False, f.late_meta, f.k_hot),
            ),
            chain(lambda: hot_steps(f.late_meta, f.k_hot), lambda: hot_steps(f.meta_in, f.h_hot)),
            weights_steps(f),
        )

    three = launch(
        "middle", 4, all_axes,
        dict(**gains, delta=(cotangent, VMEM), arriving=(two.result, VMEM)),
        dict(
            **either(kept(zero), kept(two)), **heavy, late_arrived=two.arrived,
            late_meta=two.meta, state=two.state, summed=two.summed,
            pieces_in=zero.pieces, **small,
        ),
        dict(**BACKWARD_OUTS, **LINEAR_OUTS, packed=((R, 2 * Q), BF)),
        dict(
            **prefixed("s_", to_experts_scratch(False)), **prefixed("f_", expert_scratch()), **backward_scratch,
            pieces=pltpu.VMEM((2, NR, Q), BF), k_hot=HOTS, delta_kept=pltpu.VMEM((NR, D), BF),
        ),
        middle,
    )

    def ending(f):
        delta = f.arriving[...].reshape(NR, D)
        f.delta_kept[...] = delta
        drive(spread_steps(f, True, delta, f.meta_in))
        drive(
            experts_backward_steps(f, f.arrived_in),
            hot_steps(f.meta_in, f.h_hot),
            weights_steps(f),
        )
        drive(
            collect_steps(f, f.meta_in, lambda k: f.pieces_in[k], f.delta_kept)
        )
        drive(layer_steps(f, True, f.meta_in, f.delta_kept))

    wide = ((NT, R, 2 * Q), BF)
    four = launch(
        "ending", 5, (TENSOR, DP),
        dict(**gains, arriving=(three.result, VMEM)),
        dict(
            **kept(one), **heavy, pieces_in=one.pieces, **small,
            own_in=three.chunk, wide_one_in=one.packed,
            wide_two_in=three.packed, grads_one=three.grads,
            grads_first=two.grads,
        ),
        dict(
            **BACKWARD_OUTS, whole=((2, 8, GR, GP), BF), own=((NT, CH, D), BF),
            wide_one=wide, wide_two=wide,
        ),
        dict(
            **prefixed("s_", to_experts_scratch(True)), **backward_scratch, **SUM_SCRATCH,
            delta_kept=pltpu.VMEM((NR, D), BF),
        ),
        ending,
    )

    def outer(saved, results):
        return (saved.arrived, results.dpre, results.hidden, results.delta_arrived)

    early = stage == 0
    middle_arrived = jnp.where(early, zero.arrived, two.arrived)
    grad_first, grad_second = expert_grads(
        stage.reshape(1).astype(jnp.int32),
        outer(SimpleNamespace(arrived=middle_arrived), three),
        outer(one, four),
        outer(one, two),
    )
    section_out, input_grad, project_grad, output_grad, router_grad, gain_grads = finish(
        stage.reshape(1, 1).astype(jnp.int32),
        [zero.onward, one.onward, four.wide_one, four.wide_two],
        [
            array.reshape(NR, D)
            for array in (four.own, four.result, two.result, three.result)
        ],
        four.whole.reshape(D, GP),
    )
    return (
        section_out[None],
        input_grad[None],
        gain_grads[1:2],
        project_grad.reshape(1, 3, GW, D).transpose(0, 3, 1, 2),
        output_grad[None],
        gain_grads[0:1],
        router_grad.T[None],
        grad_first[None],
        grad_second[None],
    )


def solution(mesh):
    placed = (
        P(None, DP, None),
        P(None, DP, None),
        P(),
        P(None, DP, None),
        P(PIPE, None),
        P(PIPE, None, None, TENSOR),
        P(PIPE, TENSOR, None),
        P(PIPE, None),
        P(PIPE, None, None),
        P(PIPE, DP, None, TENSOR),
        P(PIPE, DP, TENSOR, None),
    )
    return jax.shard_map(
        body,
        mesh=mesh,
        in_specs=placed,
        out_specs=(
            P(PIPE, None, DP, None),
            P(PIPE, None, DP, None),
            P(PIPE, None),
            P(PIPE, None, None, TENSOR),
            P(PIPE, TENSOR, None),
            P(PIPE, None),
            P(PIPE, None, None),
            P(PIPE, DP, None, TENSOR),
            P(PIPE, DP, TENSOR, None),
        ),
        check_vma=False,
    )
```

```python
from types import SimpleNamespace

import jax
import jax.numpy as jnp
from jax import lax
from jax.experimental import pallas as pl
from jax.experimental.pallas import tpu as pltpu
from jax.sharding import PartitionSpec as P

TENSOR, PIPE, DP = "tensor", "pipe", "dp"
BF = jnp.bfloat16
F32 = jnp.float32
MESH = pl.DeviceIdType.MESH
D = 768
HD = 64
NH = 3
GW = NH * HD
IMG_LEN = 197
R = 224
NR = 2 * R
CH = NR // 4
EXPERTS = 32
SL = 32
NT = 4
NDP = 16
Q = D // NT
EPSILON = 1e-06
VMEM_BYTES = 58 * 1024 * 1024
GP = 896


def dot(a, b, ca=1, cb=0):
    return lax.dot_general(a, b, (((ca,), (cb,)), ((), ())), preferred_element_type=F32)


def params(**more):
    return pltpu.CompilerParams(vmem_limit_bytes=VMEM_BYTES, **more)


def norm_parts(values):
    mean = jnp.mean(values, axis=-1, keepdims=True)
    centred = values - mean
    inverse = lax.rsqrt(jnp.mean(centred * centred, axis=-1, keepdims=True) + EPSILON)
    return centred * inverse, inverse


def norm_back(delta, gain, normal, inverse):
    scaled = delta * gain
    return inverse * (
        scaled
        - jnp.mean(scaled, axis=-1, keepdims=True)
        - normal * jnp.mean(scaled * normal, axis=-1, keepdims=True)
    )


def pick(index, options):
    result = options[0]
    for number in range(1, len(options)):
        result = jnp.where(index == number, options[number], result)
    return result


def column_quarter(values, member):
    return pick(member, [values[:, Q * q : Q * (q + 1)] for q in range(NT)])


def unpack(packed):
    images = [
        jnp.concatenate([packed[q][:, Q * i : Q * (i + 1)] for q in range(NT)], axis=1)
        for i in range(2)
    ]
    return jnp.concatenate(images, axis=0)


def head_parts(projected, image, head):
    rows = slice(image * R, (image + 1) * R)
    return [
        projected[rows, part * GW + head * HD : part * GW + (head + 1) * HD] for part in range(3)
    ]


def probabilities(queries, keys):
    scores = dot(queries, keys, 1, 1) * (HD**-0.5)
    held = lax.broadcasted_iota(jnp.int32, scores.shape, 1) < IMG_LEN
    scores = jnp.where(held, scores, -1e30)
    exponent = jnp.exp(scores - jnp.max(scores, axis=-1, keepdims=True))
    return exponent / jnp.sum(exponent, axis=-1, keepdims=True)


VMEM = pl.BlockSpec(memory_space=pltpu.VMEM)
SMEM = pl.BlockSpec(memory_space=pltpu.SMEM)
ANYWHERE = pl.BlockSpec(memory_space=pl.ANY)


def drive(*running):
    running = list(running)
    while running:
        for steps in list(running):
            if next(steps, StopIteration) is StopIteration:
                running.remove(steps)


OUT, SEM, SOURCE = "out ", "sem ", ("/0", "/1")


def prefixed(prefix, items):
    return {prefix + name: item for name, item in items.items()}


def chain(*makers):
    for maker in makers:
        yield from maker()


class Frame:
    def __init__(self, barrier, count):
        self.barrier = barrier
        self.count = count
        self.met = False
        self.loading = {}
        self.storing = []
        self.refs = {}

    def meet(self):
        if not self.met:
            pl.semaphore_wait(self.barrier, self.count)
            self.met = True

    def __getattr__(self, name):
        if name in self.loading:
            self.loading.pop(name).wait()
        return self.refs[name]

    def group(self, prefix):
        size = len(prefix)
        return SimpleNamespace(
            **{name[size:]: ref for name, ref in self.refs.items() if name[:size] == prefix}
        )

    def flush(self, *refs):
        for ref in refs:
            name = next(name for name, known in self.refs.items() if known is ref)
            copy = pltpu.make_async_copy(ref, self.refs[OUT + name], self.refs[SEM + name])
            copy.start()
            self.storing.append(copy)


def greet(axes):
    barrier = pltpu.get_barrier_semaphore()
    count = 0
    for axis in axes:
        size = lax.axis_size(axis)
        me = lax.axis_index(axis)
        for step in range(1, size):
            pl.semaphore_signal(
                barrier, inc=1, device_id={axis: (me + step) % size}, device_id_type=MESH
            )
        count += size - 1
    return barrier, count


def launch(name, number, axes, plain, lazy, outs, scratch, program):
    arrays, specs, places = [], [], []
    for key, (array, spec) in plain.items():
        arrays.append(array)
        specs.append(spec)
        places.append(key)
    for key, item in lazy.items():
        for position, array in enumerate(item if isinstance(item, tuple) else (item,)):
            arrays.append(array)
            specs.append(ANYWHERE)
            places.append(key + SOURCE[position])
    held = dict(scratch)
    for key, item in lazy.items():
        array = item[0] if isinstance(item, tuple) else item
        held[key] = pltpu.VMEM(array.shape, array.dtype)
        held[SEM + key] = pltpu.SemaphoreType.DMA
    for key, (shape, dtype) in outs.items():
        held[key] = pltpu.VMEM(shape, dtype)
        held[SEM + key] = pltpu.SemaphoreType.DMA

    def kernel(*refs):
        frame = Frame(*greet(axes))
        names = places + [OUT + key for key in outs] + list(held)
        frame.refs = dict(zip(names, refs))
        stage = lax.axis_index(PIPE)
        for key, item in lazy.items():
            target, sem = frame.refs[key], frame.refs[SEM + key]
            copy = pltpu.make_async_copy(frame.refs[key + SOURCE[0]], target, sem)
            if isinstance(item, tuple):
                other = pltpu.make_async_copy(frame.refs[key + SOURCE[1]], target, sem)
                pl.when(stage == 0)(copy.start)
                pl.when(stage != 0)(other.start)
            else:
                copy.start()
            frame.loading[key] = copy
        program(frame)
        for copy in list(frame.loading.values()) + frame.storing:
            copy.wait()

    results = pl.pallas_call(
        kernel,
        in_specs=specs,
        out_specs=[ANYWHERE] * len(outs),
        out_shape=[jax.ShapeDtypeStruct(*out) for out in outs.values()],
        scratch_shapes=list(held.values()),
        compiler_params=params(collective_id=number, has_side_effects=True),
        name=name,
    )(*arrays)
    return SimpleNamespace(**dict(zip(outs, results)))


def send(source, target, send_sem, recv_sem, axis, peer):
    copy = pltpu.make_async_remote_copy(
        src_ref=source,
        dst_ref=target,
        send_sem=send_sem,
        recv_sem=recv_sem,
        device_id={axis: peer},
        device_id_type=MESH,
    )
    copy.start()
    return copy


def sems(*shape):
    return pltpu.SemaphoreType.DMA(shape)


def spread_over_tensor(source, target_of, pairs, row):
    me = lax.axis_index(TENSOR)
    return [
        send(
            source, target_of(me), pairs.at[row, step], pairs.at[row + 1, step], TENSOR,
            (me + step) % NT,
        )
        for step in range(1, NT)
    ]


def padded(values):
    kind = values.dtype
    values = values if kind == jnp.int32 else values.astype(F32)
    blank = jnp.zeros((R - IMG_LEN, values.shape[1]), values.dtype)
    return jnp.concatenate(
        [values[:IMG_LEN], blank, values[IMG_LEN:], blank], axis=0
    ).astype(kind)


def forward_scratch():
    return dict(
        a_part=pltpu.VMEM((NT, CH, D), BF),
        a_held=pltpu.VMEM((NT, CH, D), BF),
        a_mine=pltpu.VMEM((CH, D), BF),
        a_pairs=sems(8, NT),
        d_hot=pltpu.VMEM((NR, EXPERTS * SL), BF),
        d_match=pltpu.VMEM((2, NR, EXPERTS), F32),
    )


FORWARD_OUTS = dict(
    state=((NR, D), BF),
    qkv=((NR, 3 * GW), BF),
    ctx=((NR, GW), BF),
    summed=((NT, CH, D), BF),
    meta=((NR, 128), F32),
    arrived=((NDP, 2 * SL, D), BF),
)


def attention_steps(f, state):
    part, held, mine, pairs = (f.a_part, f.a_held, f.a_mine, f.a_pairs)
    qkv, ctx, summed = f.qkv, f.ctx, f.summed
    f.state[...] = state
    normal, _ = norm_parts(state.astype(F32))
    normed = (normal * f.gain_one[...]).astype(BF)
    projected = dot(normed, f.project[...], 1, 1).astype(BF)
    qkv[...] = projected
    for image in range(2):
        for head in range(NH):
            queries, keys, values = head_parts(projected, image, head)
            weights = probabilities(queries, keys).astype(BF)
            ctx[image * R : (image + 1) * R, head * HD : (head + 1) * HD] = dot(
                weights, values
            ).astype(BF)
    part[...] = dot(ctx[...], f.output[...]).astype(BF).reshape(NT, CH, D)
    f.meet()
    me = lax.axis_index(TENSOR)
    scattered = [
        [
            send(
                part.at[(me + step) % NT, pl.ds(start, size)], held.at[me, pl.ds(start, size)],
                pairs.at[4 * i, step], pairs.at[4 * i + 1, step], TENSOR, (me + step) % NT,
            )
            for step in range(1, NT)
        ]
        for i, (start, size) in enumerate(RS_ROWS)
    ]
    f.flush(f.state, f.qkv, f.ctx)
    yield
    copies = []
    for i, (start, size) in enumerate(RS_ROWS):
        rows = pl.ds(start, size)
        for copy in scattered[i]:
            copy.wait()
        total = part[me, rows].astype(F32)
        for step in range(1, NT):
            total = total + held[(me + step) % NT, rows].astype(F32)
        mine[rows] = total.astype(BF)
        copies += spread_over_tensor(
            mine.at[rows], lambda me: summed.at[me, rows], pairs, 4 * i + 2
        )
    summed[me] = mine[...]
    yield
    for copy in copies:
        copy.wait()
    f.flush(f.summed)


RELATIVE = [(dy, dx, dc) for dy in (2, 1, 3, 0) for dx in (1, 0) for dc in (0, 1)]
RELATIVE.remove((0, 0, 0))


def peer_at(relative, sign):
    dy, dx, dc = relative
    me = lax.axis_index(DP)
    row = (me // 4 + sign * dy + 4) % 4
    return row * 4 + ((me // 2 + dx) % 2) * 2 + (me + dc) % 2


def quartered(relative):
    return relative[0] != 0 and relative[1] == 1


SHORT = [relative for relative in RELATIVE if quartered(relative)]


def to_experts(outbox, arrived, pairs, relayed, hybrid):
    me = lax.axis_index(DP)
    member = lax.axis_index(TENSOR)
    rows = pl.ds(pl.multiple_of(member * 16, 16), 16)
    direct, relays, order = [], [], []
    for number, relative in enumerate(RELATIVE):
        peer = peer_at(relative, 1)
        short = hybrid and quartered(relative)
        copy = send(
            outbox.at[peer, rows] if short else outbox.at[peer],
            arrived.at[me, rows] if short else arrived.at[me],
            pairs.at[0, number],
            pairs.at[1, number],
            DP,
            peer,
        )
        if short:
            order.append((number, relative, copy))
        else:
            direct.append(copy)
    arrived[me] = outbox[me]
    yield
    order.sort(key=lambda item: item[1][0] == 2)
    for _, relative, copy in order:
        number = SHORT.index(relative)
        copy.wait_recv()
        source = peer_at(relative, -1)
        for step in range(1, NT):
            relays.append(
                send(
                    arrived.at[source, rows],
                    arrived.at[source, rows],
                    relayed.at[0, number, step],
                    relayed.at[1, number, step],
                    TENSOR,
                    (member + step) % NT,
                )
            )
    for _ in range(6):
        yield
    for copy in direct:
        copy.wait()
    for _, _, copy in order:
        copy.wait_send()
    for copy in relays:
        copy.wait()


def to_experts_scratch(hybrid):
    return dict(
        outbox=pltpu.VMEM((NDP, 2 * SL, D), BF),
        pairs=sems(2, NDP),
        relayed=sems(2, len(SHORT), NT) if hybrid else sems(2, 1, 1),
    )


def live_rows(count):
    row = lax.broadcasted_iota(jnp.int32, (NR, 1), 0)
    image = (row >= R).astype(jnp.int32)
    return (image < count) & (row - image * R < IMG_LEN)


def places_steps(f, count, routes):
    meta = f.meta
    live = live_rows(count)
    experts = lax.broadcasted_iota(jnp.int32, (NR, EXPERTS), 1)
    route = [routes[:, k : k + 1] for k in range(2)]
    match = [jnp.where(live & (route[k] == experts), 1.0, 0.0) for k in range(2)]
    above = lax.broadcasted_iota(jnp.int32, (NR, NR), 1) < lax.broadcasted_iota(
        jnp.int32, (NR, NR), 0
    )
    before = dot(jnp.where(above, 1.0, 0.0).astype(BF), (match[0] + match[1]).astype(BF))
    hot = None
    slots = lax.broadcasted_iota(jnp.int32, (NR, EXPERTS * SL), 1)
    for k in range(2):
        slot = jnp.sum(match[k] * before, axis=1, keepdims=True).astype(jnp.int32)
        position = jnp.where(live, route[k] * SL + slot, -1)
        meta[:, 34 + k : 35 + k] = position.astype(F32)
        meta[:, 36 + k : 37 + k] = route[k].astype(F32)
        f.d_match[k] = match[k]
        same = slots == position
        hot = same if hot is None else hot | same
    meta[:, 38:39] = jnp.where(live, 1.0, 0.0)
    f.d_hot[...] = jnp.where(hot, 1.0, 0.0).astype(BF)
    yield


def dispatch_steps(f, hybrid):
    state, summed, meta = f.state, f.summed, f.meta
    outbox, arrived = f.d_outbox, f.arrived
    values = state[...].astype(F32) + summed[...].reshape(NR, D).astype(F32)
    normal, _ = norm_parts(values)
    normed = (normal * f.gain_two[...]).astype(BF)
    outbox[...] = dot(f.d_hot[...], normed, 0, 0).astype(BF).reshape(NDP, 2 * SL, D)
    f.meet()
    sending = to_experts(outbox, arrived, f.d_pairs, f.d_relayed, hybrid)
    next(sending)
    logits = dot(normed, f.router[...], 1, 1)
    exponent = jnp.exp(logits - jnp.max(logits, axis=-1, keepdims=True))
    gate = exponent / jnp.sum(exponent, axis=-1, keepdims=True)
    meta[:, 0:EXPERTS] = gate
    for k in range(2):
        meta[:, 32 + k : 33 + k] = jnp.sum(f.d_match[k] * gate, axis=1, keepdims=True)
    f.flush(f.meta)
    yield
    yield from sending
    f.flush(f.arrived)


def spread_steps(f, hybrid, delta, meta):
    outbox, arrived = f.s_outbox, f.delta_arrived
    values = delta[...].astype(F32) * meta[:, 38:39]
    slots = lax.broadcasted_iota(jnp.int32, (NR, EXPERTS * SL), 1)
    total = None
    for k in range(2):
        position = meta[:, 34 + k : 35 + k].astype(jnp.int32)
        hot = jnp.where(slots == position, 1.0, 0.0).astype(BF)
        scaled = (values * meta[:, 32 + k : 33 + k]).astype(BF)
        term = dot(hot, scaled, 0, 0)
        total = term if total is None else total + term
    outbox[...] = total.astype(BF).reshape(NDP, 2 * SL, D)
    f.meet()
    yield from to_experts(outbox, arrived, f.s_pairs, f.s_relayed, hybrid)
    f.flush(f.delta_arrived)


CUBE = 0.044715
ROOT = 0.7978845608028654


def gelu_parts(pre):
    squared = pre * pre
    inner = jnp.tanh(ROOT * (pre + CUBE * pre * squared))
    return 0.5 * pre * (1.0 + inner), inner, squared


def store_quarters(target, expert, values):
    values = values.astype(BF).reshape(NDP, 2, 16, D)
    for q in range(NT):
        for half in range(2):
            target[q, expert, :, :, half * Q : (half + 1) * Q] = values[
                :, half, :, q * Q : (q + 1) * Q
            ]


def expert_steps(f, key, compute):
    part, held, mine, passing, pairs = (key.part, key.held, key.mine, key.passing, key.pairs)
    me = lax.axis_index(TENSOR)
    home = lax.axis_index(DP)
    group = home // 4
    near = ((me + 1) % NT, (me + 3) % NT)
    far = (me + 2) % NT
    half = (pl.ds(0, 8), pl.ds(8, 8))

    def begin(expert):
        return [
            send(
                part.at[far, expert, half[way]], passing.at[way, expert],
                key.pass_sems.at[0, way, expert], key.pass_sems.at[1, way, expert],
                TENSOR, near[way],
            )
            for way in range(2)
        ]

    def add_passing(expert, copies):
        for way in range(2):
            copies[way].wait()
            rows = (near[way], expert, half[way])
            part[rows] = (part[rows].astype(F32) + passing[way, expert].astype(F32)).astype(BF)

    store_quarters(part, 0, compute(0))
    f.meet()
    one = begin(0)
    yield
    store_quarters(part, 1, compute(1))
    two = begin(1)
    add_passing(0, one)
    whole = [
        send(
            part.at[near[way], 0], held.at[way, 0], key.sums.at[0, 4, way],
            key.sums.at[1, 4, way], TENSOR, near[way],
        )
        for way in range(2)
    ]
    yield
    add_passing(1, two)
    scattered = []
    for turn in range(4):
        block = ((group + turn + 1) % 4) * 4
        for way in range(2):
            scattered.append(
                send(
                    part.at[near[way], 1, pl.ds(block, 4)],
                    held.at[way, 1, pl.ds(block, 4)],
                    key.sums.at[0, turn, way],
                    key.sums.at[1, turn, way],
                    TENSOR,
                    near[way],
                )
            )
    yield
    for copy in whole:
        copy.wait()
    total = part[me, 0].astype(F32) + held[0, 0].astype(F32) + held[1, 0].astype(F32)
    mine[:, 0] = total.astype(BF)
    returned = []
    for turn in range(4):
        block = ((group + turn + 1) % 4) * 4
        for way in range(2):
            scattered[turn * 2 + way].wait_recv()
        rows = pl.ds(block, 4)
        total = part[me, 1, rows].astype(F32)
        for way in range(2):
            total = total + held[way, 1, rows].astype(F32)
        mine[rows, 1] = total.astype(BF)
        for number in range(4):
            if turn == 3 and number == 0:
                key.returned[home] = mine[home]
                continue
            offset = (turn + 1) % 4 * 4 + number
            peer = block + (home + number) % 4
            returned.append(
                send(
                    mine.at[peer], key.returned.at[home], pairs.at[0, offset],
                    pairs.at[1, offset], DP, peer,
                )
            )
        yield
    for copy in returned:
        copy.wait()
    for copy in scattered:
        copy.wait_send()


def expert_scratch():
    return dict(
        part=pltpu.VMEM((NT, 2, NDP, 16, 2 * Q), BF),
        held=pltpu.VMEM((2, 2, NDP, 16, 2 * Q), BF),
        passing=pltpu.VMEM((2, 2, 8, 16, 2 * Q), BF),
        pass_sems=sems(2, 2, 2),
        mine=pltpu.VMEM((NDP, 2, 16, 2 * Q), BF),
        sums=sems(2, 5, 2),
        pairs=sems(2, NDP),
        returned=pltpu.VMEM((NDP, 2, 16, 2 * Q), BF),
    )


def expert_rows(ref, expert):
    return ref[:, expert * SL : (expert + 1) * SL].reshape(NDP * SL, D)


def experts_forward_steps(f, arrived):
    def compute(expert):
        hidden = gelu_parts(dot(expert_rows(arrived, expert), f.first[expert]))[0].astype(BF)
        return dot(hidden, f.second[expert])

    yield from expert_steps(f, f.group("f_"), compute)


def experts_backward_steps(f, arrived):
    delta, hidden_out, dpre_out = f.delta_arrived, f.hidden, f.dpre

    def compute(expert):
        place = slice(expert * SL, (expert + 1) * SL)
        pre = dot(expert_rows(arrived, expert), f.first[expert])
        hidden, inner, squared = gelu_parts(pre)
        hidden_out[:, place] = hidden.astype(BF).reshape(NDP, SL, D)
        slope = 0.5 * (1.0 + inner) + (0.5 * ROOT) * pre * (1.0 - inner * inner) * (
            1.0 + 3.0 * CUBE * squared
        )
        dhidden = dot(expert_rows(delta, expert), f.second[expert], 1, 1)
        dpre = (dhidden.astype(BF).astype(F32) * slope).astype(BF)
        dpre_out[:, place] = dpre.reshape(NDP, SL, D)
        result = dot(dpre, f.first[expert], 1, 1)
        if expert == 1:
            f.flush(f.hidden, f.dpre)
        return result

    yield from expert_steps(f, f.group("b_"), compute)


def expert_grads_kernel(stage, *refs):
    grad_first, grad_second = refs[12:]

    def flat(ref):
        return ref[...].reshape(NDP * SL, D)

    def pairs(a, b):
        grad_first[0] = dot(flat(a[0]), flat(a[1]), 0, 0) + dot(flat(b[0]), flat(b[1]), 0, 0)
        grad_second[0] = dot(flat(a[2]), flat(a[3]), 0, 0) + dot(flat(b[2]), flat(b[3]), 0, 0)

    @pl.when(stage[0] == 0)
    def _():
        pairs(refs[0:4], refs[4:8])

    @pl.when(stage[0] != 0)
    def _():
        pairs(refs[0:4], refs[8:12])


def expert_grads(stage, both, first_only, last_only):
    shape = (NDP, SL, D)
    weights = pl.BlockSpec((1, D, D), lambda p, s: (p, 0, 0))
    return pl.pallas_call(
        expert_grads_kernel,
        grid_spec=pltpu.PrefetchScalarGridSpec(
            num_scalar_prefetch=1,
            grid=(2,),
            in_specs=[pl.BlockSpec(shape, lambda p, s: (0, p, 0))] * 4
            + [pl.BlockSpec(shape, lambda p, s: (0, p * (1 - s[0]), 0))] * 4
            + [pl.BlockSpec(shape, lambda p, s: (0, p * s[0], 0))] * 4,
            out_specs=[weights, weights],
        ),
        out_shape=[jax.ShapeDtypeStruct((2, D, D), F32)] * 2,
        compiler_params=params(),
        name="expert_grads",
    )(stage, *both, *first_only, *last_only)


def hot_steps(meta, hots):
    yield
    for k in range(2):
        position = meta[:, 34 + k : 35 + k].astype(jnp.int32)
        place = jnp.where(position >= 0, (position // SL) * 16 + position % 16, -1)
        hot = lax.broadcasted_iota(jnp.int32, (NR, NDP * SL), 1) == place
        hots[k] = jnp.where(hot, 1.0, 0.0).astype(BF)


def gathered(returned, meta, k, hots):
    position = meta[:, 34 + k : 35 + k].astype(jnp.int32)
    odd = (position // 16) % 2 == 1
    both = dot(hots[k], returned)
    return jnp.where(odd, both[:, Q:], both[:, :Q])


HOTS = pltpu.VMEM((2, NR, NDP * SL), BF)
HALVES = (slice(0, CH), slice(CH, R))


def combine_steps(f, onward, meta, hots):
    packed, pieces, returned = f.packed, f.pieces, f.f_returned
    member = lax.axis_index(TENSOR)
    live = meta[:, 38:39]
    total = column_quarter(f.state[...], member).astype(F32) + column_quarter(
        f.summed[...].reshape(NR, D), member
    ).astype(F32)
    rows = returned[...].reshape(NDP * SL, 2 * Q)
    for k in range(2):
        piece = gathered(rows, meta, k, hots)
        pieces[k] = piece.astype(BF)
        total = total + meta[:, 32 + k : 33 + k] * piece
    total = (total * live).astype(BF)
    packed[:, :Q] = total[:R]
    packed[:, Q:] = total[R:]
    f.flush(f.packed)
    if not onward:
        return
    f.flush(f.pieces)
    result = f.onward
    near, chosen, across_sems, pairs = (f.c_near, f.c_chosen, f.c_across, f.c_pairs)
    stage = lax.axis_index(PIPE)
    across = [
        send(
            packed.at[half], near.at[half], across_sems.at[0, i], across_sems.at[1, i], PIPE,
            1 - stage,
        )
        for i, half in enumerate(HALVES)
    ]
    copies = []
    for i, half in enumerate(HALVES):
        across[i].wait_recv()
        chosen[half] = jnp.where(stage == 0, packed[half], near[half])
        copies += spread_over_tensor(
            chosen.at[half], lambda me: result.at[me, half], pairs, 2 * i
        )
    result[member] = chosen[...]
    yield
    for copy in copies:
        copy.wait()
    for copy in across:
        copy.wait_send()
    f.flush(f.onward)


def combine_scratch():
    return dict(
        c_near=pltpu.VMEM((R, 2 * Q), BF),
        c_chosen=pltpu.VMEM((R, 2 * Q), BF),
        c_across=sems(2, 2),
        c_pairs=sems(4, NT),
        h_hot=HOTS,
    )


def collect_steps(f, meta, pieces, delta):
    returned, result, dpicks_all = f.b_returned, f.g_result, f.g_dpicks_all
    packed, dpicks, pairs = f.g_packed, f.g_dpicks, f.g_pairs
    member = lax.axis_index(TENSOR)
    total = None
    rows = returned[...].reshape(NDP * SL, 2 * Q)
    lanes = lax.broadcasted_iota(jnp.int32, (NR, 128), 1)
    columns = jnp.zeros((NR, 128), F32)
    part = column_quarter(delta[...], member).astype(F32) * meta[:, 38:39]
    for k in range(2):
        piece = gathered(rows, meta, k, f.h_hot)
        total = piece if total is None else total + piece
        dots = jnp.sum(pieces(k).astype(F32) * part, axis=1, keepdims=True)
        columns = jnp.where(lanes == k, dots, columns)
    total = total.astype(BF)
    packed[:, :Q] = total[:R]
    packed[:, Q:] = total[R:]
    dpicks[:, :NR] = jnp.transpose(columns)[:8]
    dpicks[:, NR:] = jnp.zeros((8, 512 - NR), F32)
    copies = spread_over_tensor(packed, lambda me: result.at[me], pairs, 0)
    copies += spread_over_tensor(dpicks, lambda me: dpicks_all.at[me], pairs, 2)
    result[member] = packed[...]
    dpicks_all[member] = dpicks[...]
    yield
    for copy in copies:
        copy.wait()


def collect_scratch():
    return dict(
        g_packed=pltpu.VMEM((R, 2 * Q), BF),
        g_dpicks=pltpu.VMEM((8, 512), F32),
        g_pairs=sems(4, NT),
        g_result=pltpu.VMEM((NT, R, 2 * Q), BF),
        g_dpicks_all=pltpu.VMEM((NT, 8, 512), F32),
    )


def halves(values):
    high = values.astype(BF)
    return high, (values - high.astype(F32)).astype(BF)


RS_ROWS = ((0, 64), (64, 48))
GR = D // NDP


def sum_dp(pack, result, near, half, held, mine, tile, tiles, core_sems, chip_sems, tile_sems):
    home = lax.axis_index(DP)
    core = home % 2
    chip = home // 2
    partner = home + 1 - 2 * core
    copy = send(pack.at[1 - core], near, core_sems.at[0, 0], core_sems.at[1, 0], DP, partner)
    yield
    copy.wait()
    half[...] = (pack[core].astype(F32) + near[...].astype(F32)).astype(BF)
    chips = [(dy, dx) for dy in (2, 1, 3, 0) for dx in (1, 0) if (dy, dx) != (0, 0)]

    def chip_at(dy, dx):
        return ((chip // 2 + dy) % 4) * 2 + (chip + dx) % 2

    copies = []
    for number, (dy, dx) in enumerate(chips):
        other = chip_at(dy, dx)
        copies.append(
            send(
                half.at[other], held.at[chip], chip_sems.at[0, number], chip_sems.at[1, number],
                DP, other * 2 + core,
            )
        )
    yield
    for copy in copies:
        copy.wait()
    total = half[chip].astype(F32)
    for step in range(1, 8):
        total = total + held[(chip + step) % 8].astype(F32)
    mine[...] = total[:, :768].astype(BF)
    tile[...] = total[:, 768:]
    small = spread_over_tensor(tile, lambda me: tiles.at[me], tile_sems, 0)
    copies = []
    for number, (dy, dx) in enumerate(chips):
        other = chip_at(dy, dx)
        copies.append(
            send(
                mine, result.at[core, chip, :, pl.ds(0, 768)], chip_sems.at[2, number],
                chip_sems.at[3, number], DP, other * 2 + core,
            )
        )
    result[core, chip, :, 0:768] = mine[...]
    yield
    for copy in small:
        copy.wait()
    me = lax.axis_index(TENSOR)
    others = tile[...]
    for step in range(1, NT):
        others = others + tiles[(me + step) % NT]
    lanes = lax.broadcasted_iota(jnp.int32, (GR, 128), 1)
    result[core, chip, :, 768:] = jnp.where(lanes == 33, others, tile[...]).astype(BF)
    for number, (dy, dx) in enumerate(chips):
        other = chip_at(dy, dx)
        place = result.at[core, chip, :, pl.ds(768, 128)]
        copies.append(
            send(
                place, place, chip_sems.at[4, number], chip_sems.at[5, number], DP,
                other * 2 + core,
            )
        )
    yield
    for copy in copies:
        copy.wait()
    copy = send(
        result.at[core], result.at[core], core_sems.at[0, 1], core_sems.at[1, 1], DP, partner
    )
    yield
    copy.wait()


SUM_SCRATCH = dict(
    t_near=pltpu.VMEM((8, GR, GP), BF),
    t_half=pltpu.VMEM((8, GR, GP), BF),
    t_held=pltpu.VMEM((8, GR, GP), BF),
    t_mine=pltpu.VMEM((GR, D), BF),
    t_tile=pltpu.VMEM((GR, 128), F32),
    t_tiles=pltpu.VMEM((NT, GR, 128), F32),
    t_core=sems(2, 2),
    t_chip=sems(6, 8),
    t_tile_sems=sems(2, NT),
    t_pack=pltpu.VMEM((2, 8, GR, GP), BF),
    t_gathers=sems(6, NT),
)


def gathers(sources, targets, pairs, begin):
    def handle(chosen):
        me = lax.axis_index(TENSOR)
        for number in chosen:
            for step in range(1, NT):
                copy = pltpu.make_async_remote_copy(
                    src_ref=sources[number],
                    dst_ref=targets[number].at[me],
                    send_sem=pairs.at[2 * number, step],
                    recv_sem=pairs.at[2 * number + 1, step],
                    device_id={TENSOR: (me + step) % NT},
                    device_id_type=MESH,
                )
                if begin:
                    copy.start()
                else:
                    copy.wait()

    @pl.when(lax.axis_index(PIPE) == 0)
    def _():
        handle((0,))

    @pl.when(lax.axis_index(PIPE) == 1)
    def _():
        handle((1, 2))


def weights_steps(f):
    yield
    projected = f.qkv_in[...]
    for image in range(2):
        for head in range(NH):
            queries, keys, _ = head_parts(projected, image, head)
            f.l_weights[image * NH + head] = probabilities(queries, keys)


def layer_steps(f, last, meta, delta):
    packed, dpicks, state = f.g_result, f.g_dpicks_all, f.state_in
    dqkv, part, dx1_kept, held, near, chosen, pairs, across_sems = (
        f.l_dqkv, f.l_part, f.l_dx1, f.l_held, f.l_near, f.l_chosen, f.l_pairs, f.l_across
    )
    x1 = state[...].astype(F32) + f.summed_in[...].reshape(NR, D).astype(F32)
    live = meta[:, 38:39]
    gate = meta[:, 0:EXPERTS]
    dx2 = delta[...].astype(F32) * live
    total = dpicks[0] + dpicks[1] + dpicks[2] + dpicks[3]
    total = jnp.concatenate([total, jnp.zeros((120, 512), F32)], axis=0)
    columns = jnp.transpose(total)[:NR]
    experts = lax.broadcasted_iota(jnp.int32, (NR, EXPERTS), 1)
    dgate = jnp.zeros((NR, EXPERTS), F32)
    for k in range(2):
        route = meta[:, 36 + k : 37 + k].astype(jnp.int32)
        dgate = dgate + jnp.where(route == experts, columns[:, k : k + 1] * live, 0.0)
    dlogits = gate * (dgate - jnp.sum(gate * dgate, axis=-1, keepdims=True))
    normal, inverse = norm_parts(x1)
    high, low = halves(dlogits)
    dz2 = (
        unpack(packed).astype(F32) + dot(high, f.router[...]) + dot(low, f.router[...])
    )
    dx1 = dx2 + norm_back(dz2, f.gain_two[...], normal, inverse)
    dx1_kept[...] = dx1.reshape(NT, CH, D)
    dattn = dx1.astype(BF)
    if last:
        sources = [f.own_in, f.wide_one_in, f.wide_two_in]
        targets = [f.own, f.wide_one, f.wide_two]
        gathers(sources, targets, f.t_gathers, True)
        for source, target in zip(sources, targets):
            target[lax.axis_index(TENSOR)] = source[...]
    dctx = dot(dattn, f.output[...], 1, 1).astype(BF)
    scale = HD**-0.5
    projected = f.qkv_in[...]
    for image in range(2):
        rows = slice(image * R, (image + 1) * R)
        for head in range(NH):
            queries, keys, values = head_parts(projected, image, head)
            dc = dctx[rows, head * HD : (head + 1) * HD]
            weights = f.l_weights[image * NH + head]
            dweights = dot(dc, values, 1, 1)
            dvalues = dot(weights.astype(BF), dc, 0, 0)
            dscores = weights * (dweights - jnp.sum(weights * dweights, axis=-1, keepdims=True))
            dscores = dscores.astype(BF)
            dqueries = dot(dscores, keys) * scale
            dkeys = dot(dscores, queries, 0, 0) * scale
            for number, value in enumerate((dqueries, dkeys, dvalues)):
                start = number * GW + head * HD
                dqkv[rows, start : start + HD] = value.astype(BF)
    own_part = dot(dqkv[...], f.project[...]).astype(BF)
    part[...] = own_part.reshape(NT, CH, D)
    me = lax.axis_index(TENSOR)
    stage = lax.axis_index(PIPE)
    scattered = [
        [
            send(
                part.at[(me + step) % NT, pl.ds(start, size)],
                held.at[me, pl.ds(start, size)],
                pairs.at[2 * i, step],
                pairs.at[2 * i + 1, step],
                TENSOR,
                (me + step) % NT,
            )
            for step in range(1, NT)
        ]
        for i, (start, size) in enumerate(RS_ROWS)
    ]
    normal_one, _ = norm_parts(state[...].astype(F32))
    normed_one = (normal_one * f.gain_one[...]).astype(BF)
    normed = (normal * f.gain_two[...]).astype(BF)
    gain_rows = [
        jnp.sum(dz2 * normal, axis=0, keepdims=True),
        jnp.sum(own_part.astype(F32) * normal_one, axis=0, keepdims=True),
    ]
    places = lax.broadcasted_iota(jnp.int32, (128, D), 0)
    tall = jnp.where(places == 32, gain_rows[0], 0.0)
    tall = jnp.where(places == 33, gain_rows[1], tall)
    terms = [
        (0, 576, dot(normed_one, dqkv[...], 0, 0)),
        (576, 768, dot(dattn, f.ctx_in[...], 0, 0)),
    ]
    side = jnp.transpose(tall)
    router_term = dot(normed, high, 0, 0) + dot(normed, low, 0, 0)
    side = side + jnp.concatenate([router_term, jnp.zeros((D, 96), F32)], axis=1)
    terms.append((768, GP, side))
    if last:
        one, first, pack = f.grads_one, f.grads_first, f.t_pack
        for low_end, high_end, term in terms:
            term = jnp.where(stage == 0, term, first[:, low_end:high_end])
            term = term + one[:, low_end:high_end]
            pack[:, :, :, low_end:high_end] = term.astype(BF).reshape(
                2, 8, GR, high_end - low_end
            )
        summing = sum_dp(
            pack,
            f.whole,
            f.t_near, f.t_half, f.t_held, f.t_mine, f.t_tile, f.t_tiles, f.t_core, f.t_chip,
            f.t_tile_sems,
        )
        next(summing)
        next(summing)
    else:
        for low_end, high_end, term in terms:
            f.grads[:, low_end:high_end] = term
        f.flush(f.grads)
        summing = iter(())
    waiting = []
    result = f.result
    chunk = chosen if last else f.chunk
    across = []
    for i, (start, size) in enumerate(RS_ROWS):
        rows = pl.ds(start, size)
        for copy in scattered[i]:
            copy.wait_recv()
        dz1 = part[me, rows].astype(F32)
        for step in range(1, NT):
            dz1 = dz1 + held[(me + step) % NT, rows].astype(F32)
        here = pl.ds(pl.multiple_of(me * CH + start, 16), size)
        normal_here, inverse_here = norm_parts(state[here].astype(F32))
        delta_here = norm_back(dz1, f.gain_one[...], normal_here, inverse_here)
        chunk[rows] = (dx1_kept[me, rows] + delta_here).astype(BF)
        if not last:
            across.append(
                send(
                    chunk.at[rows], near.at[rows], across_sems.at[0, i], across_sems.at[1, i],
                    PIPE, 1 - stage,
                )
            )
    for i, (start, size) in enumerate(RS_ROWS):
        rows = pl.ds(start, size)
        if not last:
            across[i].wait_recv()
            chosen[rows] = jnp.where(stage == 1, chunk[rows], near[rows])
        waiting += spread_over_tensor(
            chosen.at[rows], lambda me: result.at[me, rows], pairs, 4 + 2 * i
        )
    result[me] = chosen[...]
    yield
    for _ in summing:
        yield
    if last:
        gathers(sources, targets, f.t_gathers, False)
        f.flush(f.own, f.wide_one, f.wide_two, f.whole)
    for copy in waiting:
        copy.wait()
    for group in scattered:
        for copy in group:
            copy.wait_send()
    for copy in across:
        copy.wait_send()
    f.flush(f.result)
    if not last:
        f.flush(f.chunk)


LAYER_SCRATCH = dict(
    l_dqkv=pltpu.VMEM((NR, 3 * GW), BF),
    l_part=pltpu.VMEM((NT, CH, D), BF),
    l_dx1=pltpu.VMEM((NT, CH, D), F32),
    l_held=pltpu.VMEM((NT, CH, D), BF),
    l_near=pltpu.VMEM((CH, D), BF),
    l_chosen=pltpu.VMEM((CH, D), BF),
    l_pairs=sems(8, NT),
    l_across=sems(2, 2),
    l_weights=pltpu.VMEM((2 * NH, R, R), F32),
    h_hot=HOTS,
)
ROWS_OUT = ((NDP, 2 * SL, D), BF)
BACKWARD_OUTS = dict(
    delta_arrived=ROWS_OUT,
    hidden=ROWS_OUT,
    dpre=ROWS_OUT,
    result=((NT, CH, D), BF),
)
LINEAR_OUTS = dict(chunk=((CH, D), BF), grads=((D, GP), F32))


def finish_kernel(stage, *refs):
    states, grads, whole = refs[:4], refs[4:8], refs[8]
    section_out, input_grad, project_grad, output_grad, router_grad, gains = refs[9:]

    def rows(values):
        values = values.astype(F32)
        return jnp.concatenate([values[:IMG_LEN], values[R : R + IMG_LEN]], axis=0).astype(BF)

    def place(base):
        for micro in range(2):
            section_out[micro] = rows(unpack(states[base + micro]))
            input_grad[micro] = rows(grads[base + micro][...])

    @pl.when(stage[0, 0] == 0)
    def _():
        place(0)

    @pl.when(stage[0, 0] != 0)
    def _():
        place(2)

    project_grad[...] = jnp.transpose(whole[:, :576].astype(F32))
    output_grad[...] = jnp.transpose(whole[:, 576:768].astype(F32))
    side = whole[:, 768:].astype(F32)
    side = jnp.transpose(side)
    router_grad[...] = side[:EXPERTS]
    gains[...] = side[EXPERTS : EXPERTS + 8]


def finish(stage, states, grads, whole):
    return pl.pallas_call(
        finish_kernel,
        in_specs=[SMEM] + [VMEM] * 9,
        out_shape=[
            jax.ShapeDtypeStruct((2, 2 * IMG_LEN, D), BF),
            jax.ShapeDtypeStruct((2, 2 * IMG_LEN, D), BF),
            jax.ShapeDtypeStruct((3 * GW, D), F32),
            jax.ShapeDtypeStruct((GW, D), F32),
            jax.ShapeDtypeStruct((EXPERTS, D), F32),
            jax.ShapeDtypeStruct((8, D), F32),
        ],
        compiler_params=params(),
        name="finish",
    )(stage, *states, *grads, whole)


def body(
    tokens,
    cotangent,
    image_counts,
    routes,
    attn_norm_gain,
    query_key_value,
    attn_output,
    moe_norm_gain,
    router_weight,
    expert_in,
    expert_down,
):
    project = query_key_value[0].transpose(1, 2, 0).reshape(3 * GW, D)
    stage = lax.axis_index(PIPE)
    all_axes = (TENSOR, DP, PIPE)
    gains = dict(gain_one=(attn_norm_gain, VMEM), gain_two=(moe_norm_gain, VMEM))
    small = dict(project=project, output=attn_output[0], router=router_weight[0].T)
    heavy = dict(first=expert_in[0], second=expert_down[0])
    placing = dict(counts=(image_counts, SMEM), routes=(routes, VMEM))

    def place_of(f, moment):
        home = lax.axis_index(DP)
        one, other = min(moment, 1), max(moment - 1, 0)
        early = lax.axis_index(PIPE) == 0
        count = jnp.where(early, f.counts[one, home], f.counts[other, home])
        path = jnp.where(early, f.routes[one], f.routes[other])
        return count, padded(path)

    def forward(moment, arriving):
        def program(f):
            if moment == 0:
                state = padded(f.tokens[0])
            else:
                early = lax.axis_index(PIPE) == 0
                state = jnp.where(early, padded(f.tokens[1]), unpack(f.arriving))
            drive(attention_steps(f, state), places_steps(f, *place_of(f, moment)))
            drive(dispatch_steps(f, True), hot_steps(f.meta, f.h_hot))
            drive(experts_forward_steps(f, f.arrived))
            drive(combine_steps(f, True, f.meta, f.h_hot))

        outs = dict(FORWARD_OUTS)
        outs["packed"] = ((R, 2 * Q), BF)
        outs["pieces"] = ((2, NR, Q), BF)
        outs["onward"] = ((NT, R, 2 * Q), BF)
        plain = dict(**gains, **placing, tokens=(tokens, VMEM))
        if moment > 0:
            plain["arriving"] = (arriving, VMEM)
        return launch(
            "forward_%d" % moment, 1 + moment, all_axes, plain, dict(**small, **heavy), outs,
            dict(
                **forward_scratch(), **prefixed("d_", to_experts_scratch(True)), **prefixed("f_", expert_scratch()),
                **combine_scratch(),
            ),
            program,
        )

    def kept(saved):
        return dict(
            state_in=saved.state,
            summed_in=saved.summed,
            qkv_in=saved.qkv,
            ctx_in=saved.ctx,
            meta_in=saved.meta,
            arrived_in=saved.arrived,
        )

    def either(one, other):
        return {key: (one[key], other[key]) for key in one}

    backward_scratch = dict(**prefixed("b_", expert_scratch()), **collect_scratch(), **LAYER_SCRATCH)
    zero = forward(0, None)
    one = forward(1, zero.onward)

    def turning(f):
        state = unpack(f.arriving)
        delta = padded(f.delta[0])
        f.delta_kept[...] = delta
        drive(
            chain(
                lambda: spread_steps(f, False, delta, f.meta_in),
                lambda: experts_backward_steps(f, f.arrived_in),
                lambda: collect_steps(f, f.meta_in, lambda k: f.pieces_in[k], f.delta_kept),
                lambda: layer_steps(f, False, f.meta_in, f.delta_kept),
            ),
            chain(lambda: attention_steps(f, state), lambda: dispatch_steps(f, False)),
            places_steps(f, *place_of(f, 2)),
            hot_steps(f.meta_in, f.h_hot),
            weights_steps(f),
        )

    two = launch(
        "turning", 3, all_axes,
        dict(**gains, **placing, delta=(cotangent, VMEM), arriving=(one.onward, VMEM)),
        dict(**small, **kept(one), pieces_in=one.pieces, **heavy),
        dict(**FORWARD_OUTS, **BACKWARD_OUTS, **LINEAR_OUTS),
        dict(
            **forward_scratch(), **prefixed("d_", to_experts_scratch(False)),
            **prefixed("s_", to_experts_scratch(False)), **backward_scratch,
            delta_kept=pltpu.VMEM((NR, D), BF),
        ),
        turning,
    )

    def middle(f):
        early = lax.axis_index(PIPE) == 0
        delta = jnp.where(early, f.arriving[...].reshape(NR, D), padded(f.delta[1]))
        f.delta_kept[...] = delta
        drive(
            chain(
                lambda: spread_steps(f, False, delta, f.meta_in),
                lambda: experts_backward_steps(f, f.arrived_in),
                lambda: collect_steps(
                    f,
                    f.meta_in,
                    lambda k: jnp.where(early, f.pieces_in[k], f.pieces[k]),
                    f.delta_kept,
                ),
                lambda: layer_steps(f, False, f.meta_in, f.delta_kept),
            ),
            chain(
                lambda: experts_forward_steps(f, f.late_arrived),
                lambda: combine_steps(f, False, f.late_meta, f.k_hot),
            ),
            chain(lambda: hot_steps(f.late_meta, f.k_hot), lambda: hot_steps(f.meta_in, f.h_hot)),
            weights_steps(f),
        )

    three = launch(
        "middle", 4, all_axes,
        dict(**gains, delta=(cotangent, VMEM), arriving=(two.result, VMEM)),
        dict(
            **either(kept(zero), kept(two)), **heavy, late_arrived=two.arrived,
            late_meta=two.meta, state=two.state, summed=two.summed,
            pieces_in=zero.pieces, **small,
        ),
        dict(**BACKWARD_OUTS, **LINEAR_OUTS, packed=((R, 2 * Q), BF)),
        dict(
            **prefixed("s_", to_experts_scratch(False)), **prefixed("f_", expert_scratch()), **backward_scratch,
            pieces=pltpu.VMEM((2, NR, Q), BF), k_hot=HOTS, delta_kept=pltpu.VMEM((NR, D), BF),
        ),
        middle,
    )

    def ending(f):
        delta = f.arriving[...].reshape(NR, D)
        f.delta_kept[...] = delta
        drive(
            chain(
                lambda: spread_steps(f, True, delta, f.meta_in),
                lambda: experts_backward_steps(f, f.arrived_in),
                lambda: collect_steps(f, f.meta_in, lambda k: f.pieces_in[k], f.delta_kept),
                lambda: layer_steps(f, True, f.meta_in, f.delta_kept),
            ),
            hot_steps(f.meta_in, f.h_hot),
            weights_steps(f),
        )

    wide = ((NT, R, 2 * Q), BF)
    four = launch(
        "ending", 5, (TENSOR, DP),
        dict(**gains, arriving=(three.result, VMEM)),
        dict(
            **kept(one), **heavy, pieces_in=one.pieces, **small,
            own_in=three.chunk, wide_one_in=one.packed,
            wide_two_in=three.packed, grads_one=three.grads,
            grads_first=two.grads,
        ),
        dict(
            **BACKWARD_OUTS, whole=((2, 8, GR, GP), BF), own=((NT, CH, D), BF),
            wide_one=wide, wide_two=wide,
        ),
        dict(
            **prefixed("s_", to_experts_scratch(True)), **backward_scratch, **SUM_SCRATCH,
            delta_kept=pltpu.VMEM((NR, D), BF),
        ),
        ending,
    )

    def outer(saved, results):
        return (saved.arrived, results.dpre, results.hidden, results.delta_arrived)

    early = stage == 0
    middle_arrived = jnp.where(early, zero.arrived, two.arrived)
    grad_first, grad_second = expert_grads(
        stage.reshape(1).astype(jnp.int32),
        outer(SimpleNamespace(arrived=middle_arrived), three),
        outer(one, four),
        outer(one, two),
    )
    section_out, input_grad, project_grad, output_grad, router_grad, gain_grads = finish(
        stage.reshape(1, 1).astype(jnp.int32),
        [zero.onward, one.onward, four.wide_one, four.wide_two],
        [
            array.reshape(NR, D)
            for array in (four.own, four.result, two.result, three.result)
        ],
        four.whole.reshape(D, GP),
    )
    return (
        section_out[None],
        input_grad[None],
        gain_grads[1:2],
        project_grad.reshape(1, 3, GW, D).transpose(0, 3, 1, 2),
        output_grad[None],
        gain_grads[0:1],
        router_grad.T[None],
        grad_first[None],
        grad_second[None],
    )


def solution(mesh):
    placed = (
        P(None, DP, None),
        P(None, DP, None),
        P(),
        P(None, DP, None),
        P(PIPE, None),
        P(PIPE, None, None, TENSOR),
        P(PIPE, TENSOR, None),
        P(PIPE, None),
        P(PIPE, None, None),
        P(PIPE, DP, None, TENSOR),
        P(PIPE, DP, TENSOR, None),
    )
    return jax.shard_map(
        body,
        mesh=mesh,
        in_specs=placed,
        out_specs=(
            P(PIPE, None, DP, None),
            P(PIPE, None, DP, None),
            P(PIPE, None),
            P(PIPE, None, None, TENSOR),
            P(PIPE, TENSOR, None),
            P(PIPE, None),
            P(PIPE, None, None),
            P(PIPE, DP, None, TENSOR),
            P(PIPE, DP, TENSOR, None),
        ),
        check_vma=False,
    )
```
